32 devices in a mesh: elem: 8 (over z, x), band: 4 (over y, core).
Axes of the slice: x: 2, y: 2, z: 4, core: 2. Of those that a mesh axis runs over, the one named last changes fastest.
Arguments:
- basis_sizes: int32 [128], P('elem'), may hold values from 96 to 160, as said below
- coupling_pattern: int32 [128], P('elem'), may hold values 0 or 1
- h_diag: bfloat16 [128, 160, 160], P('elem'), may hold values from -0.6708204 to 0.6708204, as said below
- h_couple: bfloat16 [128, 160, 160], P('elem'), may hold values from -0.25 to 0.25
- bands: bfloat16 [1024, 20480], P('band', 'elem'), may hold values from -1500 to 1500
Outputs:
- filtered: bfloat16 [1024, 20480], P('band', 'elem')
The draws below stay inside these ranges and needn't reach their ends.
Inputs may be any that keep to these rules, and one draw needn't show every extreme that they name: `basis_sizes`: every element has between 96 and 160 basis functions; some element has exactly 160 and some exactly 96. `h_diag`: each block is symmetric.
All inputs are finite; a program needn't handle non-finite values. No bound on the sum of `coupling_pattern` on one device may be relied on, other than what follows from the above.
Results may differ from the reference program's by a relative error of at most 0.0085.
Values may be sent and summed in bfloat16 or wider, within the bound.
No kernel may reach another device: no remote copies, remote signals or barrier semaphores. Data moves between devices by JAX's collectives and lax.ppermute only.
A program may use at most 64 MiB of HBM per device.

```python
import math
import jax
import jax.numpy as jnp
from jax import lax

NB = 160
NB_MIN = 96
BANDS = 1024
DEGREE = 6
E = 128


def draw_basis_sizes(key, part):
    key_counts = jax.random.fold_in(key, 11)
    key_largest = jax.random.fold_in(key, 12)
    key_offset = jax.random.fold_in(key, 13)
    counts_drawn = jax.random.randint(key_counts, (E,), NB_MIN, NB + 1)
    largest = jax.random.randint(key_largest, (), 0, E)
    offset_draw = jax.random.randint(key_offset, (), 1, E)
    smallest = (largest + offset_draw) % E
    counts_drawn = counts_drawn.at[largest].set(NB)
    counts_drawn = counts_drawn.at[smallest].set(NB_MIN)
    return counts_drawn.astype(jnp.int32)


def draw_h_diag(key, part):
    noise_key = jax.random.fold_in(key, 23)
    raw_noise = jnp.clip(jax.random.normal(noise_key, (E, NB, NB), jnp.float32), -6.0, 6.0)
    scaled = raw_noise * (2.0 * NB) ** (-0.5)
    return (scaled + jnp.swapaxes(scaled, 1, 2)).astype(jnp.bfloat16)


def draw_bands(key, part):
    noise_key = jax.random.fold_in(key, 37)
    element_key = jax.random.fold_in(key, 41)
    band_key = jax.random.fold_in(key, 43)
    heavy_key = jax.random.fold_in(key, 47)
    second_key = jax.random.fold_in(key, 53)
    noise_values = jnp.clip(jax.random.normal(noise_key, (BANDS, E, NB), jnp.float32), -6.0, 6.0)
    upper_scale = 10.0
    element_scale = jnp.exp(jax.random.uniform(element_key, (E,), jnp.float32, 0.0, math.log(upper_scale)))
    first_heavy = jax.random.randint(heavy_key, (), 0, E)
    second_heavy = (first_heavy + jax.random.randint(second_key, (), 1, E)) % E
    element_ids = lax.broadcasted_iota(jnp.int32, (E,), 0)
    heavy_mask = (element_ids == first_heavy) | (element_ids == second_heavy)
    element_scale = jnp.where(heavy_mask, 60.0, element_scale)
    band_scale = jnp.exp(jax.random.uniform(band_key, (BANDS,), jnp.float32, 0.0, math.log(4.0)))
    values = noise_values * element_scale[None, :, None] * band_scale[:, None, None]
    return values.reshape(BANDS, E * NB).astype(jnp.bfloat16)


def place_ends(values, own_key, low, high):
    extent = values.shape
    index_at = [jax.random.randint(jax.random.fold_in(own_key, axis), (), 0, extent[axis]) for axis in range(len(extent))]
    values = values.at[tuple(index_at)].set(low)
    longest = extent.index(max(extent))
    index_at[longest] = (index_at[longest] + 1) % extent[longest]
    return values.at[tuple(index_at)].set(high)


def levels(rng, shape, cuts, least, top_value):
    factor_of = 1.0
    for dim, blocks in cuts:
        heights = jax.random.uniform(jax.random.fold_in(jax.random.fold_in(rng, 6), dim), (blocks,), jnp.float32, least / len(cuts), top_value / len(cuts))
        factor_of = factor_of * jnp.repeat(jnp.exp(heights), shape[dim] // blocks).reshape((-1,) + (1,) * (len(shape) - 1 - dim))
    return factor_of


def normal_values(rng, extent, deviation, limit, pieces=(), kind=jnp.bfloat16):
    entries = deviation * jax.random.normal(rng, extent, jnp.float32)
    if pieces:
        entries = entries * levels(rng, extent, pieces, -0.22, 0.18)
    return jnp.clip(entries, -limit, limit).astype(kind)


def setup_inputs(seed: int = 0) -> dict:
    key_of = jax.random.split(jax.random.key(seed), 6)
    return {
        "basis_sizes": draw_basis_sizes(jax.random.fold_in(key_of[5], 71), 0),
        "coupling_pattern": place_ends((jax.random.randint(key_of[1], (E,), 0, 4) < 3).astype(jnp.int32), jax.random.fold_in(key_of[1], 1), 0, 1),
        "h_diag": draw_h_diag(jax.random.fold_in(key_of[5], 71), 0),
        "h_couple": normal_values(key_of[3], (E, NB, NB), (4 * NB) ** -0.5, 0.25, ((0, 8),)),
        "bands": draw_bands(jax.random.fold_in(key_of[5], 71), 0),
    }


center_shift = 0.4
half_width = 2.8
epsilon_norm = 1e-06

def hamiltonian(vectors, diagonal_blocks, coupling, valid_rows):
    local_term = jnp.einsum('eij,bej->bei', diagonal_blocks, vectors)
    ahead_rows = jnp.roll(vectors, -1, axis=1)
    upper_term = jnp.einsum('eij,bej->bei', coupling, ahead_rows)
    carried = jnp.einsum('eji,bej->bei', coupling, vectors)
    lower_term = jnp.roll(carried, 1, axis=1)
    return (local_term + upper_term + lower_term) * valid_rows[None]

def reference(basis_sizes, coupling_pattern, h_diag, h_couple, bands):
    columns = lax.broadcasted_iota(jnp.int32, (E, NB), 1)
    valid_rows = (columns < basis_sizes[:, None]).astype(jnp.float32)
    diagonal_blocks = h_diag.astype(jnp.float32)
    coupling = h_couple.astype(jnp.float32) * coupling_pattern.astype(jnp.float32)[:, None, None]
    current = (bands.reshape(BANDS, E, NB).astype(jnp.float32) * valid_rows[None]).astype(jnp.bfloat16)
    previous = current
    for degree in range(DEGREE):
        current_float = current.astype(jnp.float32)
        applied = hamiltonian(current_float, diagonal_blocks, coupling, valid_rows)
        shifted = applied - center_shift * current_float
        if degree == 0:
            following = shifted / half_width
        else:
            following = 2.0 * shifted / half_width - previous.astype(jnp.float32)
        previous, current = (current, following.astype(jnp.bfloat16))
    filtered = current.reshape(BANDS, E * NB)
    gram = jnp.dot(filtered, filtered.T, preferred_element_type=jnp.float32)
    scales = lax.rsqrt(jnp.diagonal(gram) + epsilon_norm)
    normed = scales[:, None] * gram * scales[None, :]
    identity = jnp.eye(BANDS, dtype=jnp.float32)
    weights = (math.sqrt(E * NB) * scales[:, None] * (1.5 * identity - 0.5 * normed)).astype(jnp.bfloat16)
    return jnp.dot(weights.T, filtered, preferred_element_type=jnp.float32).astype(jnp.bfloat16)
```

```python
import functools
import math

import jax
import jax.numpy as jnp
from jax import lax
from jax.experimental import pallas as pl
from jax.experimental.pallas import tpu as pltpu
from jax.sharding import PartitionSpec as P

DEGREE = 6
STRIPS = (3, 3)

center_shift = 0.4
half_width = 2.8
epsilon_norm = 1e-06

LANES = 128
VMEM = pl.BlockSpec(memory_space=pltpu.VMEM)
SMEM = pl.BlockSpec(memory_space=pltpu.SMEM)
BF16 = jnp.bfloat16
F32 = jnp.float32


def from_behind(value, axis, steps):
    count = lax.axis_size(axis)
    pairs = [(source, (source + steps) % count) for source in range(count)]
    return lax.ppermute(value, axis, pairs)


def swap(value, axis, bit):
    count = lax.axis_size(axis)
    return lax.ppermute(value, axis, [(source, source ^ bit) for source in range(count)])


def params():
    return pltpu.CompilerParams(vmem_limit_bytes=52 * 1024 * 1024)


def advance(row, window, center, before, first):
    total = jnp.dot(row, window, preferred_element_type=F32)
    shifted = total - center_shift * center.astype(F32)
    if first:
        return (shifted * (1.0 / half_width)).astype(BF16)
    return (shifted * (2.0 / half_width) - before.astype(F32)).astype(BF16)


def add_squares(total, values):
    values = values.astype(F32)
    return total + jnp.sum(values * values, axis=0, keepdims=True)


def interior_kernel(width, count, y_ref, rows_ref, out_ref, left_ref, right_ref, squares_ref, odd_ref, even_ref):
    n = width
    buffers = (even_ref, odd_ref)
    for step in range(DEGREE):
        source = y_ref if step == 0 else buffers[step % 2]
        target = buffers[(step + 1) % 2]
        older = y_ref if step == 1 else target
        left_ref[step] = source[step * n : (step + 2) * n, :]
        right_ref[step] = source[(count - step - 2) * n : (count - step) * n, :]

        def body(e, carry):
            at = pl.multiple_of(e * n, 16)
            window = source[pl.ds(pl.multiple_of((e - 1) * n, 16), 3 * n), :]
            center = source[pl.ds(at, n), :]
            before = older[pl.ds(at, n), :]
            target[pl.ds(at, n), :] = advance(rows_ref[e, :, : 3 * n], window, center, before, step == 0)
            return carry

        lax.fori_loop(step + 1, count - 1 - step, body, 0, unroll=2)
    result = buffers[DEGREE % 2][DEGREE * n : (count - DEGREE) * n, :]
    out_ref[...] = result
    squares_ref[...] = add_squares(jnp.zeros(squares_ref.shape, F32), result)


def strip_kernel(
    width,
    count,
    strip,
    offset,
    last,
    me_ref,
    left_y_ref,
    right_y_ref,
    left_edge_ref,
    right_edge_ref,
    rows_ref,
    left_rows_ref,
    right_rows_ref,
    squares_in_ref,
    out_ref,
    left_out_ref,
    right_out_ref,
    squares_ref,
    left_scr,
    right_scr,
    halo_left,
    halo_right,
):
    n = width
    depth = DEGREE - 1
    me = me_ref[0]
    pieces = left_rows_ref.shape[0]
    lanes = left_rows_ref.shape[2]
    for piece in range(pieces):
        owner = me ^ piece
        halo_left[:, :, piece * lanes : (piece + 1) * lanes] = left_rows_ref[owner].reshape(depth, n, lanes)
        halo_right[:, :, piece * lanes : (piece + 1) * lanes] = right_rows_ref[owner].reshape(depth, n, lanes)

    def left_row(e):
        if e < 0:
            return halo_left[depth + e, :, : 3 * n]
        if e > 0:
            return rows_ref[e, :, : 3 * n]
        turned = jnp.transpose(halo_left[depth - 1, :, 2 * n : 3 * n].astype(F32))
        keep = rows_ref[0, :, 3 * n : 3 * n + 1].astype(F32)
        return jnp.concatenate([(turned * keep).astype(BF16), rows_ref[0, :, n : 3 * n]], axis=1)

    def right_row(e):
        if e < count:
            return rows_ref[e, :, : 3 * n]
        if e > count:
            return halo_right[e - count, :, : 3 * n]
        turned = jnp.transpose(rows_ref[count - 1, :, 2 * n : 3 * n].astype(F32))
        keep = halo_right[0, :, 3 * n : 3 * n + 1].astype(F32)
        return jnp.concatenate([(turned * keep).astype(BF16), halo_right[0, :, n : 3 * n]], axis=1)

    left_scr[0, : strip * n, :] = left_y_ref[...]
    right_scr[0, 2 * n :, :] = right_y_ref[...]
    for step in range(DEGREE):
        left_scr[step, strip * n :, :] = left_edge_ref[step]
        right_scr[step, : 2 * n, :] = right_edge_ref[step]
        for j in range(strip):
            e = offset + step + 1 + j
            left_scr[step + 1, j * n : (j + 1) * n, :] = advance(
                left_row(e),
                left_scr[step, j * n : (j + 3) * n, :],
                left_scr[step, (j + 1) * n : (j + 2) * n, :],
                left_scr[max(step - 1, 0), (j + 2) * n : (j + 3) * n, :],
                step == 0,
            )
            e = count - 1 - (offset + strip + step) + j
            right_scr[step + 1, (j + 2) * n : (j + 3) * n, :] = advance(
                right_row(e),
                right_scr[step, j * n : (j + 3) * n, :],
                right_scr[step, (j + 1) * n : (j + 2) * n, :],
                right_scr[max(step - 1, 0), j * n : (j + 1) * n, :],
                step == 0,
            )
        if not last:
            left_out_ref[step] = left_scr[step, : 2 * n, :]
            right_out_ref[step] = right_scr[step, strip * n : (strip + 2) * n, :]
    result_left = left_scr[DEGREE, : strip * n, :]
    result_right = right_scr[DEGREE, 2 * n :, :]
    out_ref[: strip * n, :] = result_left
    out_ref[strip * n : 2 * strip * n, :] = result_right
    squares = add_squares(add_squares(squares_in_ref[...], result_left), result_right)
    squares_ref[...] = squares
    if last:
        high = squares.astype(BF16).astype(F32)
        low = squares - high
        place = lax.broadcasted_iota(jnp.int32, (16, squares.shape[1]), 0)
        both = jnp.where(place == 0, high, jnp.where(place == 1, low, 0.0))
        out_ref[2 * strip * n :, :] = both.astype(BF16)


def gram_kernel(chunks, blocks, shares, *refs):
    out_ref = refs[-1]
    grid = [refs[c * blocks : (c + 1) * blocks] for c in range(chunks)]
    local = grid[0][0].shape[1]
    rows = local // shares
    full = [grid[c][0].shape[0] - (16 if c == chunks - 1 else 0) for c in range(chunks)]
    totals = [None] * blocks
    for c in range(chunks):
        turned = jnp.transpose(grid[c][0][: full[c], :])
        for r in range(blocks):
            term = jnp.dot(turned, grid[c][r][: full[c], :], preferred_element_type=F32)
            totals[r] = term if totals[r] is None else totals[r] + term
    for r in range(blocks):
        out_ref[:, :, r * local : (r + 1) * local] = totals[r].astype(BF16).reshape(shares, rows, local)
    tail = jnp.zeros((rows, LANES), BF16)
    place = lax.broadcasted_iota(jnp.int32, (rows, LANES), 0)
    parts = local // LANES
    extra = jnp.zeros((rows, LANES), F32)
    for r in range(blocks):
        both = grid[chunks - 1][r][full[-1] :, :].astype(F32)
        for p in range(parts):
            for half in range(2):
                line = both[half : half + 1, p * LANES : (p + 1) * LANES]
                extra = jnp.where(place == half * blocks * parts + r * parts + p, line, extra)
    for share in range(shares):
        out_ref[share, :, blocks * local :] = extra.astype(BF16)


def weights_kernel(total_columns, blocks, me_ref, got_ref, out_ref):
    shares, rows, wide = got_ref.shape
    bands = wide - LANES
    local = bands // blocks
    parts = bands // LANES
    total = got_ref[0].astype(F32)
    for share in range(1, shares):
        total = total + got_ref[share].astype(F32)
    tail = total[:, bands:]
    squares = tail[:parts, :] + tail[parts : 2 * parts, :]
    scales = lax.rsqrt(squares + epsilon_norm)
    me = me_ref[0]
    first = me * rows
    row_ids = lax.broadcasted_iota(jnp.int32, (rows, LANES), 0) + first
    lane_ids = lax.broadcasted_iota(jnp.int32, (rows, LANES), 1)
    own = jnp.zeros((rows, 1), F32)
    for p in range(local // LANES):
        hit = row_ids == lane_ids + p * LANES
        own = own + jnp.sum(jnp.where(hit, scales[p : p + 1, :], 0.0), axis=1, keepdims=True)
    for p in range(parts):
        part = total[:, p * LANES : (p + 1) * LANES]
        across = scales[p : p + 1, :]
        diagonal = 0.0
        if p < local // LANES:
            hit = row_ids == lane_ids + p * LANES
            part = jnp.where(hit, squares[p : p + 1, :], part)
            diagonal = jnp.where(hit, 1.5, 0.0)
        weights = math.sqrt(total_columns) * across * (diagonal - 0.5 * (own * part * across))
        weights = weights.astype(BF16)
        for share in range(shares):
            out_ref[share, :, p * LANES : (p + 1) * LANES] = weights


def rotate_kernel(chunks, blocks, spans, weights_ref, *refs):
    out_ref = refs[-1]
    grid = [refs[c * blocks : (c + 1) * blocks] for c in range(chunks)]
    local = grid[0][0].shape[1]
    for c in range(chunks):
        for begin, size, column in spans[c]:
            total = None
            for r in range(blocks):
                term = lax.dot_general(
                    weights_ref[:, r * local : (r + 1) * local],
                    grid[c][r][begin : begin + size, :],
                    (((1,), (1,)), ((), ())),
                    preferred_element_type=F32,
                )
                total = term if total is None else total + term
            out_ref[:, column : column + size] = total.astype(BF16)


def gather_blocks(own):
    held = [own]
    bit = lax.axis_size("band") // 2
    found = {0: own}
    while bit:
        for index in list(found):
            found[index ^ bit] = swap(found[index], "band", bit)
        bit //= 2
    del held
    return [found[index] for index in range(lax.axis_size("band"))]


def fast_shards(basis_sizes, coupling_pattern, h_diag, h_couple, bands):
    count, n = h_diag.shape[:2]
    local = bands.shape[0]
    elem_size, band_size = lax.axis_size("elem"), lax.axis_size("band")
    total_columns = elem_size * count * n
    depth = DEGREE - 1
    wide = -(-(3 * n + 1) // LANES) * LANES
    lanes = wide // band_size
    elem_me = lax.axis_index("elem").astype(jnp.int32).reshape(1)
    band_me = lax.axis_index("band").astype(jnp.int32).reshape(1)

    valid = (lax.broadcasted_iota(jnp.int32, (count, n), 1) < basis_sizes[:, None]).astype(BF16)
    start = jnp.transpose(bands) * valid.reshape(count * n, 1)

    with jax.named_scope("halo_vectors"):
        left_y, right_y = [], []
        near = 0
        for strip in STRIPS:
            far = near + strip
            left_y.append(from_behind(start[(count - far) * n : (count - near) * n], "elem", 1))
            right_y.append(from_behind(start[near * n : far * n], "elem", -1))
            near = far

    with jax.named_scope("rows"):
        coupling = h_couple * coupling_pattern.astype(BF16)[:, None, None]
        turned = jnp.swapaxes(coupling, 1, 2)
        behind = jnp.concatenate([jnp.zeros_like(turned[:1]), turned[:-1]], axis=0)
        spare = jnp.broadcast_to(valid[:, :, None], (count, n, wide - 3 * n))
        rows = jnp.concatenate([behind, h_diag, coupling, spare], axis=2) * valid[:, :, None]

    with jax.named_scope("halo_rows"):

        def piece(block):
            return lax.dynamic_slice_in_dim(block.reshape(depth * n, wide), band_me[0] * lanes, lanes, 1)

        left_rows = from_behind(piece(rows[count - depth :]), "elem", 1)
        right_rows = from_behind(piece(rows[:depth]), "elem", -1)
        both = gather_blocks(jnp.stack([left_rows, right_rows]))
        left_rows = jnp.stack([block[0] for block in both])
        right_rows = jnp.stack([block[1] for block in both])

    inner = (count - 2 * DEGREE) * n
    edges = jax.ShapeDtypeStruct((DEGREE, 2 * n, local), BF16)
    squares_shape = jax.ShapeDtypeStruct((1, local), F32)
    chunk, left_edge, right_edge, squares = pl.pallas_call(
        functools.partial(interior_kernel, n, count),
        out_shape=[jax.ShapeDtypeStruct((inner, local), BF16), edges, edges, squares_shape],
        in_specs=[VMEM] * 2,
        out_specs=[VMEM] * 4,
        scratch_shapes=[pltpu.VMEM((count * n, local), BF16)] * 2,
        compiler_params=params(),
        name="interior",
    )(start, rows)
    chunks = [gather_blocks(chunk)]
    spans = [[(0, inner, DEGREE * n)]]
    offset = 0
    for index, strip in enumerate(STRIPS):
        last = index == len(STRIPS) - 1
        offset -= strip
        size = 2 * strip * n + (16 if last else 0)
        chunk, left_edge, right_edge, squares = pl.pallas_call(
            functools.partial(strip_kernel, n, count, strip, offset, last),
            out_shape=[jax.ShapeDtypeStruct((size, local), BF16), edges, edges, squares_shape],
            in_specs=[SMEM] + [VMEM] * 8,
            out_specs=[VMEM] * 4,
            scratch_shapes=[pltpu.VMEM((DEGREE + 1, (strip + 2) * n, local), BF16)] * 2
            + [pltpu.VMEM((depth, n, wide), BF16)] * 2,
            compiler_params=params(),
            name="strip",
        )(band_me, left_y[index], right_y[index], left_edge, right_edge, rows, left_rows, right_rows, squares)
        chunks.append(gather_blocks(chunk))
        first = offset + DEGREE
        spans.append([(0, strip * n, first * n), (strip * n, strip * n, (count - first - strip) * n)])

    flat = [block for blocks in chunks for block in blocks]
    slice_rows = local // elem_size
    all_bands = local * band_size
    partial = pl.pallas_call(
        functools.partial(gram_kernel, len(chunks), band_size, elem_size),
        out_shape=jax.ShapeDtypeStruct((elem_size, slice_rows, all_bands + LANES), BF16),
        in_specs=[VMEM] * len(flat),
        out_specs=VMEM,
        compiler_params=params(),
        name="gram",
    )(*flat)
    got = lax.all_to_all(partial, "elem", 0, 0, tiled=True)
    mine = pl.pallas_call(
        functools.partial(weights_kernel, total_columns, band_size),
        out_shape=jax.ShapeDtypeStruct((elem_size, slice_rows, all_bands), BF16),
        in_specs=[SMEM, VMEM],
        out_specs=VMEM,
        compiler_params=params(),
        name="weights",
    )(elem_me, got)
    weights = lax.all_to_all(mine, "elem", 0, 0, tiled=True).reshape(local, all_bands)
    return pl.pallas_call(
        functools.partial(rotate_kernel, len(chunks), band_size, spans),
        out_shape=jax.ShapeDtypeStruct((local, count * n), BF16),
        in_specs=[VMEM] * (1 + len(flat)),
        out_specs=VMEM,
        compiler_params=params(),
        name="rotate",
    )(weights, *flat)


def identity_block(shape, offset):
    row_ids = lax.broadcasted_iota(jnp.int32, shape, 0) + offset
    col_ids = lax.broadcasted_iota(jnp.int32, shape, 1)
    return (row_ids == col_ids).astype(jnp.float32)


def rotation_columns(gram_strip, scales, offset, total_rows):
    own_scales = lax.dynamic_slice_in_dim(scales, offset, gram_strip.shape[0], 0)
    identity = identity_block(gram_strip.shape, offset)
    normed = own_scales[:, None] * gram_strip * scales[None, :]
    return (math.sqrt(total_rows) * scales[None, :] * (1.5 * identity - 0.5 * normed)).astype(
        jnp.bfloat16
    )


def general_shards(basis_sizes, coupling_pattern, h_diag, h_couple, bands):
    elem_local = h_diag.shape[0]
    basis_width = h_diag.shape[1]
    band_local = bands.shape[0]
    total_rows = elem_local * lax.axis_size("elem") * basis_width
    columns = lax.broadcasted_iota(jnp.int32, (elem_local, basis_width), 1)
    valid_rows = (columns < basis_sizes[:, None]).astype(jnp.float32)
    coupling = h_couple * coupling_pattern.astype(jnp.bfloat16)[:, None, None]
    current = (
        bands.reshape(band_local, elem_local, basis_width) * valid_rows.astype(jnp.bfloat16)[None]
    )
    previous = current
    for degree in range(DEGREE):
        current_float = current.astype(jnp.float32)
        local_term = jnp.einsum("eij,bej->bei", h_diag, current, preferred_element_type=jnp.float32)
        following = from_behind(current[:, 0], "elem", -1)
        ahead_rows = jnp.concatenate([current[:, 1:], following[:, None]], axis=1)
        upper_term = jnp.einsum(
            "eij,bej->bei", coupling, ahead_rows, preferred_element_type=jnp.float32
        )
        carried = jnp.einsum("eji,bej->bei", coupling, current, preferred_element_type=jnp.float32)
        arrived = from_behind(carried[:, -1], "elem", 1)
        lower_term = jnp.concatenate([arrived[:, None], carried[:, :-1]], axis=1)
        applied = (local_term + upper_term + lower_term) * valid_rows[None]
        shifted = applied - center_shift * current_float
        if degree == 0:
            next_iterate = shifted / half_width
        else:
            next_iterate = 2.0 * shifted / half_width - previous.astype(jnp.float32)
        previous, current = (current, next_iterate.astype(jnp.bfloat16))
    filtered = current.reshape(band_local, elem_local * basis_width)
    every_band = lax.all_gather(filtered, "band", axis=0, tiled=True)
    strip = lax.dot_general(
        filtered, every_band, (((1,), (1,)), ((), ())), preferred_element_type=jnp.float32
    )
    squares = jnp.sum(jnp.square(every_band.astype(jnp.float32)), axis=1)
    strip, squares = lax.psum((strip, squares), "elem")
    scales = lax.rsqrt(squares + epsilon_norm)
    offset = lax.axis_index("band") * band_local
    weights = rotation_columns(strip, scales, offset, total_rows)
    return jnp.dot(weights, every_band, preferred_element_type=jnp.float32).astype(jnp.bfloat16)


def shards(basis_sizes, coupling_pattern, h_diag, h_couple, bands):
    count, n = h_diag.shape[:2]
    local = bands.shape[0]
    elem_size, band_size = lax.axis_size("elem"), lax.axis_size("band")
    rows = local // elem_size
    wide = -(-(3 * n + 1) // LANES) * LANES
    fits = (
        band_size & (band_size - 1) == 0
        and wide % (band_size * LANES) == 0
        and local % LANES == 0
        and local % elem_size == 0
        and rows % 16 == 0
        and rows * LANES >= 2 * local * band_size
        and count > 2 * DEGREE
        and n % 16 == 0
    )
    form = fast_shards if fits else general_shards
    return form(basis_sizes, coupling_pattern, h_diag, h_couple, bands)


def solution(mesh):
    in_specs = (
        P("elem"),
        P("elem"),
        P("elem", None, None),
        P("elem", None, None),
        P("band", "elem"),
    )
    out_specs = P("band", "elem")
    return jax.shard_map(shards, mesh=mesh, in_specs=in_specs, out_specs=out_specs, check_vma=False)
```

```python
import functools
import math

import jax
import jax.numpy as jnp
from jax import lax
from jax.experimental import pallas as pl
from jax.experimental.pallas import tpu as pltpu
from jax.sharding import PartitionSpec as P

DEGREE = 6
STRIPS = (3, 3)
SPLIT = 2

center_shift = 0.4
half_width = 2.8
epsilon_norm = 1e-06

LANES = 128
VMEM = pl.BlockSpec(memory_space=pltpu.VMEM)
SMEM = pl.BlockSpec(memory_space=pltpu.SMEM)
BF16 = jnp.bfloat16
F32 = jnp.float32


def from_behind(value, axis, steps):
    count = lax.axis_size(axis)
    pairs = [(source, (source + steps) % count) for source in range(count)]
    return lax.ppermute(value, axis, pairs)


def swap(value, axis, bit):
    count = lax.axis_size(axis)
    return lax.ppermute(value, axis, [(source, source ^ bit) for source in range(count)])


def after(value, *others):
    return lax.optimization_barrier((value, *others))[0]


def params(mib):
    return pltpu.CompilerParams(vmem_limit_bytes=mib * 1024 * 1024)


def about(microseconds):
    return pl.CostEstimate(flops=int(microseconds * 1.15e9), bytes_accessed=1, transcendentals=0)


def rows_kernel(width, lanes, me_ref, sizes_ref, pattern_ref, diag_ref, couple_ref, rows_ref, first_ref, last_ref):
    n = width
    count = rows_ref.shape[0]
    depth = DEGREE - 1
    wide = rows_ref.shape[2]
    place = lax.broadcasted_iota(jnp.int32, (n, wide), 0)
    behind = jnp.zeros((n, n), F32)
    ones = jnp.ones((n, wide - 3 * n), F32)
    for e in range(count):
        couple = couple_ref[e].astype(F32) * pattern_ref[e].astype(F32)
        whole = jnp.concatenate([behind, diag_ref[e].astype(F32), couple, ones], axis=1)
        rows_ref[e] = jnp.where(place < sizes_ref[e], whole, 0.0).astype(BF16)
        behind = jnp.transpose(couple)
    at = pl.ds(pl.multiple_of(me_ref[0] * lanes, lanes), lanes)
    for e in range(depth):
        first_ref[e * n : (e + 1) * n, :] = rows_ref[e, :, at]
        last_ref[e * n : (e + 1) * n, :] = rows_ref[count - depth + e, :, at]


def vectors_kernel(width, count, group, sizes_ref, bands_ref, out_ref, *edge_refs):
    n = width
    local = bands_ref.shape[0]
    place = lax.broadcasted_iota(jnp.int32, (n, local), 0)
    for begin in range(0, count, group):
        turned = jnp.transpose(bands_ref[:, begin * n : (begin + group) * n])
        for e in range(begin, begin + group):
            part = turned[(e - begin) * n : (e - begin + 1) * n, :].astype(F32)
            out_ref[e * n : (e + 1) * n, :] = jnp.where(place < sizes_ref[e], part, 0.0).astype(BF16)
    near = 0
    for index, strip in enumerate(STRIPS):
        far = near + strip
        edge_refs[2 * index][...] = out_ref[near * n : far * n, :]
        edge_refs[2 * index + 1][...] = out_ref[(count - far) * n : (count - near) * n, :]
        near = far


def advance(row, window, center, before, first):
    total = jnp.dot(row, window, preferred_element_type=F32)
    shifted = total - center_shift * center.astype(F32)
    if first:
        return (shifted * (1.0 / half_width)).astype(BF16)
    return (shifted * (2.0 / half_width) - before.astype(F32)).astype(BF16)


def add_squares(total, values):
    values = values.astype(F32)
    return total + jnp.sum(values * values, axis=0, keepdims=True)


def interior_kernel(width, count, begin, end, rows_ref, *refs):
    n = width
    if begin == 0:
        first_ref, refs = refs[0], refs[1:]
    else:
        older_ref, newer_ref, refs = refs[0], refs[1], refs[2:]
    if end < DEGREE:
        left_ref, right_ref, even_ref, odd_ref = refs
    else:
        left_ref, right_ref, out_ref, squares_ref, even_ref, odd_ref = refs
    buffers = (even_ref, odd_ref)
    for step in range(begin, end):
        source = buffers[step % 2]
        older = target = buffers[(step + 1) % 2]
        if step == begin:
            source = first_ref if begin == 0 else newer_ref
        if step == 1 and begin == 0:
            older = first_ref
        elif step == begin and begin > 0:
            older = older_ref
        elif step == begin + 1 and begin > 0:
            older = newer_ref
        left_ref[step - begin] = source[step * n : (step + 2) * n, :]
        right_ref[step - begin] = source[(count - step - 2) * n : (count - step) * n, :]

        def body(e, carry):
            at = pl.multiple_of(e * n, 16)
            window = source[pl.ds(pl.multiple_of((e - 1) * n, 16), 3 * n), :]
            center = source[pl.ds(at, n), :]
            before = older[pl.ds(at, n), :]
            target[pl.ds(at, n), :] = advance(rows_ref[e, :, : 3 * n], window, center, before, step == 0)
            return carry

        lax.fori_loop(step + 1, count - 1 - step, body, 0, unroll=2)
    if end == DEGREE:
        result = buffers[DEGREE % 2][DEGREE * n : (count - DEGREE) * n, :]
        out_ref[...] = result
        squares_ref[...] = add_squares(jnp.zeros(squares_ref.shape, F32), result)


def strip_kernel(
    width,
    count,
    strip,
    offset,
    last,
    edge_sizes,
    pieces,
    me_ref,
    left_y_ref,
    right_y_ref,
    rows_ref,
    squares_in_ref,
    *refs,
):
    n = width
    depth = DEGREE - 1
    me = me_ref[0]
    refs, outs = refs[:-8], refs[-8:]
    all_ref = outs[1]
    half = len(edge_sizes)
    left_edge = [ref.at[k] for ref, size in zip(refs[:half], edge_sizes) for k in range(size)]
    right_edge = [ref.at[k] for ref, size in zip(refs[half : 2 * half], edge_sizes) for k in range(size)]
    refs = refs[2 * half :]
    before = refs[4 * pieces :]
    out_ref, left_out_ref, right_out_ref, squares_ref, left_scr, right_scr, halo_left, halo_right = outs
    lanes = refs[0].shape[1]
    for index in range(pieces):
        for side in range(2):
            at = pl.ds(pl.multiple_of((me ^ (side * pieces + index)) * lanes, lanes), lanes)
            halo_left[:, :, at] = refs[2 * side * pieces + index][...].reshape(depth, n, lanes)
            halo_right[:, :, at] = refs[(2 * side + 1) * pieces + index][...].reshape(depth, n, lanes)

    def left_row(e):
        if e < 0:
            return halo_left[depth + e, :, : 3 * n]
        if e > 0:
            return rows_ref[e, :, : 3 * n]
        turned = jnp.transpose(halo_left[depth - 1, :, 2 * n : 3 * n].astype(F32))
        keep = rows_ref[0, :, 3 * n : 3 * n + 1].astype(F32)
        return jnp.concatenate([(turned * keep).astype(BF16), rows_ref[0, :, n : 3 * n]], axis=1)

    def right_row(e):
        if e < count:
            return rows_ref[e, :, : 3 * n]
        if e > count:
            return halo_right[e - count, :, : 3 * n]
        turned = jnp.transpose(rows_ref[count - 1, :, 2 * n : 3 * n].astype(F32))
        keep = halo_right[0, :, 3 * n : 3 * n + 1].astype(F32)
        return jnp.concatenate([(turned * keep).astype(BF16), halo_right[0, :, n : 3 * n]], axis=1)

    left_scr[0, : strip * n, :] = left_y_ref[...]
    right_scr[0, 2 * n :, :] = right_y_ref[...]
    for step in range(DEGREE):
        left_scr[step, strip * n :, :] = left_edge[step][...]
        right_scr[step, : 2 * n, :] = right_edge[step][...]
        for j in range(strip):
            e = offset + step + 1 + j
            left_scr[step + 1, j * n : (j + 1) * n, :] = advance(
                left_row(e),
                left_scr[step, j * n : (j + 3) * n, :],
                left_scr[step, (j + 1) * n : (j + 2) * n, :],
                left_scr[max(step - 1, 0), (j + 2) * n : (j + 3) * n, :],
                step == 0,
            )
            e = count - 1 - (offset + strip + step) + j
            right_scr[step + 1, (j + 2) * n : (j + 3) * n, :] = advance(
                right_row(e),
                right_scr[step, j * n : (j + 3) * n, :],
                right_scr[step, (j + 1) * n : (j + 2) * n, :],
                right_scr[max(step - 1, 0), j * n : (j + 1) * n, :],
                step == 0,
            )
        if not last:
            left_out_ref[step] = left_scr[step, : 2 * n, :]
            right_out_ref[step] = right_scr[step, strip * n : (strip + 2) * n, :]
    result_left = left_scr[DEGREE, : strip * n, :]
    result_right = right_scr[DEGREE, 2 * n :, :]
    out_ref[: strip * n, :] = result_left
    out_ref[strip * n : 2 * strip * n, :] = result_right
    squares = add_squares(add_squares(squares_in_ref[...], result_left), result_right)
    squares_ref[...] = squares
    if last:
        high = squares.astype(BF16).astype(F32)
        low = squares - high
        place = lax.broadcasted_iota(jnp.int32, (16, squares.shape[1]), 0)
        both = jnp.where(place == 0, high, jnp.where(place == 1, low, 0.0))
        out_ref[2 * strip * n :, :] = both.astype(BF16)
        begin = 0
        for ref in (*before, out_ref):
            all_ref[begin : begin + ref.shape[0], :] = ref[...]
            begin += ref.shape[0]


def gram_kernel(chunks, blocks, shares, early, *refs):
    outs = refs[-2:] if early else refs[-1:]
    out_ref = outs[0]
    half = blocks // 2
    rows = out_ref.shape[1]
    lower = refs[:half]
    local = lower[0].shape[1]
    length = lower[0].shape[0] - 16
    totals = [None] * half
    if early:
        turned_ref = outs[1]
        turned_ref[...] = jnp.transpose(lower[0][:length, :])
        for r in range(half):
            totals[r] = jnp.dot(turned_ref[...], lower[r][:length, :], preferred_element_type=F32)
    else:
        turned_ref = refs[half]
        begin = 0
        upper = [refs[half + 1 + c * half : half + 1 + (c + 1) * half] for c in range(chunks)]
        for c in range(chunks):
            size = upper[c][0].shape[0] - (16 if c == chunks - 1 else 0)
            for r in range(half):
                term = jnp.dot(
                    turned_ref[:, begin : begin + size], upper[c][r][:size, :], preferred_element_type=F32
                )
                totals[r] = term if c == 0 else totals[r] + term
            begin += size
    base = 0 if early else half
    for r in range(half):
        at = (base + r) * local
        out_ref[:, :, at : at + local] = totals[r].astype(BF16).reshape(shares, rows, local)
    if early:
        return
    out_ref[:, :, : half * local] = refs[-2][...]
    place = lax.broadcasted_iota(jnp.int32, (rows, LANES), 0)
    parts = local // LANES
    extra = jnp.zeros((rows, LANES), F32)
    for r in range(blocks):
        ref = lower[r] if r < half else upper[-1][r - half]
        both = ref[ref.shape[0] - 16 :, :].astype(F32)
        for p in range(parts):
            for part in range(2):
                line = both[part : part + 1, p * LANES : (p + 1) * LANES]
                extra = jnp.where(place == part * blocks * parts + r * parts + p, line, extra)
    for share in range(shares):
        out_ref[share, :, blocks * local :] = extra.astype(BF16)


def weights_kernel(total_columns, blocks, me_ref, got_ref, out_ref):
    shares, rows, wide = got_ref.shape
    bands = wide - LANES
    local = bands // blocks
    parts = bands // LANES
    total = got_ref[0].astype(F32)
    for share in range(1, shares):
        total = total + got_ref[share].astype(F32)
    tail = total[:, bands:]
    squares = tail[:parts, :] + tail[parts : 2 * parts, :]
    scales = lax.rsqrt(squares + epsilon_norm)
    me = me_ref[0]
    first = me * rows
    row_ids = lax.broadcasted_iota(jnp.int32, (rows, LANES), 0) + first
    lane_ids = lax.broadcasted_iota(jnp.int32, (rows, LANES), 1)
    own = jnp.zeros((rows, 1), F32)
    for p in range(local // LANES):
        hit = row_ids == lane_ids + p * LANES
        own = own + jnp.sum(jnp.where(hit, scales[p : p + 1, :], 0.0), axis=1, keepdims=True)
    for p in range(parts):
        part = total[:, p * LANES : (p + 1) * LANES]
        across = scales[p : p + 1, :]
        diagonal = 0.0
        if p < local // LANES:
            hit = row_ids == lane_ids + p * LANES
            part = jnp.where(hit, squares[p : p + 1, :], part)
            diagonal = jnp.where(hit, 1.5, 0.0)
        weights = math.sqrt(total_columns) * across * (diagonal - 0.5 * (own * part * across))
        weights = weights.astype(BF16)
        for share in range(shares):
            out_ref[share, :, p * LANES : (p + 1) * LANES] = weights


def rotate_kernel(chunks, blocks, spans, weights_ref, *refs):
    out_ref = refs[-1]
    half = blocks // 2
    lower = refs[:half]
    upper = [refs[half + c * half : half + (c + 1) * half] for c in range(chunks)]
    local = lower[0].shape[1]
    start = 0
    for c in range(chunks):
        for begin, size, column in spans[c]:
            total = None
            for r in range(blocks):
                if r < half:
                    part = lower[r][start + begin : start + begin + size, :]
                else:
                    part = upper[c][r - half][begin : begin + size, :]
                term = lax.dot_general(
                    weights_ref[:, r * local : (r + 1) * local],
                    part,
                    (((1,), (1,)), ((), ())),
                    preferred_element_type=F32,
                )
                total = term if total is None else total + term
            out_ref[:, column : column + size] = total.astype(BF16)
        start += sum(size for _, size, _ in spans[c])


def lower_blocks(own):
    bit = lax.axis_size("band") // 4
    found = {0: own}
    while bit:
        for index in list(found):
            found[index ^ bit] = swap(found[index], "band", bit)
        bit //= 2
    return [found[index] for index in sorted(found)]


def fast_shards(basis_sizes, coupling_pattern, h_diag, h_couple, bands):
    count, n = h_diag.shape[:2]
    local = bands.shape[0]
    elem_size, band_size = lax.axis_size("elem"), lax.axis_size("band")
    total_columns = elem_size * count * n
    depth = DEGREE - 1
    wide = -(-(3 * n + 1) // LANES) * LANES
    lanes = wide // band_size
    half = band_size // 2
    elem_me = lax.axis_index("elem").astype(jnp.int32).reshape(1)
    band_me = lax.axis_index("band").astype(jnp.int32).reshape(1)

    rows, first_rows, last_rows = pl.pallas_call(
        functools.partial(rows_kernel, n, lanes),
        out_shape=[jax.ShapeDtypeStruct((count, n, wide), BF16)]
        + [jax.ShapeDtypeStruct((depth * n, lanes), BF16)] * 2,
        in_specs=[SMEM] * 3 + [VMEM] * 2,
        out_specs=[VMEM] * 3,
        compiler_params=params(16),
        cost_estimate=about(0.01),
        name="rows",
    )(band_me, basis_sizes, coupling_pattern, h_diag, h_couple)
    left_rows = from_behind(last_rows, "elem", 1)
    right_rows = from_behind(first_rows, "elem", -1)

    start, *ends = pl.pallas_call(
        functools.partial(vectors_kernel, n, count, math.lcm(n, LANES) // n),
        out_shape=[jax.ShapeDtypeStruct((count * n, local), BF16)]
        + [jax.ShapeDtypeStruct((strip * n, local), BF16) for strip in STRIPS for _ in range(2)],
        in_specs=[SMEM, VMEM],
        out_specs=[VMEM] * (1 + 2 * len(STRIPS)),
        compiler_params=params(16),
        cost_estimate=about(0.01),
        name="vectors",
    )(basis_sizes, bands)
    left_y = [from_behind(ends[2 * index + 1], "elem", 1) for index in range(len(STRIPS))]
    right_y = [from_behind(ends[2 * index], "elem", -1) for index in range(len(STRIPS))]

    inner = (count - 2 * DEGREE) * n
    whole = jax.ShapeDtypeStruct((count * n, local), BF16)
    squares_shape = jax.ShapeDtypeStruct((1, local), F32)

    def edges(steps):
        return [jax.ShapeDtypeStruct((steps, 2 * n, local), BF16)] * 2

    left_edge, right_edge, even, odd = pl.pallas_call(
        functools.partial(interior_kernel, n, count, 0, SPLIT),
        out_shape=edges(SPLIT) + [whole] * 2,
        in_specs=[VMEM] * 2,
        out_specs=[VMEM] * 4,
        compiler_params=params(20),
        cost_estimate=about(0.01),
        name="interior_first",
    )(rows, start)
    own_rows = [after(side, even) for side in (left_rows, right_rows)]
    across_rows = [swap(side, "band", half) for side in own_rows]
    older, newer = (odd, even) if SPLIT % 2 == 0 else (even, odd)
    left_more, right_more, chunk, squares = pl.pallas_call(
        functools.partial(interior_kernel, n, count, SPLIT, DEGREE),
        out_shape=edges(DEGREE - SPLIT) + [jax.ShapeDtypeStruct((inner, local), BF16), squares_shape],
        in_specs=[VMEM] * 3,
        out_specs=[VMEM] * 4,
        scratch_shapes=[pltpu.VMEM((count * n, local), BF16)] * 2,
        compiler_params=params(20),
        cost_estimate=about(0.01),
        name="interior_rest",
    )(rows, older, newer)
    left_edge = [left_edge, left_more]
    right_edge = [right_edge, right_more]
    across_rows = [after(side, chunk, left_y[0], right_y[0]) for side in across_rows]
    both = [block for side in (*own_rows, *across_rows) for block in lower_blocks(side)]
    chunks, across = [chunk], [swap(chunk, "band", half)]
    spans = [[(0, inner, DEGREE * n)]]
    offset = 0
    for index, strip in enumerate(STRIPS):
        last = index == len(STRIPS) - 1
        offset -= strip
        if index:
            left_edge = [after(left_edge[0], across[index - 1])]
        size = 2 * strip * n + (16 if last else 0)
        sizes = [edge.shape[0] for edge in left_edge]
        shape = jax.ShapeDtypeStruct((size, local), BF16)
        full = jax.ShapeDtypeStruct((count * n + 16, local), BF16)
        before = chunks if last else []
        chunk, *others, squares = pl.pallas_call(
            functools.partial(strip_kernel, n, count, strip, offset, last, sizes, half),
            out_shape=[shape, *([full, jax.ShapeDtypeStruct((8, LANES), F32)] if last else edges(DEGREE)), squares_shape],
            in_specs=[SMEM] + [VMEM] * (4 + 2 * len(sizes) + 4 * half + len(before)),
            out_specs=[VMEM] * 4,
            scratch_shapes=[pltpu.VMEM((DEGREE + 1, (strip + 2) * n, local), BF16)] * 2
            + [pltpu.VMEM((depth, n, wide), BF16)] * 2,
            compiler_params=params(32),
            cost_estimate=about(3),
            name="strip",
        )(band_me, left_y[index], right_y[index], rows, squares, *left_edge, *right_edge, *both, *before)
        left_edge, right_edge = [others[0]], [others[1]]
        if last:
            own = others[0]
            chunk = after(chunk, across[index])
        chunks.append(chunk)
        across.append(swap(chunk, "band", half))
        first = offset + DEGREE
        spans.append([(0, strip * n, first * n), (strip * n, strip * n, (count - first - strip) * n)])

    slice_rows = local // elem_size
    all_bands = local * band_size

    def gram(early, blocks):
        wide = all_bands // 2 if early else all_bands + LANES
        shapes = [jax.ShapeDtypeStruct((elem_size, slice_rows, wide), BF16)]
        if early:
            shapes.append(jax.ShapeDtypeStruct((local, count * n), BF16))
        return pl.pallas_call(
            functools.partial(gram_kernel, len(chunks), band_size, elem_size, early),
            out_shape=shapes,
            in_specs=[VMEM] * len(blocks),
            out_specs=[VMEM] * len(shapes),
            compiler_params=params(20),
            cost_estimate=about(0.01),
            name="gram_early" if early else "gram_late",
        )(*blocks)

    lower = lower_blocks(after(own, across[-2]))
    early, turned = gram(True, lower)
    upper = [block for chunk in across for block in lower_blocks(chunk)]
    (partial,) = gram(False, [*lower, turned, *upper, early])
    got = lax.all_to_all(partial, "elem", 0, 0, tiled=True)
    flat = [*lower, *upper]
    mine = pl.pallas_call(
        functools.partial(weights_kernel, total_columns, band_size),
        out_shape=jax.ShapeDtypeStruct((elem_size, slice_rows, all_bands), BF16),
        in_specs=[SMEM, VMEM],
        out_specs=VMEM,
        compiler_params=params(8),
        cost_estimate=about(0.01),
        name="weights",
    )(elem_me, got)
    weights = lax.all_to_all(mine, "elem", 0, 0, tiled=True).reshape(local, all_bands)
    return pl.pallas_call(
        functools.partial(rotate_kernel, len(chunks), band_size, spans),
        out_shape=jax.ShapeDtypeStruct((local, count * n), BF16),
        in_specs=[VMEM] * (1 + len(flat)),
        out_specs=VMEM,
        compiler_params=params(24),
        cost_estimate=about(0.01),
        name="rotate",
    )(weights, *flat)


def identity_block(shape, offset):
    row_ids = lax.broadcasted_iota(jnp.int32, shape, 0) + offset
    col_ids = lax.broadcasted_iota(jnp.int32, shape, 1)
    return (row_ids == col_ids).astype(jnp.float32)


def rotation_columns(gram_strip, scales, offset, total_rows):
    own_scales = lax.dynamic_slice_in_dim(scales, offset, gram_strip.shape[0], 0)
    identity = identity_block(gram_strip.shape, offset)
    normed = own_scales[:, None] * gram_strip * scales[None, :]
    return (math.sqrt(total_rows) * scales[None, :] * (1.5 * identity - 0.5 * normed)).astype(
        jnp.bfloat16
    )


def general_shards(basis_sizes, coupling_pattern, h_diag, h_couple, bands):
    elem_local = h_diag.shape[0]
    basis_width = h_diag.shape[1]
    band_local = bands.shape[0]
    total_rows = elem_local * lax.axis_size("elem") * basis_width
    columns = lax.broadcasted_iota(jnp.int32, (elem_local, basis_width), 1)
    valid_rows = (columns < basis_sizes[:, None]).astype(jnp.float32)
    coupling = h_couple * coupling_pattern.astype(jnp.bfloat16)[:, None, None]
    current = (
        bands.reshape(band_local, elem_local, basis_width) * valid_rows.astype(jnp.bfloat16)[None]
    )
    previous = current
    for degree in range(DEGREE):
        current_float = current.astype(jnp.float32)
        local_term = jnp.einsum("eij,bej->bei", h_diag, current, preferred_element_type=jnp.float32)
        following = from_behind(current[:, 0], "elem", -1)
        ahead_rows = jnp.concatenate([current[:, 1:], following[:, None]], axis=1)
        upper_term = jnp.einsum(
            "eij,bej->bei", coupling, ahead_rows, preferred_element_type=jnp.float32
        )
        carried = jnp.einsum("eji,bej->bei", coupling, current, preferred_element_type=jnp.float32)
        arrived = from_behind(carried[:, -1], "elem", 1)
        lower_term = jnp.concatenate([arrived[:, None], carried[:, :-1]], axis=1)
        applied = (local_term + upper_term + lower_term) * valid_rows[None]
        shifted = applied - center_shift * current_float
        if degree == 0:
            next_iterate = shifted / half_width
        else:
            next_iterate = 2.0 * shifted / half_width - previous.astype(jnp.float32)
        previous, current = (current, next_iterate.astype(jnp.bfloat16))
    filtered = current.reshape(band_local, elem_local * basis_width)
    every_band = lax.all_gather(filtered, "band", axis=0, tiled=True)
    strip = lax.dot_general(
        filtered, every_band, (((1,), (1,)), ((), ())), preferred_element_type=jnp.float32
    )
    squares = jnp.sum(jnp.square(every_band.astype(jnp.float32)), axis=1)
    strip, squares = lax.psum((strip, squares), "elem")
    scales = lax.rsqrt(squares + epsilon_norm)
    offset = lax.axis_index("band") * band_local
    weights = rotation_columns(strip, scales, offset, total_rows)
    return jnp.dot(weights, every_band, preferred_element_type=jnp.float32).astype(jnp.bfloat16)


def shards(basis_sizes, coupling_pattern, h_diag, h_couple, bands):
    count, n = h_diag.shape[:2]
    local = bands.shape[0]
    elem_size, band_size = lax.axis_size("elem"), lax.axis_size("band")
    rows = local // elem_size
    wide = -(-(3 * n + 1) // LANES) * LANES
    fits = (
        band_size & (band_size - 1) == 0
        and wide % (band_size * LANES) == 0
        and local % LANES == 0
        and local % elem_size == 0
        and rows % 16 == 0
        and rows * LANES >= 2 * local * band_size
        and count > 2 * DEGREE
        and n % 16 == 0
    )
    form = fast_shards if fits else general_shards
    return form(basis_sizes, coupling_pattern, h_diag, h_couple, bands)


def solution(mesh):
    in_specs = (
        P("elem"),
        P("elem"),
        P("elem", None, None),
        P("elem", None, None),
        P("band", "elem"),
    )
    out_specs = P("band", "elem")
    return jax.shard_map(shards, mesh=mesh, in_specs=in_specs, out_specs=out_specs, check_vma=False)
```

```python
import functools
import math

import jax
import jax.numpy as jnp
from jax import lax
from jax.experimental import pallas as pl
from jax.experimental.pallas import tpu as pltpu
from jax.sharding import PartitionSpec as P

DEGREE = 6
STRIPS = (3, 3)
SPLIT = 2

center_shift = 0.4
half_width = 2.8
epsilon_norm = 1e-06

LANES = 128
VMEM = pl.BlockSpec(memory_space=pltpu.VMEM)
HBM = pl.BlockSpec(memory_space=pltpu.HBM)
SMEM = pl.BlockSpec(memory_space=pltpu.SMEM)
BF16 = jnp.bfloat16
F32 = jnp.float32


def from_behind(value, axis, steps):
    count = lax.axis_size(axis)
    pairs = [(source, (source + steps) % count) for source in range(count)]
    return lax.ppermute(value, axis, pairs)


def swap(value, axis, bit):
    count = lax.axis_size(axis)
    return lax.ppermute(value, axis, [(source, source ^ bit) for source in range(count)])


def after(value, *others):
    return lax.optimization_barrier((value, *others))[0]


def params(mib):
    return pltpu.CompilerParams(vmem_limit_bytes=mib * 1024 * 1024)


def about(microseconds):
    return pl.CostEstimate(flops=int(microseconds * 1.15e9), bytes_accessed=1, transcendentals=0)


def rows_kernel(
    width, lanes, me_ref, sizes_in, pattern_in, diag_in, couple_in, rows_ref, first_ref, last_ref, *scratch
):
    sizes_ref, pattern_ref, diag_ref, couple_ref, scalar_sems, diag_sems, couple_sems = scratch
    parts = diag_sems.shape[0]
    each = diag_in.shape[0] // parts
    scalars = [
        pltpu.make_async_copy(sizes_in, sizes_ref, scalar_sems.at[0]),
        pltpu.make_async_copy(pattern_in, pattern_ref, scalar_sems.at[1]),
    ]
    blocks = []
    for part in range(parts):
        at = pl.ds(part * each, each)
        blocks.append(pltpu.make_async_copy(couple_in.at[at], couple_ref.at[at], couple_sems.at[part]))
        blocks.append(pltpu.make_async_copy(diag_in.at[at], diag_ref.at[at], diag_sems.at[part]))
    for copy in scalars + blocks:
        copy.start()
    for copy in scalars:
        copy.wait()
    n = width
    count = rows_ref.shape[0]
    depth = DEGREE - 1
    wide = rows_ref.shape[2]
    place = lax.broadcasted_iota(jnp.int32, (n, wide), 0)
    behind = jnp.zeros((n, n), F32)
    ones = jnp.ones((n, wide - 3 * n), F32)
    for e in range(count):
        if e % each == 0:
            blocks[2 * (e // each)].wait()
            blocks[2 * (e // each) + 1].wait()
        couple = couple_ref[e].astype(F32) * pattern_ref[e].astype(F32)
        whole = jnp.concatenate([behind, diag_ref[e].astype(F32), couple, ones], axis=1)
        rows_ref[e] = jnp.where(place < sizes_ref[e], whole, 0.0).astype(BF16)
        behind = jnp.transpose(couple)
    at = pl.ds(pl.multiple_of(me_ref[0] * lanes, lanes), lanes)
    for e in range(depth):
        first_ref[e * n : (e + 1) * n, :] = rows_ref[e, :, at]
        last_ref[e * n : (e + 1) * n, :] = rows_ref[count - depth + e, :, at]


def vectors_kernel(width, count, group, sizes_ref, bands_ref, out_ref, first_ref, last_ref):
    n = width
    local = bands_ref.shape[0]
    place = lax.broadcasted_iota(jnp.int32, (n, local), 0)
    for begin in range(0, count, group):
        turned = jnp.transpose(bands_ref[:, begin * n : (begin + group) * n])
        for e in range(begin, begin + group):
            part = turned[(e - begin) * n : (e - begin + 1) * n, :].astype(F32)
            out_ref[e * n : (e + 1) * n, :] = jnp.where(place < sizes_ref[e], part, 0.0).astype(BF16)
    first_ref[...] = out_ref[: DEGREE * n, :]
    last_ref[...] = out_ref[(count - DEGREE) * n :, :]


def advance(row, window, center, before, first):
    total = jnp.dot(row, window, preferred_element_type=F32)
    shifted = total - center_shift * center.astype(F32)
    if first:
        return (shifted * (1.0 / half_width)).astype(BF16)
    return (shifted * (2.0 / half_width) - before.astype(F32)).astype(BF16)


def add_squares(total, values):
    values = values.astype(F32)
    return total + jnp.sum(values * values, axis=0, keepdims=True)


def interior_kernel(width, count, begin, end, rows_ref, *refs):
    n = width
    if begin == 0:
        first_ref, refs = refs[0], refs[1:]
    else:
        older_ref, newer_ref, refs = refs[0], refs[1], refs[2:]
    if end < DEGREE:
        left_ref, right_ref, even_ref, odd_ref = refs
    else:
        left_ref, right_ref, out_ref, squares_ref, even_ref, odd_ref = refs
    buffers = (even_ref, odd_ref)
    for step in range(begin, end):
        source = buffers[step % 2]
        older = target = buffers[(step + 1) % 2]
        if step == begin:
            source = first_ref if begin == 0 else newer_ref
        if step == 1 and begin == 0:
            older = first_ref
        elif step == begin and begin > 0:
            older = older_ref
        elif step == begin + 1 and begin > 0:
            older = newer_ref
        left_ref[step - begin] = source[step * n : (step + 2) * n, :]
        right_ref[step - begin] = source[(count - step - 2) * n : (count - step) * n, :]

        def body(e, carry):
            at = pl.multiple_of(e * n, 16)
            window = source[pl.ds(pl.multiple_of((e - 1) * n, 16), 3 * n), :]
            center = source[pl.ds(at, n), :]
            before = older[pl.ds(at, n), :]
            target[pl.ds(at, n), :] = advance(rows_ref[e, :, : 3 * n], window, center, before, step == 0)
            return carry

        lax.fori_loop(step + 1, count - 1 - step, body, 0, unroll=2)
    if end == DEGREE:
        result = buffers[DEGREE % 2][DEGREE * n : (count - DEGREE) * n, :]
        out_ref[...] = result
        squares_ref[...] = add_squares(jnp.zeros(squares_ref.shape, F32), result)


def strip_kernel(
    width,
    count,
    strip,
    offset,
    last,
    edge_sizes,
    pieces,
    me_ref,
    left_y_ref,
    right_y_ref,
    rows_ref,
    squares_in_ref,
    *refs,
):
    n = width
    depth = DEGREE - 1
    me = me_ref[0]
    refs, outs = refs[:-8], refs[-8:]
    half = len(edge_sizes)
    left_edge = [ref.at[k] for ref, size in zip(refs[:half], edge_sizes) for k in range(size)]
    right_edge = [ref.at[k] for ref, size in zip(refs[half : 2 * half], edge_sizes) for k in range(size)]
    refs = refs[2 * half :]
    out_ref, left_out_ref, right_out_ref, squares_ref, left_scr, right_scr, halo_left, halo_right = outs
    lanes = refs[0].shape[1]
    for index in range(pieces):
        for side in range(2):
            at = pl.ds(pl.multiple_of((me ^ (side * pieces + index)) * lanes, lanes), lanes)
            halo_left[:, :, at] = refs[2 * side * pieces + index][...].reshape(depth, n, lanes)
            halo_right[:, :, at] = refs[(2 * side + 1) * pieces + index][...].reshape(depth, n, lanes)

    def left_row(e):
        if e < 0:
            return halo_left[depth + e, :, : 3 * n]
        if e > 0:
            return rows_ref[e, :, : 3 * n]
        turned = jnp.transpose(halo_left[depth - 1, :, 2 * n : 3 * n].astype(F32))
        keep = rows_ref[0, :, 3 * n : 3 * n + 1].astype(F32)
        return jnp.concatenate([(turned * keep).astype(BF16), rows_ref[0, :, n : 3 * n]], axis=1)

    def right_row(e):
        if e < count:
            return rows_ref[e, :, : 3 * n]
        if e > count:
            return halo_right[e - count, :, : 3 * n]
        turned = jnp.transpose(rows_ref[count - 1, :, 2 * n : 3 * n].astype(F32))
        keep = halo_right[0, :, 3 * n : 3 * n + 1].astype(F32)
        return jnp.concatenate([(turned * keep).astype(BF16), halo_right[0, :, n : 3 * n]], axis=1)

    near = -offset - strip
    left_scr[0, : strip * n, :] = left_y_ref[(DEGREE + offset) * n : (DEGREE - near) * n, :]
    right_scr[0, 2 * n :, :] = right_y_ref[near * n : (near + strip) * n, :]
    for step in range(DEGREE):
        left_scr[step, strip * n :, :] = left_edge[step][...]
        right_scr[step, : 2 * n, :] = right_edge[step][...]
        for j in range(strip):
            e = offset + step + 1 + j
            left_scr[step + 1, j * n : (j + 1) * n, :] = advance(
                left_row(e),
                left_scr[step, j * n : (j + 3) * n, :],
                left_scr[step, (j + 1) * n : (j + 2) * n, :],
                left_scr[max(step - 1, 0), (j + 2) * n : (j + 3) * n, :],
                step == 0,
            )
            e = count - 1 - (offset + strip + step) + j
            right_scr[step + 1, (j + 2) * n : (j + 3) * n, :] = advance(
                right_row(e),
                right_scr[step, j * n : (j + 3) * n, :],
                right_scr[step, (j + 1) * n : (j + 2) * n, :],
                right_scr[max(step - 1, 0), j * n : (j + 1) * n, :],
                step == 0,
            )
        if not last:
            left_out_ref[step] = left_scr[step, : 2 * n, :]
            right_out_ref[step] = right_scr[step, strip * n : (strip + 2) * n, :]
    result_left = left_scr[DEGREE, : strip * n, :]
    result_right = right_scr[DEGREE, 2 * n :, :]
    out_ref[: strip * n, :] = result_left
    out_ref[strip * n : 2 * strip * n, :] = result_right
    squares = add_squares(add_squares(squares_in_ref[...], result_left), result_right)
    squares_ref[...] = squares
    if last:
        high = squares.astype(BF16).astype(F32)
        low = squares - high
        place = lax.broadcasted_iota(jnp.int32, (16, squares.shape[1]), 0)
        both = jnp.where(place == 0, high, jnp.where(place == 1, low, 0.0))
        out_ref[2 * strip * n :, :] = both.astype(BF16)


def gram_kernel(chunks, half, shares, early, *refs):
    if early:
        refs, (out_ref, tails_ref, turned_ref) = refs[:-3], refs[-3:]
    else:
        early_ref, turned_ref, tails_ref, *refs, out_ref = refs
    grid = [refs[c * half : (c + 1) * half] for c in range(chunks)]
    rows = out_ref.shape[1]
    local = grid[0][0].shape[1]
    sizes = [grid[c][0].shape[0] - (16 if c == chunks - 1 else 0) for c in range(chunks)]
    places = [slice(sum(sizes[:c]), sum(sizes[: c + 1])) for c in range(chunks)]
    tails = [grid[-1][r][sizes[-1] :, :] for r in range(half)]
    if early:
        for c in range(chunks):
            turned_ref[:, places[c]] = jnp.transpose(grid[c][0][: sizes[c], :])
        for r in range(half):
            tails_ref[r] = tails[r]
    for r in range(half):
        total = None
        for c in range(chunks):
            term = jnp.dot(turned_ref[:, places[c]], grid[c][r][: sizes[c], :], preferred_element_type=F32)
            total = term if c == 0 else total + term
        at = (r if early else half + r) * local
        out_ref[:, :, at : at + local] = total.astype(BF16).reshape(shares, rows, local)
    if early:
        return
    out_ref[:, :, : half * local] = early_ref[...]
    place = lax.broadcasted_iota(jnp.int32, (rows, LANES), 0)
    parts = local // LANES
    extra = jnp.zeros((rows, LANES), F32)
    for r in range(2 * half):
        both = (tails_ref[r] if r < half else tails[r - half]).astype(F32)
        for p in range(parts):
            for part in range(2):
                line = both[part : part + 1, p * LANES : (p + 1) * LANES]
                extra = jnp.where(place == part * 2 * half * parts + r * parts + p, line, extra)
    for share in range(shares):
        out_ref[share, :, 2 * half * local :] = extra.astype(BF16)


def halves(squares, rows):
    high = squares.astype(BF16).astype(F32)
    spare = jnp.zeros((rows - 2 * squares.shape[0], LANES), F32)
    return jnp.concatenate([high, squares - high, spare])


def sums_kernel(got_ref, mine_ref, send_ref):
    shares, rows, wide = got_ref.shape
    bands = wide - LANES
    parts = bands // LANES
    total = got_ref[0].astype(F32)
    for share in range(1, shares):
        total = total + got_ref[share].astype(F32)
    tail = halves(total[:parts, bands:] + total[parts : 2 * parts, bands:], rows)
    mine_ref[:, :bands] = total[:, :bands]
    mine_ref[:, bands:] = tail
    send_ref[:, :bands] = total[:, :bands].astype(BF16)
    send_ref[:, bands:] = tail.astype(BF16)


def weights_kernel(total_columns, blocks, me_ref, mine_ref, other_ref, out_ref):
    rows, wide = mine_ref.shape
    shares = out_ref.shape[0]
    bands = wide - LANES
    local = bands // blocks
    parts = bands // LANES
    total = mine_ref[...] + other_ref[...].astype(F32)
    tail = total[:, bands:]
    squares = tail[:parts, :] + tail[parts : 2 * parts, :]
    scales = lax.rsqrt(squares + epsilon_norm)
    me = me_ref[0]
    first = me * rows
    row_ids = lax.broadcasted_iota(jnp.int32, (rows, LANES), 0) + first
    lane_ids = lax.broadcasted_iota(jnp.int32, (rows, LANES), 1)
    own = jnp.zeros((rows, 1), F32)
    for p in range(local // LANES):
        hit = row_ids == lane_ids + p * LANES
        own = own + jnp.sum(jnp.where(hit, scales[p : p + 1, :], 0.0), axis=1, keepdims=True)
    for p in range(parts):
        part = total[:, p * LANES : (p + 1) * LANES]
        across = scales[p : p + 1, :]
        diagonal = 0.0
        if p < local // LANES:
            hit = row_ids == lane_ids + p * LANES
            part = jnp.where(hit, squares[p : p + 1, :], part)
            diagonal = jnp.where(hit, 1.5, 0.0)
        weights = math.sqrt(total_columns) * across * (diagonal - 0.5 * (own * part * across))
        weights = weights.astype(BF16)
        for share in range(shares):
            out_ref[share, :, p * LANES : (p + 1) * LANES] = weights


def rotate_kernel(chunks, blocks, spans, weights_ref, *refs):
    out_ref = refs[-1]
    grid = [refs[c * blocks : (c + 1) * blocks] for c in range(chunks)]
    local = grid[0][0].shape[1]
    for c in range(chunks):
        for begin, size, column in spans[c]:
            total = None
            for r in range(blocks):
                term = lax.dot_general(
                    weights_ref[:, r * local : (r + 1) * local],
                    grid[c][r][begin : begin + size, :],
                    (((1,), (1,)), ((), ())),
                    preferred_element_type=F32,
                )
                total = term if total is None else total + term
            out_ref[:, column : column + size] = total.astype(BF16)


def lower_blocks(own):
    bit = lax.axis_size("band") // 4
    found = {0: own}
    while bit:
        for index in list(found):
            found[index ^ bit] = swap(found[index], "band", bit)
        bit //= 2
    return [found[index] for index in sorted(found)]


def fast_shards(basis_sizes, coupling_pattern, h_diag, h_couple, bands):
    count, n = h_diag.shape[:2]
    local = bands.shape[0]
    elem_size, band_size = lax.axis_size("elem"), lax.axis_size("band")
    total_columns = elem_size * count * n
    depth = DEGREE - 1
    wide = -(-(3 * n + 1) // LANES) * LANES
    lanes = wide // band_size
    half = band_size // 2
    elem_me = lax.axis_index("elem").astype(jnp.int32).reshape(1)
    band_me = lax.axis_index("band").astype(jnp.int32).reshape(1)

    rows, first_rows, last_rows = pl.pallas_call(
        functools.partial(rows_kernel, n, lanes),
        out_shape=[jax.ShapeDtypeStruct((count, n, wide), BF16)]
        + [jax.ShapeDtypeStruct((depth * n, lanes), BF16)] * 2,
        in_specs=[SMEM] + [HBM] * 4,
        out_specs=[VMEM] * 3,
        scratch_shapes=[pltpu.SMEM((count,), jnp.int32)] * 2
        + [pltpu.VMEM((count, n, n), BF16)] * 2
        + [pltpu.SemaphoreType.DMA((2,))]
        + [pltpu.SemaphoreType.DMA((math.gcd(count, 4),))] * 2,
        compiler_params=params(60),
        cost_estimate=about(0.01),
        name="rows",
    )(band_me, basis_sizes, coupling_pattern, h_diag, h_couple)
    left_rows = from_behind(last_rows, "elem", 1)
    right_rows = from_behind(first_rows, "elem", -1)

    halo = jax.ShapeDtypeStruct((DEGREE * n, local), BF16)
    start, first_y, last_y = pl.pallas_call(
        functools.partial(vectors_kernel, n, count, math.lcm(n, LANES) // n),
        out_shape=[jax.ShapeDtypeStruct((count * n, local), BF16), halo, halo],
        in_specs=[SMEM, VMEM],
        out_specs=[VMEM] * 3,
        compiler_params=params(16),
        cost_estimate=about(0.01),
        name="vectors",
    )(basis_sizes, bands)
    left_y = from_behind(last_y, "elem", 1)
    right_y = from_behind(first_y, "elem", -1)

    inner = (count - 2 * DEGREE) * n
    whole = jax.ShapeDtypeStruct((count * n, local), BF16)
    squares_shape = jax.ShapeDtypeStruct((1, local), F32)

    def edges(steps):
        return [jax.ShapeDtypeStruct((steps, 2 * n, local), BF16)] * 2

    left_edge, right_edge, even, odd = pl.pallas_call(
        functools.partial(interior_kernel, n, count, 0, SPLIT),
        out_shape=edges(SPLIT) + [whole] * 2,
        in_specs=[VMEM] * 2,
        out_specs=[VMEM] * 4,
        compiler_params=params(20),
        cost_estimate=about(0.01),
        name="interior_first",
    )(rows, start)
    own_rows = [after(side, even) for side in (left_rows, right_rows)]
    across_rows = [swap(side, "band", half) for side in own_rows]
    older, newer = (odd, even) if SPLIT % 2 == 0 else (even, odd)
    left_more, right_more, chunk, squares = pl.pallas_call(
        functools.partial(interior_kernel, n, count, SPLIT, DEGREE),
        out_shape=edges(DEGREE - SPLIT) + [jax.ShapeDtypeStruct((inner, local), BF16), squares_shape],
        in_specs=[VMEM] * 3,
        out_specs=[VMEM] * 4,
        scratch_shapes=[pltpu.VMEM((count * n, local), BF16)] * 2,
        compiler_params=params(20),
        cost_estimate=about(0.01),
        name="interior_rest",
    )(rows, older, newer)
    left_edge = [left_edge, left_more]
    right_edge = [right_edge, right_more]
    across_rows = [after(side, chunk) for side in across_rows]
    both = [block for side in (*own_rows, *across_rows) for block in lower_blocks(side)]
    chunks, across = [chunk], [swap(chunk, "band", half)]
    spans = [[(0, inner, DEGREE * n)]]
    offset = 0
    for index, strip in enumerate(STRIPS):
        last = index == len(STRIPS) - 1
        offset -= strip
        if index:
            left_edge = [after(left_edge[0], across[index - 1])]
        size = 2 * strip * n + (16 if last else 0)
        sizes = [edge.shape[0] for edge in left_edge]
        shape = jax.ShapeDtypeStruct((size, local), BF16)
        spare = [jax.ShapeDtypeStruct((8, LANES), F32)] * 2
        chunk, *others, squares = pl.pallas_call(
            functools.partial(strip_kernel, n, count, strip, offset, last, sizes, half),
            out_shape=[shape, *(spare if last else edges(DEGREE)), squares_shape],
            in_specs=[SMEM] + [VMEM] * (4 + 2 * len(sizes) + 4 * half),
            out_specs=[VMEM] * 4,
            scratch_shapes=[pltpu.VMEM((DEGREE + 1, (strip + 2) * n, local), BF16)] * 2
            + [pltpu.VMEM((depth, n, wide), BF16)] * 2,
            compiler_params=params(32),
            cost_estimate=about(3),
            name="strip",
        )(band_me, left_y, right_y, rows, squares, *left_edge, *right_edge, *both)
        left_edge, right_edge = [others[0]], [others[1]]
        chunks.append(chunk)
        across.append(swap(chunk, "band", half))
        first = offset + DEGREE
        spans.append([(0, strip * n, first * n), (strip * n, strip * n, (count - first - strip) * n)])

    group = elem_size // 2
    groups = [list(range(begin, begin + group)) for begin in (0, group)]
    slice_rows = local // group
    all_bands = local * band_size

    def gram(early, *blocks):
        wide = all_bands // 2 if early else all_bands + LANES
        shapes = [jax.ShapeDtypeStruct((group, slice_rows, wide), BF16)]
        if early:
            shapes.append(jax.ShapeDtypeStruct((half, 16, local), BF16))
            shapes.append(jax.ShapeDtypeStruct((local, count * n), BF16))
        return pl.pallas_call(
            functools.partial(gram_kernel, len(chunks), half, group, early),
            out_shape=shapes,
            in_specs=[VMEM] * len(blocks),
            out_specs=[VMEM] * len(shapes),
            compiler_params=params(20),
            cost_estimate=about(0.01),
            name="gram_early" if early else "gram_late",
        )(*blocks)

    lower = [lower_blocks(chunk) for chunk in chunks]
    early, tails, turned = gram(True, *[block for blocks in lower for block in blocks])
    upper = [lower_blocks(chunk) for chunk in across[:-1]]
    upper.append(lower_blocks(after(across[-1], upper[-1][-1], early)))
    (late,) = gram(False, early, turned, tails, *[block for blocks in upper for block in blocks])
    got = lax.all_to_all(late, "elem", 0, 0, tiled=True, axis_index_groups=groups)
    sums = jax.ShapeDtypeStruct((slice_rows, all_bands + LANES), F32)
    mine, send = pl.pallas_call(
        sums_kernel,
        out_shape=[sums, jax.ShapeDtypeStruct(sums.shape, BF16)],
        in_specs=[VMEM],
        out_specs=[VMEM] * 2,
        compiler_params=params(8),
        cost_estimate=about(0.01),
        name="sums",
    )(got)
    other = from_behind(send, "elem", group)
    weights = pl.pallas_call(
        functools.partial(weights_kernel, total_columns, band_size),
        out_shape=jax.ShapeDtypeStruct((group, slice_rows, all_bands), BF16),
        in_specs=[SMEM, VMEM, VMEM],
        out_specs=VMEM,
        compiler_params=params(8),
        cost_estimate=about(0.01),
        name="weights",
    )(elem_me % group, mine, other)
    flat = [block for low, high in zip(lower, upper) for block in (*low, *high)]
    weights = lax.all_to_all(weights, "elem", 0, 0, tiled=True, axis_index_groups=groups).reshape(local, all_bands)
    return pl.pallas_call(
        functools.partial(rotate_kernel, len(chunks), band_size, spans),
        out_shape=jax.ShapeDtypeStruct((local, count * n), BF16),
        in_specs=[VMEM] * (1 + len(flat)),
        out_specs=VMEM,
        compiler_params=params(24),
        cost_estimate=about(0.01),
        name="rotate",
    )(weights, *flat)


def identity_block(shape, offset):
    row_ids = lax.broadcasted_iota(jnp.int32, shape, 0) + offset
    col_ids = lax.broadcasted_iota(jnp.int32, shape, 1)
    return (row_ids == col_ids).astype(jnp.float32)


def rotation_columns(gram_strip, scales, offset, total_rows):
    own_scales = lax.dynamic_slice_in_dim(scales, offset, gram_strip.shape[0], 0)
    identity = identity_block(gram_strip.shape, offset)
    normed = own_scales[:, None] * gram_strip * scales[None, :]
    return (math.sqrt(total_rows) * scales[None, :] * (1.5 * identity - 0.5 * normed)).astype(
        jnp.bfloat16
    )


def general_shards(basis_sizes, coupling_pattern, h_diag, h_couple, bands):
    elem_local = h_diag.shape[0]
    basis_width = h_diag.shape[1]
    band_local = bands.shape[0]
    total_rows = elem_local * lax.axis_size("elem") * basis_width
    columns = lax.broadcasted_iota(jnp.int32, (elem_local, basis_width), 1)
    valid_rows = (columns < basis_sizes[:, None]).astype(jnp.float32)
    coupling = h_couple * coupling_pattern.astype(jnp.bfloat16)[:, None, None]
    current = (
        bands.reshape(band_local, elem_local, basis_width) * valid_rows.astype(jnp.bfloat16)[None]
    )
    previous = current
    for degree in range(DEGREE):
        current_float = current.astype(jnp.float32)
        local_term = jnp.einsum("eij,bej->bei", h_diag, current, preferred_element_type=jnp.float32)
        following = from_behind(current[:, 0], "elem", -1)
        ahead_rows = jnp.concatenate([current[:, 1:], following[:, None]], axis=1)
        upper_term = jnp.einsum(
            "eij,bej->bei", coupling, ahead_rows, preferred_element_type=jnp.float32
        )
        carried = jnp.einsum("eji,bej->bei", coupling, current, preferred_element_type=jnp.float32)
        arrived = from_behind(carried[:, -1], "elem", 1)
        lower_term = jnp.concatenate([arrived[:, None], carried[:, :-1]], axis=1)
        applied = (local_term + upper_term + lower_term) * valid_rows[None]
        shifted = applied - center_shift * current_float
        if degree == 0:
            next_iterate = shifted / half_width
        else:
            next_iterate = 2.0 * shifted / half_width - previous.astype(jnp.float32)
        previous, current = (current, next_iterate.astype(jnp.bfloat16))
    filtered = current.reshape(band_local, elem_local * basis_width)
    every_band = lax.all_gather(filtered, "band", axis=0, tiled=True)
    strip = lax.dot_general(
        filtered, every_band, (((1,), (1,)), ((), ())), preferred_element_type=jnp.float32
    )
    squares = jnp.sum(jnp.square(every_band.astype(jnp.float32)), axis=1)
    strip, squares = lax.psum((strip, squares), "elem")
    scales = lax.rsqrt(squares + epsilon_norm)
    offset = lax.axis_index("band") * band_local
    weights = rotation_columns(strip, scales, offset, total_rows)
    return jnp.dot(weights, every_band, preferred_element_type=jnp.float32).astype(jnp.bfloat16)


def shards(basis_sizes, coupling_pattern, h_diag, h_couple, bands):
    count, n = h_diag.shape[:2]
    local = bands.shape[0]
    elem_size, band_size = lax.axis_size("elem"), lax.axis_size("band")
    rows = local // elem_size
    wide = -(-(3 * n + 1) // LANES) * LANES
    fits = (
        band_size & (band_size - 1) == 0
        and wide % (band_size * LANES) == 0
        and local % LANES == 0
        and elem_size % 2 == 0
        and local % elem_size == 0
        and rows % 16 == 0
        and rows * LANES >= 2 * local * band_size
        and count > 2 * DEGREE
        and n % 16 == 0
    )
    form = fast_shards if fits else general_shards
    return form(basis_sizes, coupling_pattern, h_diag, h_couple, bands)


def solution(mesh):
    in_specs = (
        P("elem"),
        P("elem"),
        P("elem", None, None),
        P("elem", None, None),
        P("band", "elem"),
    )
    out_specs = P("band", "elem")
    return jax.shard_map(shards, mesh=mesh, in_specs=in_specs, out_specs=out_specs, check_vma=False)
```

```python
import functools
import math

import jax
import jax.numpy as jnp
from jax import lax
from jax.experimental import pallas as pl
from jax.experimental.pallas import tpu as pltpu
from jax.sharding import PartitionSpec as P

DEGREE = 6
STRIPS = (3, 3)
SPLIT = 2

center_shift = 0.4
half_width = 2.8
epsilon_norm = 1e-06

LANES = 128
VMEM = pl.BlockSpec(memory_space=pltpu.VMEM)
HBM = pl.BlockSpec(memory_space=pltpu.HBM)
SMEM = pl.BlockSpec(memory_space=pltpu.SMEM)
BF16 = jnp.bfloat16
F32 = jnp.float32


def from_behind(value, axis, steps):
    count = lax.axis_size(axis)
    pairs = [(source, (source + steps) % count) for source in range(count)]
    return lax.ppermute(value, axis, pairs)


def swap(value, axis, bit):
    count = lax.axis_size(axis)
    return lax.ppermute(value, axis, [(source, source ^ bit) for source in range(count)])


def after(value, *others):
    return lax.optimization_barrier((value, *others))[0]


def params(mib):
    return pltpu.CompilerParams(vmem_limit_bytes=mib * 1024 * 1024)


def about(microseconds):
    return pl.CostEstimate(flops=int(microseconds * 1.15e9), bytes_accessed=1, transcendentals=0)


def joined(behind, diag, couple, size, wide):
    n = diag.shape[0]
    whole = jnp.concatenate([behind, diag.astype(F32), couple, jnp.ones((n, wide - 3 * n), F32)], axis=1)
    place = lax.broadcasted_iota(jnp.int32, (n, wide), 0)
    return jnp.where(place < size, whole, 0.0).astype(BF16)


def rows_kernel(sizes_ref, pattern_ref, diag_ref, couple_ref, rows_ref):
    count, n, wide = rows_ref.shape
    behind = jnp.zeros((n, n), F32)
    for e in range(count):
        couple = couple_ref[e].astype(F32) * pattern_ref[e].astype(F32)
        rows_ref[e] = joined(behind, diag_ref[e], couple, sizes_ref[e], wide)
        behind = jnp.transpose(couple)


def ends_kernel(wide, me_ref, sizes_in, pattern_in, diag_in, couple_in, first_ref, last_ref, *scratch):
    sizes_ref, pattern_ref, diag_ref, couple_ref, row_ref, sems = scratch
    count, n, _ = diag_in.shape
    depth = DEGREE - 1
    lanes = first_ref.shape[1]
    low, high, before = pl.ds(0, depth), pl.ds(count - depth, depth), pl.ds(count - depth - 1, depth + 1)
    pairs = [(sizes_in, sizes_ref), (pattern_in, pattern_ref)]
    pairs += [(couple_in.at[low], couple_ref.at[low]), (diag_in.at[low], diag_ref.at[low])]
    pairs += [(couple_in.at[before], couple_ref.at[before]), (diag_in.at[high], diag_ref.at[high])]
    copies = [pltpu.make_async_copy(source, target, sems.at[k]) for k, (source, target) in enumerate(pairs)]
    for copy in copies:
        copy.start()
    at = pl.ds(pl.multiple_of(me_ref[0] * lanes, lanes), lanes)

    def coupled(e):
        return couple_ref[e].astype(F32) * pattern_ref[e].astype(F32)

    for copy in copies[:4]:
        copy.wait()
    behind = jnp.zeros((n, n), F32)
    for e in range(depth):
        couple = coupled(e)
        row_ref[e] = joined(behind, diag_ref[e], couple, sizes_ref[e], wide)
        first_ref[e * n : (e + 1) * n, :] = row_ref[e, :, at]
        behind = jnp.transpose(couple)
    for copy in copies[4:]:
        copy.wait()
    behind = jnp.transpose(coupled(count - depth - 1))
    for e in range(depth):
        couple = coupled(count - depth + e)
        row_ref[depth + e] = joined(behind, diag_ref[count - depth + e], couple, sizes_ref[count - depth + e], wide)
        last_ref[e * n : (e + 1) * n, :] = row_ref[depth + e, :, at]
        behind = jnp.transpose(couple)


def vectors_kernel(width, count, group, sizes_ref, bands_ref, out_ref, *edge_refs):
    n = width
    local = bands_ref.shape[0]
    place = lax.broadcasted_iota(jnp.int32, (n, local), 0)
    for begin in range(0, count, group):
        turned = jnp.transpose(bands_ref[:, begin * n : (begin + group) * n])
        for e in range(begin, begin + group):
            part = turned[(e - begin) * n : (e - begin + 1) * n, :].astype(F32)
            out_ref[e * n : (e + 1) * n, :] = jnp.where(place < sizes_ref[e], part, 0.0).astype(BF16)
    near = 0
    for index, strip in enumerate(STRIPS):
        far = near + strip
        edge_refs[2 * index][...] = out_ref[near * n : far * n, :]
        edge_refs[2 * index + 1][...] = out_ref[(count - far) * n : (count - near) * n, :]
        near = far


def advance(row, window, center, before, first):
    total = jnp.dot(row, window, preferred_element_type=F32)
    shifted = total - center_shift * center.astype(F32)
    if first:
        return (shifted * (1.0 / half_width)).astype(BF16)
    return (shifted * (2.0 / half_width) - before.astype(F32)).astype(BF16)


def add_squares(total, values):
    values = values.astype(F32)
    return total + jnp.sum(values * values, axis=0, keepdims=True)


def interior_kernel(width, count, begin, end, rows_ref, *refs):
    n = width
    if begin == 0:
        first_ref, refs = refs[0], refs[1:]
    else:
        older_ref, newer_ref, refs = refs[0], refs[1], refs[2:]
    if end < DEGREE:
        left_ref, right_ref, even_ref, odd_ref = refs
    else:
        left_ref, right_ref, out_ref, squares_ref, even_ref, odd_ref = refs
    buffers = (even_ref, odd_ref)
    for step in range(begin, end):
        source = buffers[step % 2]
        older = target = buffers[(step + 1) % 2]
        if step == begin:
            source = first_ref if begin == 0 else newer_ref
        if step == 1 and begin == 0:
            older = first_ref
        elif step == begin and begin > 0:
            older = older_ref
        elif step == begin + 1 and begin > 0:
            older = newer_ref
        left_ref[step - begin] = source[step * n : (step + 2) * n, :]
        right_ref[step - begin] = source[(count - step - 2) * n : (count - step) * n, :]

        def body(e, carry):
            at = pl.multiple_of(e * n, 16)
            window = source[pl.ds(pl.multiple_of((e - 1) * n, 16), 3 * n), :]
            center = source[pl.ds(at, n), :]
            before = older[pl.ds(at, n), :]
            target[pl.ds(at, n), :] = advance(rows_ref[e, :, : 3 * n], window, center, before, step == 0)
            return carry

        lax.fori_loop(step + 1, count - 1 - step, body, 0, unroll=2)
    if end == DEGREE:
        result = buffers[DEGREE % 2][DEGREE * n : (count - DEGREE) * n, :]
        out_ref[...] = result
        squares_ref[...] = add_squares(jnp.zeros(squares_ref.shape, F32), result)


def strip_kernel(
    width,
    count,
    strip,
    offset,
    last,
    edge_sizes,
    pieces,
    me_ref,
    left_y_ref,
    right_y_ref,
    rows_ref,
    squares_in_ref,
    *refs,
):
    n = width
    depth = DEGREE - 1
    me = me_ref[0]
    refs, outs = refs[:-8], refs[-8:]
    half = len(edge_sizes)
    left_edge = [ref.at[k] for ref, size in zip(refs[:half], edge_sizes) for k in range(size)]
    right_edge = [ref.at[k] for ref, size in zip(refs[half : 2 * half], edge_sizes) for k in range(size)]
    refs = refs[2 * half :]
    out_ref, left_out_ref, right_out_ref, squares_ref, left_scr, right_scr, halo_left, halo_right = outs
    lanes = refs[0].shape[1]
    for index in range(pieces):
        for side in range(2):
            at = pl.ds(pl.multiple_of((me ^ (side * pieces + index)) * lanes, lanes), lanes)
            halo_left[:, :, at] = refs[2 * side * pieces + index][...].reshape(depth, n, lanes)
            halo_right[:, :, at] = refs[(2 * side + 1) * pieces + index][...].reshape(depth, n, lanes)

    def left_row(e):
        if e < 0:
            return halo_left[depth + e, :, : 3 * n]
        if e > 0:
            return rows_ref[e, :, : 3 * n]
        turned = jnp.transpose(halo_left[depth - 1, :, 2 * n : 3 * n].astype(F32))
        keep = rows_ref[0, :, 3 * n : 3 * n + 1].astype(F32)
        return jnp.concatenate([(turned * keep).astype(BF16), rows_ref[0, :, n : 3 * n]], axis=1)

    def right_row(e):
        if e < count:
            return rows_ref[e, :, : 3 * n]
        if e > count:
            return halo_right[e - count, :, : 3 * n]
        turned = jnp.transpose(rows_ref[count - 1, :, 2 * n : 3 * n].astype(F32))
        keep = halo_right[0, :, 3 * n : 3 * n + 1].astype(F32)
        return jnp.concatenate([(turned * keep).astype(BF16), halo_right[0, :, n : 3 * n]], axis=1)

    left_scr[0, : strip * n, :] = left_y_ref[...]
    right_scr[0, 2 * n :, :] = right_y_ref[...]
    for step in range(DEGREE):
        left_scr[step, strip * n :, :] = left_edge[step][...]
        right_scr[step, : 2 * n, :] = right_edge[step][...]
        for j in range(strip):
            e = offset + step + 1 + j
            left_scr[step + 1, j * n : (j + 1) * n, :] = advance(
                left_row(e),
                left_scr[step, j * n : (j + 3) * n, :],
                left_scr[step, (j + 1) * n : (j + 2) * n, :],
                left_scr[max(step - 1, 0), (j + 2) * n : (j + 3) * n, :],
                step == 0,
            )
            e = count - 1 - (offset + strip + step) + j
            right_scr[step + 1, (j + 2) * n : (j + 3) * n, :] = advance(
                right_row(e),
                right_scr[step, j * n : (j + 3) * n, :],
                right_scr[step, (j + 1) * n : (j + 2) * n, :],
                right_scr[max(step - 1, 0), j * n : (j + 1) * n, :],
                step == 0,
            )
        if not last:
            left_out_ref[step] = left_scr[step, : 2 * n, :]
            right_out_ref[step] = right_scr[step, strip * n : (strip + 2) * n, :]
    result_left = left_scr[DEGREE, : strip * n, :]
    result_right = right_scr[DEGREE, 2 * n :, :]
    out_ref[: strip * n, :] = result_left
    out_ref[strip * n : 2 * strip * n, :] = result_right
    squares = add_squares(add_squares(squares_in_ref[...], result_left), result_right)
    squares_ref[...] = squares
    if last:
        high = squares.astype(BF16).astype(F32)
        low = squares - high
        place = lax.broadcasted_iota(jnp.int32, (16, squares.shape[1]), 0)
        both = jnp.where(place == 0, high, jnp.where(place == 1, low, 0.0))
        out_ref[2 * strip * n :, :] = both.astype(BF16)


def gram_kernel(chunks, half, shares, early, *refs):
    if early:
        refs, (out_ref, tails_ref, turned_ref) = refs[:-3], refs[-3:]
    else:
        early_ref, turned_ref, tails_ref, *refs, out_ref = refs
    grid = [refs[c * half : (c + 1) * half] for c in range(chunks)]
    rows = out_ref.shape[1]
    local = grid[0][0].shape[1]
    sizes = [grid[c][0].shape[0] - (16 if c == chunks - 1 else 0) for c in range(chunks)]
    places = [slice(sum(sizes[:c]), sum(sizes[: c + 1])) for c in range(chunks)]
    tails = [grid[-1][r][sizes[-1] :, :] for r in range(half)]
    if early:
        for c in range(chunks):
            turned_ref[:, places[c]] = jnp.transpose(grid[c][0][: sizes[c], :])
        for r in range(half):
            tails_ref[r] = tails[r]
    for r in range(half):
        total = None
        for c in range(chunks):
            term = jnp.dot(turned_ref[:, places[c]], grid[c][r][: sizes[c], :], preferred_element_type=F32)
            total = term if c == 0 else total + term
        at = (r if early else half + r) * local
        out_ref[:, :, at : at + local] = total.astype(BF16).reshape(shares, rows, local)
    if early:
        return
    out_ref[:, :, : half * local] = early_ref[...]
    place = lax.broadcasted_iota(jnp.int32, (rows, LANES), 0)
    parts = local // LANES
    extra = jnp.zeros((rows, LANES), F32)
    for r in range(2 * half):
        both = (tails_ref[r] if r < half else tails[r - half]).astype(F32)
        for p in range(parts):
            for part in range(2):
                line = both[part : part + 1, p * LANES : (p + 1) * LANES]
                extra = jnp.where(place == part * 2 * half * parts + r * parts + p, line, extra)
    for share in range(shares):
        out_ref[share, :, 2 * half * local :] = extra.astype(BF16)


def halves(squares, rows):
    high = squares.astype(BF16).astype(F32)
    spare = jnp.zeros((rows - 2 * squares.shape[0], LANES), F32)
    return jnp.concatenate([high, squares - high, spare])


def sums_kernel(got_ref, mine_ref, send_ref):
    shares, rows, wide = got_ref.shape
    bands = wide - LANES
    parts = bands // LANES
    total = got_ref[0].astype(F32)
    for share in range(1, shares):
        total = total + got_ref[share].astype(F32)
    tail = halves(total[:parts, bands:] + total[parts : 2 * parts, bands:], rows)
    mine_ref[:, :bands] = total[:, :bands]
    mine_ref[:, bands:] = tail
    send_ref[:, :bands] = total[:, :bands].astype(BF16)
    send_ref[:, bands:] = tail.astype(BF16)


def weights_kernel(total_columns, blocks, me_ref, mine_ref, other_ref, out_ref):
    rows, wide = mine_ref.shape
    shares = out_ref.shape[0]
    bands = wide - LANES
    local = bands // blocks
    parts = bands // LANES
    total = mine_ref[...] + other_ref[...].astype(F32)
    tail = total[:, bands:]
    squares = tail[:parts, :] + tail[parts : 2 * parts, :]
    scales = lax.rsqrt(squares + epsilon_norm)
    me = me_ref[0]
    first = me * rows
    row_ids = lax.broadcasted_iota(jnp.int32, (rows, LANES), 0) + first
    lane_ids = lax.broadcasted_iota(jnp.int32, (rows, LANES), 1)
    own = jnp.zeros((rows, 1), F32)
    for p in range(local // LANES):
        hit = row_ids == lane_ids + p * LANES
        own = own + jnp.sum(jnp.where(hit, scales[p : p + 1, :], 0.0), axis=1, keepdims=True)
    for p in range(parts):
        part = total[:, p * LANES : (p + 1) * LANES]
        across = scales[p : p + 1, :]
        diagonal = 0.0
        if p < local // LANES:
            hit = row_ids == lane_ids + p * LANES
            part = jnp.where(hit, squares[p : p + 1, :], part)
            diagonal = jnp.where(hit, 1.5, 0.0)
        weights = math.sqrt(total_columns) * across * (diagonal - 0.5 * (own * part * across))
        weights = weights.astype(BF16)
        for share in range(shares):
            out_ref[share, :, p * LANES : (p + 1) * LANES] = weights


def rotate_kernel(chunks, blocks, spans, weights_ref, *refs):
    out_ref = refs[-1]
    grid = [refs[c * blocks : (c + 1) * blocks] for c in range(chunks)]
    local = grid[0][0].shape[1]
    for c in range(chunks):
        for begin, size, column in spans[c]:
            total = None
            for r in range(blocks):
                term = lax.dot_general(
                    weights_ref[:, r * local : (r + 1) * local],
                    grid[c][r][begin : begin + size, :],
                    (((1,), (1,)), ((), ())),
                    preferred_element_type=F32,
                )
                total = term if total is None else total + term
            out_ref[:, column : column + size] = total.astype(BF16)


def lower_blocks(own):
    bit = lax.axis_size("band") // 4
    found = {0: own}
    while bit:
        for index in list(found):
            found[index ^ bit] = swap(found[index], "band", bit)
        bit //= 2
    return [found[index] for index in sorted(found)]


def fast_shards(basis_sizes, coupling_pattern, h_diag, h_couple, bands):
    count, n = h_diag.shape[:2]
    local = bands.shape[0]
    elem_size, band_size = lax.axis_size("elem"), lax.axis_size("band")
    total_columns = elem_size * count * n
    depth = DEGREE - 1
    wide = -(-(3 * n + 1) // LANES) * LANES
    lanes = wide // band_size
    half = band_size // 2
    elem_me = lax.axis_index("elem").astype(jnp.int32).reshape(1)
    band_me = lax.axis_index("band").astype(jnp.int32).reshape(1)

    first_rows, last_rows = pl.pallas_call(
        functools.partial(ends_kernel, wide),
        out_shape=[jax.ShapeDtypeStruct((depth * n, lanes), BF16)] * 2,
        in_specs=[SMEM] + [HBM] * 4,
        out_specs=[VMEM] * 2,
        scratch_shapes=[pltpu.SMEM((count,), jnp.int32)] * 2
        + [pltpu.VMEM((count, n, n), BF16)] * 2
        + [pltpu.VMEM((2 * depth, n, wide), BF16), pltpu.SemaphoreType.DMA((6,))],
        compiler_params=params(60),
        cost_estimate=about(0.01),
        name="ends",
    )(band_me, basis_sizes, coupling_pattern, h_diag, h_couple)
    rows = pl.pallas_call(
        rows_kernel,
        out_shape=jax.ShapeDtypeStruct((count, n, wide), BF16),
        in_specs=[SMEM] * 2 + [VMEM] * 2,
        out_specs=VMEM,
        compiler_params=params(16),
        cost_estimate=about(0.01),
        name="rows",
    )(basis_sizes, after(coupling_pattern, first_rows), h_diag, h_couple)
    left_rows = from_behind(last_rows, "elem", 1)
    right_rows = from_behind(first_rows, "elem", -1)

    start, *ends = pl.pallas_call(
        functools.partial(vectors_kernel, n, count, math.lcm(n, LANES) // n),
        out_shape=[jax.ShapeDtypeStruct((count * n, local), BF16)]
        + [jax.ShapeDtypeStruct((strip * n, local), BF16) for strip in STRIPS for _ in range(2)],
        in_specs=[SMEM, VMEM],
        out_specs=[VMEM] * (1 + 2 * len(STRIPS)),
        compiler_params=params(16),
        cost_estimate=about(0.01),
        name="vectors",
    )(basis_sizes, bands)

    inner = (count - 2 * DEGREE) * n
    whole = jax.ShapeDtypeStruct((count * n, local), BF16)
    squares_shape = jax.ShapeDtypeStruct((1, local), F32)

    def edges(steps):
        return [jax.ShapeDtypeStruct((steps, 2 * n, local), BF16)] * 2

    left_edge, right_edge, even, odd = pl.pallas_call(
        functools.partial(interior_kernel, n, count, 0, SPLIT),
        out_shape=edges(SPLIT) + [whole] * 2,
        in_specs=[VMEM] * 2,
        out_specs=[VMEM] * 4,
        compiler_params=params(20),
        cost_estimate=about(0.01),
        name="interior_first",
    )(rows, start)
    left_y = [from_behind(after(ends[1], even), "elem", 1)]
    right_y = [from_behind(after(ends[0], even), "elem", -1)]
    own_rows = [after(side, even) for side in (left_rows, right_rows)]
    across_rows = [swap(side, "band", half) for side in own_rows]
    older, newer = (odd, even) if SPLIT % 2 == 0 else (even, odd)
    left_more, right_more, chunk, squares = pl.pallas_call(
        functools.partial(interior_kernel, n, count, SPLIT, DEGREE),
        out_shape=edges(DEGREE - SPLIT) + [jax.ShapeDtypeStruct((inner, local), BF16), squares_shape],
        in_specs=[VMEM] * 3,
        out_specs=[VMEM] * 4,
        scratch_shapes=[pltpu.VMEM((count * n, local), BF16)] * 2,
        compiler_params=params(20),
        cost_estimate=about(0.01),
        name="interior_rest",
    )(rows, older, newer)
    left_edge = [left_edge, left_more]
    right_edge = [right_edge, right_more]
    across_rows = [after(side, chunk, left_y[0], right_y[0]) for side in across_rows]
    for index in range(1, len(STRIPS)):
        left_y.append(from_behind(after(ends[2 * index + 1], chunk), "elem", 1))
        right_y.append(from_behind(after(ends[2 * index], chunk), "elem", -1))
    both = [block for side in (*own_rows, *across_rows) for block in lower_blocks(side)]
    chunks, across = [chunk], [swap(chunk, "band", half)]
    spans = [[(0, inner, DEGREE * n)]]
    offset = 0
    for index, strip in enumerate(STRIPS):
        last = index == len(STRIPS) - 1
        offset -= strip
        if index:
            left_edge = [after(left_edge[0], across[index - 1])]
        size = 2 * strip * n + (16 if last else 0)
        sizes = [edge.shape[0] for edge in left_edge]
        shape = jax.ShapeDtypeStruct((size, local), BF16)
        spare = [jax.ShapeDtypeStruct((8, LANES), F32)] * 2
        chunk, *others, squares = pl.pallas_call(
            functools.partial(strip_kernel, n, count, strip, offset, last, sizes, half),
            out_shape=[shape, *(spare if last else edges(DEGREE)), squares_shape],
            in_specs=[SMEM] + [VMEM] * (4 + 2 * len(sizes) + 4 * half),
            out_specs=[VMEM] * 4,
            scratch_shapes=[pltpu.VMEM((DEGREE + 1, (strip + 2) * n, local), BF16)] * 2
            + [pltpu.VMEM((depth, n, wide), BF16)] * 2,
            compiler_params=params(32),
            cost_estimate=about(3),
            name="strip",
        )(band_me, left_y[index], right_y[index], rows, squares, *left_edge, *right_edge, *both)
        left_edge, right_edge = [others[0]], [others[1]]
        chunks.append(chunk)
        across.append(swap(chunk, "band", half))
        first = offset + DEGREE
        spans.append([(0, strip * n, first * n), (strip * n, strip * n, (count - first - strip) * n)])

    group = elem_size // 2
    groups = [list(range(begin, begin + group)) for begin in (0, group)]
    slice_rows = local // group
    all_bands = local * band_size

    def gram(early, *blocks):
        wide = all_bands // 2 if early else all_bands + LANES
        shapes = [jax.ShapeDtypeStruct((group, slice_rows, wide), BF16)]
        if early:
            shapes.append(jax.ShapeDtypeStruct((half, 16, local), BF16))
            shapes.append(jax.ShapeDtypeStruct((local, count * n), BF16))
        return pl.pallas_call(
            functools.partial(gram_kernel, len(chunks), half, group, early),
            out_shape=shapes,
            in_specs=[VMEM] * len(blocks),
            out_specs=[VMEM] * len(shapes),
            compiler_params=params(20),
            cost_estimate=about(0.01),
            name="gram_early" if early else "gram_late",
        )(*blocks)

    lower = [lower_blocks(chunk) for chunk in chunks]
    early, tails, turned = gram(True, *[block for blocks in lower for block in blocks])
    upper = [lower_blocks(chunk) for chunk in across[:-1]]
    upper.append(lower_blocks(after(across[-1], upper[-1][-1], early)))
    (late,) = gram(False, early, turned, tails, *[block for blocks in upper for block in blocks])
    got = lax.all_to_all(late, "elem", 0, 0, tiled=True, axis_index_groups=groups)
    sums = jax.ShapeDtypeStruct((slice_rows, all_bands + LANES), F32)
    mine, send = pl.pallas_call(
        sums_kernel,
        out_shape=[sums, jax.ShapeDtypeStruct(sums.shape, BF16)],
        in_specs=[VMEM],
        out_specs=[VMEM] * 2,
        compiler_params=params(8),
        cost_estimate=about(0.01),
        name="sums",
    )(got)
    other = from_behind(send, "elem", group)
    weights = pl.pallas_call(
        functools.partial(weights_kernel, total_columns, band_size),
        out_shape=jax.ShapeDtypeStruct((group, slice_rows, all_bands), BF16),
        in_specs=[SMEM, VMEM, VMEM],
        out_specs=VMEM,
        compiler_params=params(8),
        cost_estimate=about(0.01),
        name="weights",
    )(elem_me % group, mine, other)
    flat = [block for low, high in zip(lower, upper) for block in (*low, *high)]
    weights = lax.all_to_all(weights, "elem", 0, 0, tiled=True, axis_index_groups=groups).reshape(local, all_bands)
    return pl.pallas_call(
        functools.partial(rotate_kernel, len(chunks), band_size, spans),
        out_shape=jax.ShapeDtypeStruct((local, count * n), BF16),
        in_specs=[VMEM] * (1 + len(flat)),
        out_specs=VMEM,
        compiler_params=params(24),
        cost_estimate=about(0.01),
        name="rotate",
    )(weights, *flat)


def identity_block(shape, offset):
    row_ids = lax.broadcasted_iota(jnp.int32, shape, 0) + offset
    col_ids = lax.broadcasted_iota(jnp.int32, shape, 1)
    return (row_ids == col_ids).astype(jnp.float32)


def rotation_columns(gram_strip, scales, offset, total_rows):
    own_scales = lax.dynamic_slice_in_dim(scales, offset, gram_strip.shape[0], 0)
    identity = identity_block(gram_strip.shape, offset)
    normed = own_scales[:, None] * gram_strip * scales[None, :]
    return (math.sqrt(total_rows) * scales[None, :] * (1.5 * identity - 0.5 * normed)).astype(
        jnp.bfloat16
    )


def general_shards(basis_sizes, coupling_pattern, h_diag, h_couple, bands):
    elem_local = h_diag.shape[0]
    basis_width = h_diag.shape[1]
    band_local = bands.shape[0]
    total_rows = elem_local * lax.axis_size("elem") * basis_width
    columns = lax.broadcasted_iota(jnp.int32, (elem_local, basis_width), 1)
    valid_rows = (columns < basis_sizes[:, None]).astype(jnp.float32)
    coupling = h_couple * coupling_pattern.astype(jnp.bfloat16)[:, None, None]
    current = (
        bands.reshape(band_local, elem_local, basis_width) * valid_rows.astype(jnp.bfloat16)[None]
    )
    previous = current
    for degree in range(DEGREE):
        current_float = current.astype(jnp.float32)
        local_term = jnp.einsum("eij,bej->bei", h_diag, current, preferred_element_type=jnp.float32)
        following = from_behind(current[:, 0], "elem", -1)
        ahead_rows = jnp.concatenate([current[:, 1:], following[:, None]], axis=1)
        upper_term = jnp.einsum(
            "eij,bej->bei", coupling, ahead_rows, preferred_element_type=jnp.float32
        )
        carried = jnp.einsum("eji,bej->bei", coupling, current, preferred_element_type=jnp.float32)
        arrived = from_behind(carried[:, -1], "elem", 1)
        lower_term = jnp.concatenate([arrived[:, None], carried[:, :-1]], axis=1)
        applied = (local_term + upper_term + lower_term) * valid_rows[None]
        shifted = applied - center_shift * current_float
        if degree == 0:
            next_iterate = shifted / half_width
        else:
            next_iterate = 2.0 * shifted / half_width - previous.astype(jnp.float32)
        previous, current = (current, next_iterate.astype(jnp.bfloat16))
    filtered = current.reshape(band_local, elem_local * basis_width)
    every_band = lax.all_gather(filtered, "band", axis=0, tiled=True)
    strip = lax.dot_general(
        filtered, every_band, (((1,), (1,)), ((), ())), preferred_element_type=jnp.float32
    )
    squares = jnp.sum(jnp.square(every_band.astype(jnp.float32)), axis=1)
    strip, squares = lax.psum((strip, squares), "elem")
    scales = lax.rsqrt(squares + epsilon_norm)
    offset = lax.axis_index("band") * band_local
    weights = rotation_columns(strip, scales, offset, total_rows)
    return jnp.dot(weights, every_band, preferred_element_type=jnp.float32).astype(jnp.bfloat16)


def shards(basis_sizes, coupling_pattern, h_diag, h_couple, bands):
    count, n = h_diag.shape[:2]
    local = bands.shape[0]
    elem_size, band_size = lax.axis_size("elem"), lax.axis_size("band")
    rows = local // elem_size
    wide = -(-(3 * n + 1) // LANES) * LANES
    fits = (
        band_size & (band_size - 1) == 0
        and wide % (band_size * LANES) == 0
        and local % LANES == 0
        and elem_size % 2 == 0
        and local % elem_size == 0
        and rows % 16 == 0
        and rows * LANES >= 2 * local * band_size
        and count > 2 * DEGREE
        and n % 16 == 0
    )
    form = fast_shards if fits else general_shards
    return form(basis_sizes, coupling_pattern, h_diag, h_couple, bands)


def solution(mesh):
    in_specs = (
        P("elem"),
        P("elem"),
        P("elem", None, None),
        P("elem", None, None),
        P("band", "elem"),
    )
    out_specs = P("band", "elem")
    return jax.shard_map(shards, mesh=mesh, in_specs=in_specs, out_specs=out_specs, check_vma=False)
```

```python
import functools
import math

import jax
import jax.numpy as jnp
from jax import lax
from jax.experimental import pallas as pl
from jax.experimental.pallas import tpu as pltpu
from jax.sharding import PartitionSpec as P

DEGREE = 6
STRIPS = (3, 3)
SPLIT = 2

center_shift = 0.4
half_width = 2.8
epsilon_norm = 1e-06

LANES = 128
VMEM = pl.BlockSpec(memory_space=pltpu.VMEM)
HBM = pl.BlockSpec(memory_space=pltpu.HBM)
SMEM = pl.BlockSpec(memory_space=pltpu.SMEM)
BF16 = jnp.bfloat16
F32 = jnp.float32


def from_behind(value, axis, steps):
    count = lax.axis_size(axis)
    pairs = [(source, (source + steps) % count) for source in range(count)]
    return lax.ppermute(value, axis, pairs)


def swap(value, axis, bit):
    count = lax.axis_size(axis)
    return lax.ppermute(value, axis, [(source, source ^ bit) for source in range(count)])


def after(value, *others):
    return lax.optimization_barrier((value, *others))[0]


def params(mib):
    return pltpu.CompilerParams(vmem_limit_bytes=mib * 1024 * 1024)


def about(microseconds):
    return pl.CostEstimate(flops=int(microseconds * 1.15e9), bytes_accessed=1, transcendentals=0)


def joined(behind, diag, couple, size, wide):
    n = diag.shape[0]
    whole = jnp.concatenate([behind, diag.astype(F32), couple, jnp.ones((n, wide - 3 * n), F32)], axis=1)
    place = lax.broadcasted_iota(jnp.int32, (n, wide), 0)
    return jnp.where(place < size, whole, 0.0).astype(BF16)


def rows_kernel(sizes_ref, pattern_ref, diag_ref, couple_ref, rows_ref):
    count, n, wide = rows_ref.shape
    behind = jnp.zeros((n, n), F32)
    for e in range(count):
        couple = couple_ref[e].astype(F32) * pattern_ref[e].astype(F32)
        rows_ref[e] = joined(behind, diag_ref[e], couple, sizes_ref[e], wide)
        behind = jnp.transpose(couple)


def ends_kernel(wide, me_ref, sizes_in, pattern_in, diag_in, couple_in, first_ref, last_ref, *scratch):
    sizes_ref, pattern_ref, diag_ref, couple_ref, row_ref, sems = scratch
    count, n, _ = diag_in.shape
    depth = DEGREE - 1
    lanes = first_ref.shape[1]
    low, high, before = pl.ds(0, depth), pl.ds(count - depth, depth), pl.ds(count - depth - 1, depth + 1)
    pairs = [(sizes_in, sizes_ref), (pattern_in, pattern_ref)]
    pairs += [(couple_in.at[low], couple_ref.at[low]), (diag_in.at[low], diag_ref.at[low])]
    pairs += [(couple_in.at[before], couple_ref.at[before]), (diag_in.at[high], diag_ref.at[high])]
    copies = [pltpu.make_async_copy(source, target, sems.at[k]) for k, (source, target) in enumerate(pairs)]
    for copy in copies:
        copy.start()
    at = pl.ds(pl.multiple_of(me_ref[0] * lanes, lanes), lanes)

    def coupled(e):
        return couple_ref[e].astype(F32) * pattern_ref[e].astype(F32)

    for copy in copies[:4]:
        copy.wait()
    behind = jnp.zeros((n, n), F32)
    for e in range(depth):
        couple = coupled(e)
        row_ref[e] = joined(behind, diag_ref[e], couple, sizes_ref[e], wide)
        first_ref[e * n : (e + 1) * n, :] = row_ref[e, :, at]
        behind = jnp.transpose(couple)
    for copy in copies[4:]:
        copy.wait()
    behind = jnp.transpose(coupled(count - depth - 1))
    for e in range(depth):
        couple = coupled(count - depth + e)
        row_ref[depth + e] = joined(behind, diag_ref[count - depth + e], couple, sizes_ref[count - depth + e], wide)
        last_ref[e * n : (e + 1) * n, :] = row_ref[depth + e, :, at]
        behind = jnp.transpose(couple)


def vectors_kernel(width, count, group, sizes_ref, bands_ref, out_ref, *edge_refs):
    n = width
    local = bands_ref.shape[0]
    place = lax.broadcasted_iota(jnp.int32, (n, local), 0)
    for begin in range(0, count, group):
        turned = jnp.transpose(bands_ref[:, begin * n : (begin + group) * n])
        for e in range(begin, begin + group):
            part = turned[(e - begin) * n : (e - begin + 1) * n, :].astype(F32)
            out_ref[e * n : (e + 1) * n, :] = jnp.where(place < sizes_ref[e], part, 0.0).astype(BF16)
    near = 0
    for index, strip in enumerate(STRIPS):
        far = near + strip
        edge_refs[2 * index][...] = out_ref[near * n : far * n, :]
        edge_refs[2 * index + 1][...] = out_ref[(count - far) * n : (count - near) * n, :]
        near = far


def advance(row, window, center, before, first):
    total = jnp.dot(row, window, preferred_element_type=F32)
    shifted = total - center_shift * center.astype(F32)
    if first:
        return (shifted * (1.0 / half_width)).astype(BF16)
    return (shifted * (2.0 / half_width) - before.astype(F32)).astype(BF16)


def add_squares(total, values):
    values = values.astype(F32)
    return total + jnp.sum(values * values, axis=0, keepdims=True)


def interior_kernel(width, count, begin, end, rows_ref, *refs):
    n = width
    if begin == 0:
        first_ref, refs = refs[0], refs[1:]
    else:
        older_ref, newer_ref, refs = refs[0], refs[1], refs[2:]
    if end < DEGREE:
        left_ref, right_ref, even_ref, odd_ref = refs
    else:
        left_ref, right_ref, out_ref, squares_ref, even_ref, odd_ref = refs
    buffers = (even_ref, odd_ref)
    for step in range(begin, end):
        source = buffers[step % 2]
        older = target = buffers[(step + 1) % 2]
        if step == begin:
            source = first_ref if begin == 0 else newer_ref
        if step == 1 and begin == 0:
            older = first_ref
        elif step == begin and begin > 0:
            older = older_ref
        elif step == begin + 1 and begin > 0:
            older = newer_ref
        left_ref[step - begin] = source[step * n : (step + 2) * n, :]
        right_ref[step - begin] = source[(count - step - 2) * n : (count - step) * n, :]

        def body(e, carry):
            at = pl.multiple_of(e * n, 16)
            window = source[pl.ds(pl.multiple_of((e - 1) * n, 16), 3 * n), :]
            center = source[pl.ds(at, n), :]
            before = older[pl.ds(at, n), :]
            target[pl.ds(at, n), :] = advance(rows_ref[e, :, : 3 * n], window, center, before, step == 0)
            return carry

        lax.fori_loop(step + 1, count - 1 - step, body, 0, unroll=2)
    if end == DEGREE:
        result = buffers[DEGREE % 2][DEGREE * n : (count - DEGREE) * n, :]
        out_ref[...] = result
        squares_ref[...] = add_squares(jnp.zeros(squares_ref.shape, F32), result)


def strip_kernel(
    width,
    count,
    strip,
    offset,
    last,
    edge_sizes,
    pieces,
    me_ref,
    left_y_ref,
    right_y_ref,
    rows_ref,
    squares_in_ref,
    *refs,
):
    n = width
    depth = DEGREE - 1
    me = me_ref[0]
    refs, outs = refs[:-8], refs[-8:]
    half = len(edge_sizes)
    left_edge = [ref.at[k] for ref, size in zip(refs[:half], edge_sizes) for k in range(size)]
    right_edge = [ref.at[k] for ref, size in zip(refs[half : 2 * half], edge_sizes) for k in range(size)]
    refs = refs[2 * half :]
    out_ref, left_out_ref, right_out_ref, squares_ref, left_scr, right_scr, halo_left, halo_right = outs
    lanes = refs[0].shape[1]
    for index in range(pieces):
        for side in range(2):
            at = pl.ds(pl.multiple_of((me ^ (side * pieces + index)) * lanes, lanes), lanes)
            halo_left[:, :, at] = refs[2 * side * pieces + index][...].reshape(depth, n, lanes)
            halo_right[:, :, at] = refs[(2 * side + 1) * pieces + index][...].reshape(depth, n, lanes)

    def left_row(e):
        if e < 0:
            return halo_left[depth + e, :, : 3 * n]
        if e > 0:
            return rows_ref[e, :, : 3 * n]
        turned = jnp.transpose(halo_left[depth - 1, :, 2 * n : 3 * n].astype(F32))
        keep = rows_ref[0, :, 3 * n : 3 * n + 1].astype(F32)
        return jnp.concatenate([(turned * keep).astype(BF16), rows_ref[0, :, n : 3 * n]], axis=1)

    def right_row(e):
        if e < count:
            return rows_ref[e, :, : 3 * n]
        if e > count:
            return halo_right[e - count, :, : 3 * n]
        turned = jnp.transpose(rows_ref[count - 1, :, 2 * n : 3 * n].astype(F32))
        keep = halo_right[0, :, 3 * n : 3 * n + 1].astype(F32)
        return jnp.concatenate([(turned * keep).astype(BF16), halo_right[0, :, n : 3 * n]], axis=1)

    left_scr[0, : strip * n, :] = left_y_ref[...]
    right_scr[0, 2 * n :, :] = right_y_ref[...]
    for step in range(DEGREE):
        left_scr[step, strip * n :, :] = left_edge[step][...]
        right_scr[step, : 2 * n, :] = right_edge[step][...]
        for j in range(strip):
            e = offset + step + 1 + j
            left_scr[step + 1, j * n : (j + 1) * n, :] = advance(
                left_row(e),
                left_scr[step, j * n : (j + 3) * n, :],
                left_scr[step, (j + 1) * n : (j + 2) * n, :],
                left_scr[max(step - 1, 0), (j + 2) * n : (j + 3) * n, :],
                step == 0,
            )
            e = count - 1 - (offset + strip + step) + j
            right_scr[step + 1, (j + 2) * n : (j + 3) * n, :] = advance(
                right_row(e),
                right_scr[step, j * n : (j + 3) * n, :],
                right_scr[step, (j + 1) * n : (j + 2) * n, :],
                right_scr[max(step - 1, 0), j * n : (j + 1) * n, :],
                step == 0,
            )
        if not last:
            left_out_ref[step] = left_scr[step, : 2 * n, :]
            right_out_ref[step] = right_scr[step, strip * n : (strip + 2) * n, :]
    result_left = left_scr[DEGREE, : strip * n, :]
    result_right = right_scr[DEGREE, 2 * n :, :]
    out_ref[: strip * n, :] = result_left
    out_ref[strip * n : 2 * strip * n, :] = result_right
    squares = add_squares(add_squares(squares_in_ref[...], result_left), result_right)
    squares_ref[...] = squares
    if last:
        high = squares.astype(BF16).astype(F32)
        low = squares - high
        place = lax.broadcasted_iota(jnp.int32, (16, squares.shape[1]), 0)
        both = jnp.where(place == 0, high, jnp.where(place == 1, low, 0.0))
        out_ref[2 * strip * n :, :] = both.astype(BF16)


def gram_kernel(chunks, half, shares, early, *refs):
    if early:
        refs, (out_ref, tails_ref, turned_ref) = refs[:-3], refs[-3:]
    else:
        early_ref, turned_ref, tails_ref, *refs, out_ref = refs
    grid = [refs[c * half : (c + 1) * half] for c in range(chunks)]
    rows = out_ref.shape[1]
    local = grid[0][0].shape[1]
    sizes = [grid[c][0].shape[0] - (16 if c == chunks - 1 else 0) for c in range(chunks)]
    places = [slice(sum(sizes[:c]), sum(sizes[: c + 1])) for c in range(chunks)]
    tails = [grid[-1][r][sizes[-1] :, :] for r in range(half)]
    if early:
        for c in range(chunks):
            turned_ref[:, places[c]] = jnp.transpose(grid[c][0][: sizes[c], :])
        for r in range(half):
            tails_ref[r] = tails[r]
    for r in range(half):
        total = None
        for c in range(chunks):
            term = jnp.dot(turned_ref[:, places[c]], grid[c][r][: sizes[c], :], preferred_element_type=F32)
            total = term if c == 0 else total + term
        at = (r if early else half + r) * local
        out_ref[:, :, at : at + local] = total.astype(BF16).reshape(shares, rows, local)
    if early:
        return
    out_ref[:, :, : half * local] = early_ref[...]
    place = lax.broadcasted_iota(jnp.int32, (rows, LANES), 0)
    parts = local // LANES
    extra = jnp.zeros((rows, LANES), F32)
    for r in range(2 * half):
        both = (tails_ref[r] if r < half else tails[r - half]).astype(F32)
        for p in range(parts):
            for part in range(2):
                line = both[part : part + 1, p * LANES : (p + 1) * LANES]
                extra = jnp.where(place == part * 2 * half * parts + r * parts + p, line, extra)
    for share in range(shares):
        out_ref[share, :, 2 * half * local :] = extra.astype(BF16)


def halves(squares, rows):
    high = squares.astype(BF16).astype(F32)
    spare = jnp.zeros((rows - 2 * squares.shape[0], LANES), F32)
    return jnp.concatenate([high, squares - high, spare])


def sums_kernel(got_ref, out_ref):
    shares, rows, wide = got_ref.shape
    bands = wide - LANES
    parts = bands // LANES
    total = got_ref[0].astype(F32)
    for share in range(1, shares):
        total = total + got_ref[share].astype(F32)
    out_ref[:, :bands] = total[:, :bands].astype(BF16)
    out_ref[:, bands:] = halves(total[:parts, bands:] + total[parts : 2 * parts, bands:], rows).astype(BF16)


def weights_kernel(total_columns, blocks, me_ref, mine_ref, other_ref, out_ref):
    rows, wide = mine_ref.shape
    shares = out_ref.shape[0]
    bands = wide - LANES
    local = bands // blocks
    parts = bands // LANES
    total = mine_ref[...].astype(F32) + other_ref[...].astype(F32)
    tail = total[:, bands:]
    squares = tail[:parts, :] + tail[parts : 2 * parts, :]
    scales = lax.rsqrt(squares + epsilon_norm)
    me = me_ref[0]
    first = me * rows
    row_ids = lax.broadcasted_iota(jnp.int32, (rows, LANES), 0) + first
    lane_ids = lax.broadcasted_iota(jnp.int32, (rows, LANES), 1)
    own = jnp.zeros((rows, 1), F32)
    for p in range(local // LANES):
        hit = row_ids == lane_ids + p * LANES
        own = own + jnp.sum(jnp.where(hit, scales[p : p + 1, :], 0.0), axis=1, keepdims=True)
    for p in range(parts):
        part = total[:, p * LANES : (p + 1) * LANES]
        across = scales[p : p + 1, :]
        diagonal = 0.0
        if p < local // LANES:
            hit = row_ids == lane_ids + p * LANES
            part = jnp.where(hit, squares[p : p + 1, :], part)
            diagonal = jnp.where(hit, 1.5, 0.0)
        weights = math.sqrt(total_columns) * across * (diagonal - 0.5 * (own * part * across))
        weights = weights.astype(BF16)
        for share in range(shares):
            out_ref[share, :, p * LANES : (p + 1) * LANES] = weights


def rotate_kernel(chunks, blocks, spans, weights_ref, *refs):
    out_ref = refs[-1]
    grid = [refs[c * blocks : (c + 1) * blocks] for c in range(chunks)]
    local = grid[0][0].shape[1]
    for c in range(chunks):
        for begin, size, column in spans[c]:
            total = None
            for r in range(blocks):
                term = lax.dot_general(
                    weights_ref[:, r * local : (r + 1) * local],
                    grid[c][r][begin : begin + size, :],
                    (((1,), (1,)), ((), ())),
                    preferred_element_type=F32,
                )
                total = term if total is None else total + term
            out_ref[:, column : column + size] = total.astype(BF16)


def lower_blocks(own):
    bit = lax.axis_size("band") // 4
    found = {0: own}
    while bit:
        for index in list(found):
            found[index ^ bit] = swap(found[index], "band", bit)
        bit //= 2
    return [found[index] for index in sorted(found)]


def fast_shards(basis_sizes, coupling_pattern, h_diag, h_couple, bands):
    count, n = h_diag.shape[:2]
    local = bands.shape[0]
    elem_size, band_size = lax.axis_size("elem"), lax.axis_size("band")
    total_columns = elem_size * count * n
    depth = DEGREE - 1
    wide = -(-(3 * n + 1) // LANES) * LANES
    lanes = wide // band_size
    half = band_size // 2
    elem_me = lax.axis_index("elem").astype(jnp.int32).reshape(1)
    band_me = lax.axis_index("band").astype(jnp.int32).reshape(1)

    first_rows, last_rows = pl.pallas_call(
        functools.partial(ends_kernel, wide),
        out_shape=[jax.ShapeDtypeStruct((depth * n, lanes), BF16)] * 2,
        in_specs=[SMEM] + [HBM] * 4,
        out_specs=[VMEM] * 2,
        scratch_shapes=[pltpu.SMEM((count,), jnp.int32)] * 2
        + [pltpu.VMEM((count, n, n), BF16)] * 2
        + [pltpu.VMEM((2 * depth, n, wide), BF16), pltpu.SemaphoreType.DMA((6,))],
        compiler_params=params(60),
        cost_estimate=about(0.01),
        name="ends",
    )(band_me, basis_sizes, coupling_pattern, h_diag, h_couple)
    rows = pl.pallas_call(
        rows_kernel,
        out_shape=jax.ShapeDtypeStruct((count, n, wide), BF16),
        in_specs=[SMEM] * 2 + [VMEM] * 2,
        out_specs=VMEM,
        compiler_params=params(16),
        cost_estimate=about(0.01),
        name="rows",
    )(basis_sizes, after(coupling_pattern, first_rows), h_diag, h_couple)
    left_rows = from_behind(last_rows, "elem", 1)
    right_rows = from_behind(first_rows, "elem", -1)

    start, *ends = pl.pallas_call(
        functools.partial(vectors_kernel, n, count, math.lcm(n, LANES) // n),
        out_shape=[jax.ShapeDtypeStruct((count * n, local), BF16)]
        + [jax.ShapeDtypeStruct((strip * n, local), BF16) for strip in STRIPS for _ in range(2)],
        in_specs=[SMEM, VMEM],
        out_specs=[VMEM] * (1 + 2 * len(STRIPS)),
        compiler_params=params(16),
        cost_estimate=about(0.01),
        name="vectors",
    )(basis_sizes, bands)

    inner = (count - 2 * DEGREE) * n
    whole = jax.ShapeDtypeStruct((count * n, local), BF16)
    squares_shape = jax.ShapeDtypeStruct((1, local), F32)

    def edges(steps):
        return [jax.ShapeDtypeStruct((steps, 2 * n, local), BF16)] * 2

    left_edge, right_edge, even, odd = pl.pallas_call(
        functools.partial(interior_kernel, n, count, 0, SPLIT),
        out_shape=edges(SPLIT) + [whole] * 2,
        in_specs=[VMEM] * 2,
        out_specs=[VMEM] * 4,
        compiler_params=params(20),
        cost_estimate=about(0.01),
        name="interior_first",
    )(rows, start)
    left_y = [from_behind(after(ends[1], even), "elem", 1)]
    right_y = [from_behind(after(ends[0], even), "elem", -1)]
    own_rows = [after(side, even) for side in (left_rows, right_rows)]
    across_rows = [swap(side, "band", half) for side in own_rows]
    older, newer = (odd, even) if SPLIT % 2 == 0 else (even, odd)
    left_more, right_more, chunk, squares = pl.pallas_call(
        functools.partial(interior_kernel, n, count, SPLIT, DEGREE),
        out_shape=edges(DEGREE - SPLIT) + [jax.ShapeDtypeStruct((inner, local), BF16), squares_shape],
        in_specs=[VMEM] * 3,
        out_specs=[VMEM] * 4,
        scratch_shapes=[pltpu.VMEM((count * n, local), BF16)] * 2,
        compiler_params=params(20),
        cost_estimate=about(0.01),
        name="interior_rest",
    )(rows, older, newer)
    left_edge = [left_edge, left_more]
    right_edge = [right_edge, right_more]
    across_rows = [after(side, chunk, left_y[0], right_y[0]) for side in across_rows]
    for index in range(1, len(STRIPS)):
        left_y.append(from_behind(after(ends[2 * index + 1], chunk), "elem", 1))
        right_y.append(from_behind(after(ends[2 * index], chunk), "elem", -1))
    both = [block for side in (*own_rows, *across_rows) for block in lower_blocks(side)]
    chunks, across = [chunk], [swap(chunk, "band", half)]
    spans = [[(0, inner, DEGREE * n)]]
    offset = 0
    for index, strip in enumerate(STRIPS):
        last = index == len(STRIPS) - 1
        offset -= strip
        if index:
            left_edge = [after(left_edge[0], across[index - 1])]
        size = 2 * strip * n + (16 if last else 0)
        sizes = [edge.shape[0] for edge in left_edge]
        shape = jax.ShapeDtypeStruct((size, local), BF16)
        spare = [jax.ShapeDtypeStruct((8, LANES), F32)] * 2
        chunk, *others, squares = pl.pallas_call(
            functools.partial(strip_kernel, n, count, strip, offset, last, sizes, half),
            out_shape=[shape, *(spare if last else edges(DEGREE)), squares_shape],
            in_specs=[SMEM] + [VMEM] * (4 + 2 * len(sizes) + 4 * half),
            out_specs=[VMEM] * 4,
            scratch_shapes=[pltpu.VMEM((DEGREE + 1, (strip + 2) * n, local), BF16)] * 2
            + [pltpu.VMEM((depth, n, wide), BF16)] * 2,
            compiler_params=params(32),
            cost_estimate=about(3),
            name="strip",
        )(band_me, left_y[index], right_y[index], rows, squares, *left_edge, *right_edge, *both)
        left_edge, right_edge = [others[0]], [others[1]]
        chunks.append(chunk)
        across.append(swap(chunk, "band", half))
        first = offset + DEGREE
        spans.append([(0, strip * n, first * n), (strip * n, strip * n, (count - first - strip) * n)])

    group = elem_size // 2
    groups = [list(range(begin, begin + group)) for begin in (0, group)]
    slice_rows = local // group
    all_bands = local * band_size

    def gram(early, *blocks):
        wide = all_bands // 2 if early else all_bands + LANES
        shapes = [jax.ShapeDtypeStruct((group, slice_rows, wide), BF16)]
        if early:
            shapes.append(jax.ShapeDtypeStruct((half, 16, local), BF16))
            shapes.append(jax.ShapeDtypeStruct((local, count * n), BF16))
        return pl.pallas_call(
            functools.partial(gram_kernel, len(chunks), half, group, early),
            out_shape=shapes,
            in_specs=[VMEM] * len(blocks),
            out_specs=[VMEM] * len(shapes),
            compiler_params=params(20),
            cost_estimate=about(0.01),
            name="gram_early" if early else "gram_late",
        )(*blocks)

    lower = [lower_blocks(chunk) for chunk in chunks]
    early, tails, turned = gram(True, *[block for blocks in lower for block in blocks])
    upper = [lower_blocks(chunk) for chunk in across[:-1]]
    upper.append(lower_blocks(after(across[-1], upper[-1][-1], early)))
    (late,) = gram(False, early, turned, tails, *[block for blocks in upper for block in blocks])
    got = lax.all_to_all(late, "elem", 0, 0, tiled=True, axis_index_groups=groups)
    mine = pl.pallas_call(
        sums_kernel,
        out_shape=jax.ShapeDtypeStruct((slice_rows, all_bands + LANES), BF16),
        in_specs=[VMEM],
        out_specs=VMEM,
        compiler_params=params(8),
        cost_estimate=about(0.01),
        name="sums",
    )(got)
    other = from_behind(mine, "elem", group)
    weights = pl.pallas_call(
        functools.partial(weights_kernel, total_columns, band_size),
        out_shape=jax.ShapeDtypeStruct((group, slice_rows, all_bands), BF16),
        in_specs=[SMEM, VMEM, VMEM],
        out_specs=VMEM,
        compiler_params=params(8),
        cost_estimate=about(0.01),
        name="weights",
    )(elem_me % group, mine, other)
    flat = [block for low, high in zip(lower, upper) for block in (*low, *high)]
    weights = lax.all_to_all(weights, "elem", 0, 0, tiled=True, axis_index_groups=groups).reshape(local, all_bands)
    return pl.pallas_call(
        functools.partial(rotate_kernel, len(chunks), band_size, spans),
        out_shape=jax.ShapeDtypeStruct((local, count * n), BF16),
        in_specs=[VMEM] * (1 + len(flat)),
        out_specs=VMEM,
        compiler_params=params(24),
        cost_estimate=about(0.01),
        name="rotate",
    )(weights, *flat)


def identity_block(shape, offset):
    row_ids = lax.broadcasted_iota(jnp.int32, shape, 0) + offset
    col_ids = lax.broadcasted_iota(jnp.int32, shape, 1)
    return (row_ids == col_ids).astype(jnp.float32)


def rotation_columns(gram_strip, scales, offset, total_rows):
    own_scales = lax.dynamic_slice_in_dim(scales, offset, gram_strip.shape[0], 0)
    identity = identity_block(gram_strip.shape, offset)
    normed = own_scales[:, None] * gram_strip * scales[None, :]
    return (math.sqrt(total_rows) * scales[None, :] * (1.5 * identity - 0.5 * normed)).astype(
        jnp.bfloat16
    )


def general_shards(basis_sizes, coupling_pattern, h_diag, h_couple, bands):
    elem_local = h_diag.shape[0]
    basis_width = h_diag.shape[1]
    band_local = bands.shape[0]
    total_rows = elem_local * lax.axis_size("elem") * basis_width
    columns = lax.broadcasted_iota(jnp.int32, (elem_local, basis_width), 1)
    valid_rows = (columns < basis_sizes[:, None]).astype(jnp.float32)
    coupling = h_couple * coupling_pattern.astype(jnp.bfloat16)[:, None, None]
    current = (
        bands.reshape(band_local, elem_local, basis_width) * valid_rows.astype(jnp.bfloat16)[None]
    )
    previous = current
    for degree in range(DEGREE):
        current_float = current.astype(jnp.float32)
        local_term = jnp.einsum("eij,bej->bei", h_diag, current, preferred_element_type=jnp.float32)
        following = from_behind(current[:, 0], "elem", -1)
        ahead_rows = jnp.concatenate([current[:, 1:], following[:, None]], axis=1)
        upper_term = jnp.einsum(
            "eij,bej->bei", coupling, ahead_rows, preferred_element_type=jnp.float32
        )
        carried = jnp.einsum("eji,bej->bei", coupling, current, preferred_element_type=jnp.float32)
        arrived = from_behind(carried[:, -1], "elem", 1)
        lower_term = jnp.concatenate([arrived[:, None], carried[:, :-1]], axis=1)
        applied = (local_term + upper_term + lower_term) * valid_rows[None]
        shifted = applied - center_shift * current_float
        if degree == 0:
            next_iterate = shifted / half_width
        else:
            next_iterate = 2.0 * shifted / half_width - previous.astype(jnp.float32)
        previous, current = (current, next_iterate.astype(jnp.bfloat16))
    filtered = current.reshape(band_local, elem_local * basis_width)
    every_band = lax.all_gather(filtered, "band", axis=0, tiled=True)
    strip = lax.dot_general(
        filtered, every_band, (((1,), (1,)), ((), ())), preferred_element_type=jnp.float32
    )
    squares = jnp.sum(jnp.square(every_band.astype(jnp.float32)), axis=1)
    strip, squares = lax.psum((strip, squares), "elem")
    scales = lax.rsqrt(squares + epsilon_norm)
    offset = lax.axis_index("band") * band_local
    weights = rotation_columns(strip, scales, offset, total_rows)
    return jnp.dot(weights, every_band, preferred_element_type=jnp.float32).astype(jnp.bfloat16)


def shards(basis_sizes, coupling_pattern, h_diag, h_couple, bands):
    count, n = h_diag.shape[:2]
    local = bands.shape[0]
    elem_size, band_size = lax.axis_size("elem"), lax.axis_size("band")
    rows = local // elem_size
    wide = -(-(3 * n + 1) // LANES) * LANES
    fits = (
        band_size & (band_size - 1) == 0
        and wide % (band_size * LANES) == 0
        and local % LANES == 0
        and elem_size % 2 == 0
        and local % elem_size == 0
        and rows % 16 == 0
        and rows * LANES >= 2 * local * band_size
        and count > 2 * DEGREE
        and n % 16 == 0
    )
    form = fast_shards if fits else general_shards
    return form(basis_sizes, coupling_pattern, h_diag, h_couple, bands)


def solution(mesh):
    in_specs = (
        P("elem"),
        P("elem"),
        P("elem", None, None),
        P("elem", None, None),
        P("band", "elem"),
    )
    out_specs = P("band", "elem")
    return jax.shard_map(shards, mesh=mesh, in_specs=in_specs, out_specs=out_specs, check_vma=False)
```

```python
import functools
import math

import jax
import jax.numpy as jnp
from jax import lax
from jax.experimental import pallas as pl
from jax.experimental.pallas import tpu as pltpu
from jax.sharding import PartitionSpec as P

DEGREE = 6
STRIPS = (3, 3)
SPLIT = 2

center_shift = 0.4
half_width = 2.8
epsilon_norm = 1e-06

LANES = 128
VMEM = pl.BlockSpec(memory_space=pltpu.VMEM)
HBM = pl.BlockSpec(memory_space=pltpu.HBM)
SMEM = pl.BlockSpec(memory_space=pltpu.SMEM)
BF16 = jnp.bfloat16
F32 = jnp.float32


def from_behind(value, axis, steps):
    count = lax.axis_size(axis)
    pairs = [(source, (source + steps) % count) for source in range(count)]
    return lax.ppermute(value, axis, pairs)


def swap(value, axis, bit):
    count = lax.axis_size(axis)
    return lax.ppermute(value, axis, [(source, source ^ bit) for source in range(count)])


def after(value, *others):
    return lax.optimization_barrier((value, *others))[0]


def params(mib):
    return pltpu.CompilerParams(vmem_limit_bytes=mib * 1024 * 1024)


def about(microseconds):
    return pl.CostEstimate(flops=int(microseconds * 1.15e9), bytes_accessed=1, transcendentals=0)


def joined(behind, diag, couple, size, wide):
    n = diag.shape[0]
    whole = jnp.concatenate([behind, diag.astype(F32), couple, jnp.ones((n, wide - 3 * n), F32)], axis=1)
    place = lax.broadcasted_iota(jnp.int32, (n, wide), 0)
    return jnp.where(place < size, whole, 0.0).astype(BF16)


def rows_kernel(sizes_ref, pattern_ref, diag_ref, couple_ref, rows_ref):
    count, n, wide = rows_ref.shape
    behind = jnp.zeros((n, n), F32)
    for e in range(count):
        couple = couple_ref[e].astype(F32) * pattern_ref[e].astype(F32)
        rows_ref[e] = joined(behind, diag_ref[e], couple, sizes_ref[e], wide)
        behind = jnp.transpose(couple)


def packed_width(blocks, width):
    return -(-(blocks * width + DEGREE - 1) // LANES) * LANES


def ends_kernel(me_ref, sizes_in, pattern_in, diag_in, couple_in, first_ref, last_ref, *scratch):
    sizes_ref, pattern_ref, diag_ref, couple_ref, whole_first, whole_last, sems = scratch
    count, n, _ = diag_in.shape
    depth = DEGREE - 1
    share = first_ref.shape[0]
    low, high, before = pl.ds(0, depth), pl.ds(count - depth, depth), pl.ds(count - depth - 1, depth + 1)
    pairs = [(sizes_in, sizes_ref), (pattern_in, pattern_ref)]
    pairs += [(couple_in.at[low], couple_ref.at[low]), (diag_in.at[low], diag_ref.at[low])]
    pairs += [(couple_in.at[before], couple_ref.at[before]), (diag_in.at[high], diag_ref.at[high])]
    copies = [pltpu.make_async_copy(source, target, sems.at[k]) for k, (source, target) in enumerate(pairs)]
    for copy in copies:
        copy.start()
    place = lax.broadcasted_iota(jnp.int32, (n, n), 0)

    def pack(target, out_ref, coupled, elements):
        blocks = []
        for e in coupled:
            block = couple_ref[e].astype(F32) * pattern_ref[e].astype(F32)
            blocks.append(jnp.where(place < sizes_ref[e], block, 0.0))
        for e in elements:
            blocks.append(jnp.where(place < sizes_ref[e], diag_ref[e].astype(F32), 0.0))
        rest = (n, target.shape[1] - len(blocks) * n)
        row, lane = lax.broadcasted_iota(jnp.int32, rest, 0), lax.broadcasted_iota(jnp.int32, rest, 1)
        extra = jnp.zeros(rest, F32)
        for index, e in enumerate(elements):
            extra = jnp.where((lane == index) & (row < sizes_ref[e]), 1.0, extra)
        target[...] = jnp.concatenate([*blocks, extra], axis=1)
        own = pl.ds(pl.multiple_of(me_ref[0] * share, 8), share)
        out_ref[...] = target[own, :].astype(BF16)

    for copy in copies[:4]:
        copy.wait()
    pack(whole_first, first_ref, range(depth), range(depth))
    for copy in copies[4:]:
        copy.wait()
    pack(whole_last, last_ref, range(count - depth - 1, count), range(count - depth, count))


def vectors_kernel(width, count, group, sizes_ref, bands_ref, out_ref, *edge_refs):
    n = width
    local = bands_ref.shape[0]
    place = lax.broadcasted_iota(jnp.int32, (n, local), 0)
    for begin in range(0, count, group):
        turned = jnp.transpose(bands_ref[:, begin * n : (begin + group) * n])
        for e in range(begin, begin + group):
            part = turned[(e - begin) * n : (e - begin + 1) * n, :].astype(F32)
            out_ref[e * n : (e + 1) * n, :] = jnp.where(place < sizes_ref[e], part, 0.0).astype(BF16)
    near = 0
    for index, strip in enumerate(STRIPS):
        far = near + strip
        edge_refs[2 * index][...] = out_ref[near * n : far * n, :]
        edge_refs[2 * index + 1][...] = out_ref[(count - far) * n : (count - near) * n, :]
        near = far


def advance(row, window, center, before, first):
    total = jnp.dot(row, window, preferred_element_type=F32)
    shifted = total - center_shift * center.astype(F32)
    if first:
        return (shifted * (1.0 / half_width)).astype(BF16)
    return (shifted * (2.0 / half_width) - before.astype(F32)).astype(BF16)


def add_squares(total, values):
    values = values.astype(F32)
    return total + jnp.sum(values * values, axis=0, keepdims=True)


def interior_kernel(width, count, begin, end, rows_ref, *refs):
    n = width
    if begin == 0:
        first_ref, refs = refs[0], refs[1:]
    else:
        older_ref, newer_ref, refs = refs[0], refs[1], refs[2:]
    if end < DEGREE:
        left_ref, right_ref, even_ref, odd_ref = refs
    else:
        left_ref, right_ref, out_ref, squares_ref, even_ref, odd_ref = refs
    buffers = (even_ref, odd_ref)
    for step in range(begin, end):
        source = buffers[step % 2]
        older = target = buffers[(step + 1) % 2]
        if step == begin:
            source = first_ref if begin == 0 else newer_ref
        if step == 1 and begin == 0:
            older = first_ref
        elif step == begin and begin > 0:
            older = older_ref
        elif step == begin + 1 and begin > 0:
            older = newer_ref
        left_ref[step - begin] = source[step * n : (step + 2) * n, :]
        right_ref[step - begin] = source[(count - step - 2) * n : (count - step) * n, :]

        def body(e, carry):
            at = pl.multiple_of(e * n, 16)
            window = source[pl.ds(pl.multiple_of((e - 1) * n, 16), 3 * n), :]
            center = source[pl.ds(at, n), :]
            before = older[pl.ds(at, n), :]
            target[pl.ds(at, n), :] = advance(rows_ref[e, :, : 3 * n], window, center, before, step == 0)
            return carry

        lax.fori_loop(step + 1, count - 1 - step, body, 0, unroll=2)
    if end == DEGREE:
        result = buffers[DEGREE % 2][DEGREE * n : (count - DEGREE) * n, :]
        out_ref[...] = result
        squares_ref[...] = add_squares(jnp.zeros(squares_ref.shape, F32), result)


def strip_kernel(
    width,
    count,
    strip,
    offset,
    last,
    edge_sizes,
    pieces,
    me_ref,
    left_y_ref,
    right_y_ref,
    rows_ref,
    squares_in_ref,
    *refs,
):
    n = width
    depth = DEGREE - 1
    me = me_ref[0]
    refs, outs = refs[:-10], refs[-10:]
    half = len(edge_sizes)
    left_edge = [ref.at[k] for ref, size in zip(refs[:half], edge_sizes) for k in range(size)]
    right_edge = [ref.at[k] for ref, size in zip(refs[half : 2 * half], edge_sizes) for k in range(size)]
    refs = refs[2 * half :]
    out_ref, left_out_ref, right_out_ref, squares_ref, left_scr, right_scr, *scratch = outs
    halo_left, halo_right, packed_left, packed_right = scratch
    share = refs[0].shape[0]
    for index in range(pieces):
        for side in range(2):
            at = pl.ds(pl.multiple_of((me ^ (side * pieces + index)) * share, 8), share)
            packed_left[at, :] = refs[2 * side * pieces + index][...].astype(F32)
            packed_right[at, :] = refs[(2 * side + 1) * pieces + index][...].astype(F32)

    def piece(ref, block):
        return ref[:, block * n : (block + 1) * n]

    def valid(ref, blocks, index):
        return ref[:, blocks * n + index : blocks * n + index + 1]

    for index in range(max(depth + offset + 1, 0), depth):
        turned = jnp.transpose(piece(packed_left, index)) * valid(packed_left, 2 * depth + 1, index)
        parts = [turned, piece(packed_left, depth + 1 + index), piece(packed_left, index + 1)]
        halo_left[index, :, : 3 * n] = jnp.concatenate(parts, axis=1).astype(BF16)
    turned = jnp.transpose(piece(packed_left, depth)) * rows_ref[0, :, 3 * n : 3 * n + 1].astype(F32)
    halo_left[depth, :, : 3 * n] = jnp.concatenate([turned.astype(BF16), rows_ref[0, :, n : 3 * n]], axis=1)
    for index in range(min(-offset - 1, depth)):
        if index:
            coupled = piece(packed_right, index - 1)
        else:
            coupled = rows_ref[count - 1, :, 2 * n : 3 * n].astype(F32)
        turned = jnp.transpose(coupled) * valid(packed_right, 2 * depth, index)
        parts = [turned, piece(packed_right, depth + index), piece(packed_right, index)]
        halo_right[index, :, : 3 * n] = jnp.concatenate(parts, axis=1).astype(BF16)

    def left_row(e):
        return halo_left[depth + e, :, : 3 * n] if e <= 0 else rows_ref[e, :, : 3 * n]

    def right_row(e):
        return rows_ref[e, :, : 3 * n] if e < count else halo_right[e - count, :, : 3 * n]

    left_scr[0, : strip * n, :] = left_y_ref[...]
    right_scr[0, 2 * n :, :] = right_y_ref[...]
    for step in range(DEGREE):
        left_scr[step, strip * n :, :] = left_edge[step][...]
        right_scr[step, : 2 * n, :] = right_edge[step][...]
        for j in range(strip):
            e = offset + step + 1 + j
            left_scr[step + 1, j * n : (j + 1) * n, :] = advance(
                left_row(e),
                left_scr[step, j * n : (j + 3) * n, :],
                left_scr[step, (j + 1) * n : (j + 2) * n, :],
                left_scr[max(step - 1, 0), (j + 2) * n : (j + 3) * n, :],
                step == 0,
            )
            e = count - 1 - (offset + strip + step) + j
            right_scr[step + 1, (j + 2) * n : (j + 3) * n, :] = advance(
                right_row(e),
                right_scr[step, j * n : (j + 3) * n, :],
                right_scr[step, (j + 1) * n : (j + 2) * n, :],
                right_scr[max(step - 1, 0), j * n : (j + 1) * n, :],
                step == 0,
            )
        if not last:
            left_out_ref[step] = left_scr[step, : 2 * n, :]
            right_out_ref[step] = right_scr[step, strip * n : (strip + 2) * n, :]
    result_left = left_scr[DEGREE, : strip * n, :]
    result_right = right_scr[DEGREE, 2 * n :, :]
    out_ref[: strip * n, :] = result_left
    out_ref[strip * n : 2 * strip * n, :] = result_right
    squares = add_squares(add_squares(squares_in_ref[...], result_left), result_right)
    squares_ref[...] = squares
    if last:
        high = squares.astype(BF16).astype(F32)
        low = squares - high
        place = lax.broadcasted_iota(jnp.int32, (16, squares.shape[1]), 0)
        both = jnp.where(place == 0, high, jnp.where(place == 1, low, 0.0))
        out_ref[2 * strip * n :, :] = both.astype(BF16)


def gram_kernel(chunks, half, shares, early, *refs):
    if early:
        refs, (out_ref, tails_ref, turned_ref) = refs[:-3], refs[-3:]
    else:
        early_ref, turned_ref, tails_ref, *refs, out_ref = refs
    grid = [refs[c * half : (c + 1) * half] for c in range(chunks)]
    rows = out_ref.shape[1]
    local = grid[0][0].shape[1]
    sizes = [grid[c][0].shape[0] - (16 if c == chunks - 1 else 0) for c in range(chunks)]
    places = [slice(sum(sizes[:c]), sum(sizes[: c + 1])) for c in range(chunks)]
    tails = [grid[-1][r][sizes[-1] :, :] for r in range(half)]
    if early:
        for c in range(chunks):
            turned_ref[:, places[c]] = jnp.transpose(grid[c][0][: sizes[c], :])
        for r in range(half):
            tails_ref[r] = tails[r]
    for r in range(half):
        total = None
        for c in range(chunks):
            term = jnp.dot(turned_ref[:, places[c]], grid[c][r][: sizes[c], :], preferred_element_type=F32)
            total = term if c == 0 else total + term
        at = (r if early else half + r) * local
        out_ref[:, :, at : at + local] = total.astype(BF16).reshape(shares, rows, local)
    if early:
        return
    out_ref[:, :, : half * local] = early_ref[...]
    place = lax.broadcasted_iota(jnp.int32, (rows, LANES), 0)
    parts = local // LANES
    extra = jnp.zeros((rows, LANES), F32)
    for r in range(2 * half):
        both = (tails_ref[r] if r < half else tails[r - half]).astype(F32)
        for p in range(parts):
            for part in range(2):
                line = both[part : part + 1, p * LANES : (p + 1) * LANES]
                extra = jnp.where(place == part * 2 * half * parts + r * parts + p, line, extra)
    for share in range(shares):
        out_ref[share, :, 2 * half * local :] = extra.astype(BF16)


def halves(squares, rows):
    high = squares.astype(BF16).astype(F32)
    spare = jnp.zeros((rows - 2 * squares.shape[0], LANES), F32)
    return jnp.concatenate([high, squares - high, spare])


def sums_kernel(got_ref, out_ref):
    shares, rows, wide = got_ref.shape
    bands = wide - LANES
    parts = bands // LANES
    total = got_ref[0].astype(F32)
    for share in range(1, shares):
        total = total + got_ref[share].astype(F32)
    out_ref[:, :bands] = total[:, :bands].astype(BF16)
    out_ref[:, bands:] = halves(total[:parts, bands:] + total[parts : 2 * parts, bands:], rows).astype(BF16)


def weights_kernel(total_columns, blocks, me_ref, mine_ref, other_ref, out_ref):
    rows, wide = mine_ref.shape
    shares = out_ref.shape[0]
    bands = wide - LANES
    local = bands // blocks
    parts = bands // LANES
    total = mine_ref[...].astype(F32) + other_ref[...].astype(F32)
    tail = total[:, bands:]
    squares = tail[:parts, :] + tail[parts : 2 * parts, :]
    scales = lax.rsqrt(squares + epsilon_norm)
    me = me_ref[0]
    first = me * rows
    row_ids = lax.broadcasted_iota(jnp.int32, (rows, LANES), 0) + first
    lane_ids = lax.broadcasted_iota(jnp.int32, (rows, LANES), 1)
    own = jnp.zeros((rows, 1), F32)
    for p in range(local // LANES):
        hit = row_ids == lane_ids + p * LANES
        own = own + jnp.sum(jnp.where(hit, scales[p : p + 1, :], 0.0), axis=1, keepdims=True)
    for p in range(parts):
        part = total[:, p * LANES : (p + 1) * LANES]
        across = scales[p : p + 1, :]
        diagonal = 0.0
        if p < local // LANES:
            hit = row_ids == lane_ids + p * LANES
            part = jnp.where(hit, squares[p : p + 1, :], part)
            diagonal = jnp.where(hit, 1.5, 0.0)
        weights = math.sqrt(total_columns) * across * (diagonal - 0.5 * (own * part * across))
        weights = weights.astype(BF16)
        for share in range(shares):
            out_ref[share, :, p * LANES : (p + 1) * LANES] = weights


def rotate_kernel(chunks, blocks, spans, weights_ref, *refs):
    out_ref = refs[-1]
    grid = [refs[c * blocks : (c + 1) * blocks] for c in range(chunks)]
    local = grid[0][0].shape[1]
    for c in range(chunks):
        for begin, size, column in spans[c]:
            total = None
            for r in range(blocks):
                term = lax.dot_general(
                    weights_ref[:, r * local : (r + 1) * local],
                    grid[c][r][begin : begin + size, :],
                    (((1,), (1,)), ((), ())),
                    preferred_element_type=F32,
                )
                total = term if total is None else total + term
            out_ref[:, column : column + size] = total.astype(BF16)


def lower_blocks(own):
    bit = lax.axis_size("band") // 4
    found = {0: own}
    while bit:
        for index in list(found):
            found[index ^ bit] = swap(found[index], "band", bit)
        bit //= 2
    return [found[index] for index in sorted(found)]


def fast_shards(basis_sizes, coupling_pattern, h_diag, h_couple, bands):
    count, n = h_diag.shape[:2]
    local = bands.shape[0]
    elem_size, band_size = lax.axis_size("elem"), lax.axis_size("band")
    total_columns = elem_size * count * n
    depth = DEGREE - 1
    wide = -(-(3 * n + 1) // LANES) * LANES
    half = band_size // 2
    elem_me = lax.axis_index("elem").astype(jnp.int32).reshape(1)
    band_me = lax.axis_index("band").astype(jnp.int32).reshape(1)

    packs = packed_width(2 * depth, n), packed_width(2 * depth + 1, n)
    first_rows, last_rows = pl.pallas_call(
        ends_kernel,
        out_shape=[jax.ShapeDtypeStruct((n // band_size, pack), BF16) for pack in packs],
        in_specs=[SMEM] + [HBM] * 4,
        out_specs=[VMEM] * 2,
        scratch_shapes=[pltpu.SMEM((count,), jnp.int32)] * 2
        + [pltpu.VMEM((count, n, n), BF16)] * 2
        + [pltpu.VMEM((n, pack), F32) for pack in packs]
        + [pltpu.SemaphoreType.DMA((6,))],
        compiler_params=params(60),
        cost_estimate=about(0.01),
        name="ends",
    )(band_me, basis_sizes, coupling_pattern, h_diag, h_couple)
    rows = pl.pallas_call(
        rows_kernel,
        out_shape=jax.ShapeDtypeStruct((count, n, wide), BF16),
        in_specs=[SMEM] * 2 + [VMEM] * 2,
        out_specs=VMEM,
        compiler_params=params(16),
        cost_estimate=about(0.01),
        name="rows",
    )(basis_sizes, after(coupling_pattern, first_rows), h_diag, h_couple)
    left_rows = from_behind(last_rows, "elem", 1)
    right_rows = from_behind(first_rows, "elem", -1)

    start, *ends = pl.pallas_call(
        functools.partial(vectors_kernel, n, count, math.lcm(n, LANES) // n),
        out_shape=[jax.ShapeDtypeStruct((count * n, local), BF16)]
        + [jax.ShapeDtypeStruct((strip * n, local), BF16) for strip in STRIPS for _ in range(2)],
        in_specs=[SMEM, VMEM],
        out_specs=[VMEM] * (1 + 2 * len(STRIPS)),
        compiler_params=params(16),
        cost_estimate=about(0.01),
        name="vectors",
    )(basis_sizes, bands)

    inner = (count - 2 * DEGREE) * n
    whole = jax.ShapeDtypeStruct((count * n, local), BF16)
    squares_shape = jax.ShapeDtypeStruct((1, local), F32)

    def edges(steps):
        return [jax.ShapeDtypeStruct((steps, 2 * n, local), BF16)] * 2

    left_edge, right_edge, even, odd = pl.pallas_call(
        functools.partial(interior_kernel, n, count, 0, SPLIT),
        out_shape=edges(SPLIT) + [whole] * 2,
        in_specs=[VMEM] * 2,
        out_specs=[VMEM] * 4,
        compiler_params=params(20),
        cost_estimate=about(0.01),
        name="interior_first",
    )(rows, start)
    left_y = [from_behind(after(ends[1], even), "elem", 1)]
    right_y = [from_behind(after(ends[0], even), "elem", -1)]
    own_rows = [after(side, even) for side in (left_rows, right_rows)]
    across_rows = [swap(side, "band", half) for side in own_rows]
    older, newer = (odd, even) if SPLIT % 2 == 0 else (even, odd)
    left_more, right_more, chunk, squares = pl.pallas_call(
        functools.partial(interior_kernel, n, count, SPLIT, DEGREE),
        out_shape=edges(DEGREE - SPLIT) + [jax.ShapeDtypeStruct((inner, local), BF16), squares_shape],
        in_specs=[VMEM] * 3,
        out_specs=[VMEM] * 4,
        scratch_shapes=[pltpu.VMEM((count * n, local), BF16)] * 2,
        compiler_params=params(20),
        cost_estimate=about(0.01),
        name="interior_rest",
    )(rows, older, newer)
    left_edge = [left_edge, left_more]
    right_edge = [right_edge, right_more]
    across_rows = [after(side, chunk, left_y[0], right_y[0]) for side in across_rows]
    for index in range(1, len(STRIPS)):
        left_y.append(from_behind(after(ends[2 * index + 1], chunk), "elem", 1))
        right_y.append(from_behind(after(ends[2 * index], chunk), "elem", -1))
    both = [block for side in (*own_rows, *across_rows) for block in lower_blocks(side)]
    chunks, across = [chunk], [swap(chunk, "band", half)]
    spans = [[(0, inner, DEGREE * n)]]
    offset = 0
    for index, strip in enumerate(STRIPS):
        last = index == len(STRIPS) - 1
        offset -= strip
        if index:
            left_edge = [after(left_edge[0], across[index - 1])]
        size = 2 * strip * n + (16 if last else 0)
        sizes = [edge.shape[0] for edge in left_edge]
        shape = jax.ShapeDtypeStruct((size, local), BF16)
        spare = [jax.ShapeDtypeStruct((8, LANES), F32)] * 2
        chunk, *others, squares = pl.pallas_call(
            functools.partial(strip_kernel, n, count, strip, offset, last, sizes, half),
            out_shape=[shape, *(spare if last else edges(DEGREE)), squares_shape],
            in_specs=[SMEM] + [VMEM] * (4 + 2 * len(sizes) + 4 * half),
            out_specs=[VMEM] * 4,
            scratch_shapes=[pltpu.VMEM((DEGREE + 1, (strip + 2) * n, local), BF16)] * 2
            + [pltpu.VMEM((depth + 1, n, wide), BF16)] * 2
            + [pltpu.VMEM((n, packs[1]), F32), pltpu.VMEM((n, packs[0]), F32)],
            compiler_params=params(32),
            cost_estimate=about(3),
            name="strip",
        )(band_me, left_y[index], right_y[index], rows, squares, *left_edge, *right_edge, *both)
        left_edge, right_edge = [others[0]], [others[1]]
        chunks.append(chunk)
        across.append(swap(chunk, "band", half))
        first = offset + DEGREE
        spans.append([(0, strip * n, first * n), (strip * n, strip * n, (count - first - strip) * n)])

    group = elem_size // 2
    groups = [list(range(begin, begin + group)) for begin in (0, group)]
    slice_rows = local // group
    all_bands = local * band_size

    def gram(early, *blocks):
        wide = all_bands // 2 if early else all_bands + LANES
        shapes = [jax.ShapeDtypeStruct((group, slice_rows, wide), BF16)]
        if early:
            shapes.append(jax.ShapeDtypeStruct((half, 16, local), BF16))
            shapes.append(jax.ShapeDtypeStruct((local, count * n), BF16))
        return pl.pallas_call(
            functools.partial(gram_kernel, len(chunks), half, group, early),
            out_shape=shapes,
            in_specs=[VMEM] * len(blocks),
            out_specs=[VMEM] * len(shapes),
            compiler_params=params(20),
            cost_estimate=about(0.01),
            name="gram_early" if early else "gram_late",
        )(*blocks)

    lower = [lower_blocks(chunk) for chunk in chunks]
    early, tails, turned = gram(True, *[block for blocks in lower for block in blocks])
    upper = [lower_blocks(chunk) for chunk in across[:-1]]
    upper.append(lower_blocks(after(across[-1], upper[-1][-1], early)))
    (late,) = gram(False, early, turned, tails, *[block for blocks in upper for block in blocks])
    got = lax.all_to_all(late, "elem", 0, 0, tiled=True, axis_index_groups=groups)
    mine = pl.pallas_call(
        sums_kernel,
        out_shape=jax.ShapeDtypeStruct((slice_rows, all_bands + LANES), BF16),
        in_specs=[VMEM],
        out_specs=VMEM,
        compiler_params=params(8),
        cost_estimate=about(0.01),
        name="sums",
    )(got)
    other = from_behind(mine, "elem", group)
    weights = pl.pallas_call(
        functools.partial(weights_kernel, total_columns, band_size),
        out_shape=jax.ShapeDtypeStruct((group, slice_rows, all_bands), BF16),
        in_specs=[SMEM, VMEM, VMEM],
        out_specs=VMEM,
        compiler_params=params(8),
        cost_estimate=about(0.01),
        name="weights",
    )(elem_me % group, mine, other)
    flat = [block for low, high in zip(lower, upper) for block in (*low, *high)]
    weights = lax.all_to_all(weights, "elem", 0, 0, tiled=True, axis_index_groups=groups).reshape(local, all_bands)
    return pl.pallas_call(
        functools.partial(rotate_kernel, len(chunks), band_size, spans),
        out_shape=jax.ShapeDtypeStruct((local, count * n), BF16),
        in_specs=[VMEM] * (1 + len(flat)),
        out_specs=VMEM,
        compiler_params=params(24),
        cost_estimate=about(0.01),
        name="rotate",
    )(weights, *flat)


def identity_block(shape, offset):
    row_ids = lax.broadcasted_iota(jnp.int32, shape, 0) + offset
    col_ids = lax.broadcasted_iota(jnp.int32, shape, 1)
    return (row_ids == col_ids).astype(jnp.float32)


def rotation_columns(gram_strip, scales, offset, total_rows):
    own_scales = lax.dynamic_slice_in_dim(scales, offset, gram_strip.shape[0], 0)
    identity = identity_block(gram_strip.shape, offset)
    normed = own_scales[:, None] * gram_strip * scales[None, :]
    return (math.sqrt(total_rows) * scales[None, :] * (1.5 * identity - 0.5 * normed)).astype(
        jnp.bfloat16
    )


def general_shards(basis_sizes, coupling_pattern, h_diag, h_couple, bands):
    elem_local = h_diag.shape[0]
    basis_width = h_diag.shape[1]
    band_local = bands.shape[0]
    total_rows = elem_local * lax.axis_size("elem") * basis_width
    columns = lax.broadcasted_iota(jnp.int32, (elem_local, basis_width), 1)
    valid_rows = (columns < basis_sizes[:, None]).astype(jnp.float32)
    coupling = h_couple * coupling_pattern.astype(jnp.bfloat16)[:, None, None]
    current = (
        bands.reshape(band_local, elem_local, basis_width) * valid_rows.astype(jnp.bfloat16)[None]
    )
    previous = current
    for degree in range(DEGREE):
        current_float = current.astype(jnp.float32)
        local_term = jnp.einsum("eij,bej->bei", h_diag, current, preferred_element_type=jnp.float32)
        following = from_behind(current[:, 0], "elem", -1)
        ahead_rows = jnp.concatenate([current[:, 1:], following[:, None]], axis=1)
        upper_term = jnp.einsum(
            "eij,bej->bei", coupling, ahead_rows, preferred_element_type=jnp.float32
        )
        carried = jnp.einsum("eji,bej->bei", coupling, current, preferred_element_type=jnp.float32)
        arrived = from_behind(carried[:, -1], "elem", 1)
        lower_term = jnp.concatenate([arrived[:, None], carried[:, :-1]], axis=1)
        applied = (local_term + upper_term + lower_term) * valid_rows[None]
        shifted = applied - center_shift * current_float
        if degree == 0:
            next_iterate = shifted / half_width
        else:
            next_iterate = 2.0 * shifted / half_width - previous.astype(jnp.float32)
        previous, current = (current, next_iterate.astype(jnp.bfloat16))
    filtered = current.reshape(band_local, elem_local * basis_width)
    every_band = lax.all_gather(filtered, "band", axis=0, tiled=True)
    strip = lax.dot_general(
        filtered, every_band, (((1,), (1,)), ((), ())), preferred_element_type=jnp.float32
    )
    squares = jnp.sum(jnp.square(every_band.astype(jnp.float32)), axis=1)
    strip, squares = lax.psum((strip, squares), "elem")
    scales = lax.rsqrt(squares + epsilon_norm)
    offset = lax.axis_index("band") * band_local
    weights = rotation_columns(strip, scales, offset, total_rows)
    return jnp.dot(weights, every_band, preferred_element_type=jnp.float32).astype(jnp.bfloat16)


def shards(basis_sizes, coupling_pattern, h_diag, h_couple, bands):
    count, n = h_diag.shape[:2]
    local = bands.shape[0]
    elem_size, band_size = lax.axis_size("elem"), lax.axis_size("band")
    rows = local // elem_size
    wide = -(-(3 * n + 1) // LANES) * LANES
    fits = (
        band_size & (band_size - 1) == 0
        and n % (8 * band_size) == 0
        and local % LANES == 0
        and elem_size % 2 == 0
        and local % elem_size == 0
        and rows % 16 == 0
        and rows * LANES >= 2 * local * band_size
        and count > 2 * DEGREE
        and n % 16 == 0
    )
    form = fast_shards if fits else general_shards
    return form(basis_sizes, coupling_pattern, h_diag, h_couple, bands)


def solution(mesh):
    in_specs = (
        P("elem"),
        P("elem"),
        P("elem", None, None),
        P("elem", None, None),
        P("band", "elem"),
    )
    out_specs = P("band", "elem")
    return jax.shard_map(shards, mesh=mesh, in_specs=in_specs, out_specs=out_specs, check_vma=False)
```

```python
import functools
import math

import jax
import jax.numpy as jnp
from jax import lax
from jax.experimental import pallas as pl
from jax.experimental.pallas import tpu as pltpu
from jax.sharding import PartitionSpec as P

DEGREE = 6
STRIPS = (3, 3)
SPLIT = 2

center_shift = 0.4
half_width = 2.8
epsilon_norm = 1e-06

LANES = 128
VMEM = pl.BlockSpec(memory_space=pltpu.VMEM)
HBM = pl.BlockSpec(memory_space=pltpu.HBM)
SMEM = pl.BlockSpec(memory_space=pltpu.SMEM)
BF16 = jnp.bfloat16
F32 = jnp.float32


def from_behind(value, axis, steps):
    count = lax.axis_size(axis)
    pairs = [(source, (source + steps) % count) for source in range(count)]
    return lax.ppermute(value, axis, pairs)


def swap(value, axis, bit):
    count = lax.axis_size(axis)
    return lax.ppermute(value, axis, [(source, source ^ bit) for source in range(count)])


def after(value, *others):
    return lax.optimization_barrier((value, *others))[0]


def params(mib):
    return pltpu.CompilerParams(vmem_limit_bytes=mib * 1024 * 1024)


def about(microseconds):
    return pl.CostEstimate(flops=int(microseconds * 1.15e9), bytes_accessed=1, transcendentals=0)


def joined(behind, diag, couple, size, wide):
    n = diag.shape[0]
    whole = jnp.concatenate([behind, diag.astype(F32), couple, jnp.ones((n, wide - 3 * n), F32)], axis=1)
    place = lax.broadcasted_iota(jnp.int32, (n, wide), 0)
    return jnp.where(place < size, whole, 0.0).astype(BF16)


def rows_kernel(sizes_ref, pattern_ref, diag_ref, couple_ref, rows_ref):
    count, n, wide = rows_ref.shape
    behind = jnp.zeros((n, n), F32)
    for e in range(count):
        couple = couple_ref[e].astype(F32) * pattern_ref[e].astype(F32)
        rows_ref[e] = joined(behind, diag_ref[e], couple, sizes_ref[e], wide)
        behind = jnp.transpose(couple)


def packed_width(blocks, width):
    return -(-(blocks * width + DEGREE - 1) // LANES) * LANES


def ends_kernel(me_ref, sizes_in, pattern_in, diag_in, couple_in, first_ref, last_ref, *scratch):
    sizes_ref, pattern_ref, diag_ref, couple_ref, whole_first, whole_last, sems = scratch
    count, n, _ = diag_in.shape
    depth = DEGREE - 1
    share = first_ref.shape[0]
    low, high, before = pl.ds(0, depth), pl.ds(count - depth, depth), pl.ds(count - depth - 1, depth + 1)
    pairs = [(sizes_in, sizes_ref), (pattern_in, pattern_ref)]
    pairs += [(couple_in.at[low], couple_ref.at[low]), (diag_in.at[low], diag_ref.at[low])]
    pairs += [(couple_in.at[before], couple_ref.at[before]), (diag_in.at[high], diag_ref.at[high])]
    copies = [pltpu.make_async_copy(source, target, sems.at[k]) for k, (source, target) in enumerate(pairs)]
    for copy in copies:
        copy.start()
    place = lax.broadcasted_iota(jnp.int32, (n, n), 0)

    def pack(target, out_ref, coupled, elements):
        blocks = []
        for e in coupled:
            block = couple_ref[e].astype(F32) * pattern_ref[e].astype(F32)
            blocks.append(jnp.where(place < sizes_ref[e], block, 0.0))
        for e in elements:
            blocks.append(jnp.where(place < sizes_ref[e], diag_ref[e].astype(F32), 0.0))
        rest = (n, target.shape[1] - len(blocks) * n)
        row, lane = lax.broadcasted_iota(jnp.int32, rest, 0), lax.broadcasted_iota(jnp.int32, rest, 1)
        extra = jnp.zeros(rest, F32)
        for index, e in enumerate(elements):
            extra = jnp.where((lane == index) & (row < sizes_ref[e]), 1.0, extra)
        target[...] = jnp.concatenate([*blocks, extra], axis=1)
        own = pl.ds(pl.multiple_of(me_ref[0] * share, 8), share)
        out_ref[...] = target[own, :].astype(BF16)

    for copy in copies[:4]:
        copy.wait()
    pack(whole_first, first_ref, range(depth), range(depth))
    for copy in copies[4:]:
        copy.wait()
    pack(whole_last, last_ref, range(count - depth - 1, count), range(count - depth, count))


def vectors_kernel(width, count, group, sizes_ref, bands_ref, out_ref, *edge_refs):
    n = width
    local = bands_ref.shape[0]
    place = lax.broadcasted_iota(jnp.int32, (n, local), 0)
    for begin in range(0, count, group):
        turned = jnp.transpose(bands_ref[:, begin * n : (begin + group) * n])
        for e in range(begin, begin + group):
            part = turned[(e - begin) * n : (e - begin + 1) * n, :].astype(F32)
            out_ref[e * n : (e + 1) * n, :] = jnp.where(place < sizes_ref[e], part, 0.0).astype(BF16)
    near = 0
    for index, strip in enumerate(STRIPS):
        far = near + strip
        edge_refs[2 * index][...] = out_ref[near * n : far * n, :]
        edge_refs[2 * index + 1][...] = out_ref[(count - far) * n : (count - near) * n, :]
        near = far


def advance(row, window, center, before, first):
    total = jnp.dot(row, window, preferred_element_type=F32)
    shifted = total - center_shift * center.astype(F32)
    if first:
        return (shifted * (1.0 / half_width)).astype(BF16)
    return (shifted * (2.0 / half_width) - before.astype(F32)).astype(BF16)


def add_squares(total, values):
    values = values.astype(F32)
    return total + jnp.sum(values * values, axis=0, keepdims=True)


def interior_kernel(width, count, begin, end, rows_ref, *refs):
    n = width
    if begin == 0:
        first_ref, refs = refs[0], refs[1:]
    else:
        older_ref, newer_ref, refs = refs[0], refs[1], refs[2:]
    if end < DEGREE:
        left_ref, right_ref, even_ref, odd_ref = refs
    else:
        left_ref, right_ref, out_ref, squares_ref, even_ref, odd_ref = refs
    buffers = (even_ref, odd_ref)
    for step in range(begin, end):
        source = buffers[step % 2]
        older = target = buffers[(step + 1) % 2]
        if step == begin:
            source = first_ref if begin == 0 else newer_ref
        if step == 1 and begin == 0:
            older = first_ref
        elif step == begin and begin > 0:
            older = older_ref
        elif step == begin + 1 and begin > 0:
            older = newer_ref
        left_ref[step - begin] = source[step * n : (step + 2) * n, :]
        right_ref[step - begin] = source[(count - step - 2) * n : (count - step) * n, :]

        def body(e, carry):
            at = pl.multiple_of(e * n, 16)
            window = source[pl.ds(pl.multiple_of((e - 1) * n, 16), 3 * n), :]
            center = source[pl.ds(at, n), :]
            before = older[pl.ds(at, n), :]
            target[pl.ds(at, n), :] = advance(rows_ref[e, :, : 3 * n], window, center, before, step == 0)
            return carry

        lax.fori_loop(step + 1, count - 1 - step, body, 0, unroll=2)
    if end == DEGREE:
        result = buffers[DEGREE % 2][DEGREE * n : (count - DEGREE) * n, :]
        out_ref[...] = result
        squares_ref[...] = add_squares(jnp.zeros(squares_ref.shape, F32), result)


def strip_kernel(
    width,
    count,
    strip,
    offset,
    last,
    edge_sizes,
    pieces,
    me_ref,
    left_y_ref,
    right_y_ref,
    rows_ref,
    squares_in_ref,
    *refs,
):
    n = width
    depth = DEGREE - 1
    me = me_ref[0]
    refs, outs = refs[:-10], refs[-10:]
    half = len(edge_sizes)
    left_edge = [ref.at[k] for ref, size in zip(refs[:half], edge_sizes) for k in range(size)]
    right_edge = [ref.at[k] for ref, size in zip(refs[half : 2 * half], edge_sizes) for k in range(size)]
    refs = refs[2 * half :]
    out_ref, left_out_ref, right_out_ref, squares_ref, left_scr, right_scr, *scratch = outs
    halo_left, halo_right, packed_left, packed_right = scratch
    share = refs[0].shape[0]
    for index in range(pieces):
        for side in range(2):
            at = pl.ds(pl.multiple_of((me ^ (side * pieces + index)) * share, 8), share)
            packed_left[at, :] = refs[2 * side * pieces + index][...].astype(F32)
            packed_right[at, :] = refs[(2 * side + 1) * pieces + index][...].astype(F32)

    def piece(ref, block):
        return ref[:, block * n : (block + 1) * n]

    def valid(ref, blocks, index):
        return ref[:, blocks * n + index : blocks * n + index + 1]

    for index in range(max(depth + offset + 1, 0), depth):
        turned = jnp.transpose(piece(packed_left, index)) * valid(packed_left, 2 * depth + 1, index)
        parts = [turned, piece(packed_left, depth + 1 + index), piece(packed_left, index + 1)]
        halo_left[index, :, : 3 * n] = jnp.concatenate(parts, axis=1).astype(BF16)
    turned = jnp.transpose(piece(packed_left, depth)) * rows_ref[0, :, 3 * n : 3 * n + 1].astype(F32)
    halo_left[depth, :, : 3 * n] = jnp.concatenate([turned.astype(BF16), rows_ref[0, :, n : 3 * n]], axis=1)
    for index in range(min(-offset - 1, depth)):
        if index:
            coupled = piece(packed_right, index - 1)
        else:
            coupled = rows_ref[count - 1, :, 2 * n : 3 * n].astype(F32)
        turned = jnp.transpose(coupled) * valid(packed_right, 2 * depth, index)
        parts = [turned, piece(packed_right, depth + index), piece(packed_right, index)]
        halo_right[index, :, : 3 * n] = jnp.concatenate(parts, axis=1).astype(BF16)

    def left_row(e):
        return halo_left[depth + e, :, : 3 * n] if e <= 0 else rows_ref[e, :, : 3 * n]

    def right_row(e):
        return rows_ref[e, :, : 3 * n] if e < count else halo_right[e - count, :, : 3 * n]

    left_scr[0, : strip * n, :] = left_y_ref[...]
    right_scr[0, 2 * n :, :] = right_y_ref[...]
    for step in range(DEGREE):
        left_scr[step, strip * n :, :] = left_edge[step][...]
        right_scr[step, : 2 * n, :] = right_edge[step][...]
        for j in range(strip):
            e = offset + step + 1 + j
            left_scr[step + 1, j * n : (j + 1) * n, :] = advance(
                left_row(e),
                left_scr[step, j * n : (j + 3) * n, :],
                left_scr[step, (j + 1) * n : (j + 2) * n, :],
                left_scr[max(step - 1, 0), (j + 2) * n : (j + 3) * n, :],
                step == 0,
            )
            e = count - 1 - (offset + strip + step) + j
            right_scr[step + 1, (j + 2) * n : (j + 3) * n, :] = advance(
                right_row(e),
                right_scr[step, j * n : (j + 3) * n, :],
                right_scr[step, (j + 1) * n : (j + 2) * n, :],
                right_scr[max(step - 1, 0), j * n : (j + 1) * n, :],
                step == 0,
            )
        if not last:
            left_out_ref[step] = left_scr[step, : 2 * n, :]
            right_out_ref[step] = right_scr[step, strip * n : (strip + 2) * n, :]
    result_left = left_scr[DEGREE, : strip * n, :]
    result_right = right_scr[DEGREE, 2 * n :, :]
    out_ref[: strip * n, :] = result_left
    out_ref[strip * n : 2 * strip * n, :] = result_right
    squares = add_squares(add_squares(squares_in_ref[...], result_left), result_right)
    squares_ref[...] = squares
    if last:
        high = squares.astype(BF16).astype(F32)
        low = squares - high
        place = lax.broadcasted_iota(jnp.int32, (16, squares.shape[1]), 0)
        both = jnp.where(place == 0, high, jnp.where(place == 1, low, 0.0))
        out_ref[2 * strip * n :, :] = both.astype(BF16)


def gram_kernel(chunks, half, shares, early, *refs):
    if early:
        refs, (out_ref, tails_ref, turned_ref) = refs[:-3], refs[-3:]
    else:
        early_ref, turned_ref, tails_ref, *refs, out_ref = refs
    grid = [refs[c * half : (c + 1) * half] for c in range(chunks)]
    rows = out_ref.shape[1]
    local = grid[0][0].shape[1]
    sizes = [grid[c][0].shape[0] - (16 if c == chunks - 1 else 0) for c in range(chunks)]
    places = [slice(sum(sizes[:c]), sum(sizes[: c + 1])) for c in range(chunks)]
    tails = [grid[-1][r][sizes[-1] :, :] for r in range(half)]
    if early:
        for c in range(chunks):
            turned_ref[:, places[c]] = jnp.transpose(grid[c][0][: sizes[c], :])
        for r in range(half):
            tails_ref[r] = tails[r]
    for r in range(half):
        total = None
        for c in range(chunks):
            term = jnp.dot(turned_ref[:, places[c]], grid[c][r][: sizes[c], :], preferred_element_type=F32)
            total = term if c == 0 else total + term
        at = (r if early else half + r) * local
        out_ref[:, :, at : at + local] = total.astype(BF16).reshape(shares, rows, local)
    if early:
        return
    out_ref[:, :, : half * local] = early_ref[...]
    place = lax.broadcasted_iota(jnp.int32, (rows, LANES), 0)
    parts = local // LANES
    extra = jnp.zeros((rows, LANES), F32)
    for r in range(2 * half):
        both = (tails_ref[r] if r < half else tails[r - half]).astype(F32)
        for p in range(parts):
            for part in range(2):
                line = both[part : part + 1, p * LANES : (p + 1) * LANES]
                extra = jnp.where(place == part * 2 * half * parts + r * parts + p, line, extra)
    for share in range(shares):
        out_ref[share, :, 2 * half * local :] = extra.astype(BF16)


def halves(squares, rows):
    high = squares.astype(BF16).astype(F32)
    spare = jnp.zeros((rows - 2 * squares.shape[0], LANES), F32)
    return jnp.concatenate([high, squares - high, spare])


def sums_kernel(got_ref, out_ref):
    shares, rows, wide = got_ref.shape
    bands = wide - LANES
    parts = bands // LANES
    total = got_ref[0].astype(F32)
    for share in range(1, shares):
        total = total + got_ref[share].astype(F32)
    out_ref[:, :bands] = total[:, :bands].astype(BF16)
    out_ref[:, bands:] = halves(total[:parts, bands:] + total[parts : 2 * parts, bands:], rows).astype(BF16)


def weights_kernel(total_columns, blocks, me_ref, mine_ref, other_ref, out_ref):
    rows, wide = mine_ref.shape
    shares = out_ref.shape[0]
    bands = wide - LANES
    local = bands // blocks
    parts = bands // LANES
    total = mine_ref[...].astype(F32) + other_ref[...].astype(F32)
    tail = total[:, bands:]
    squares = tail[:parts, :] + tail[parts : 2 * parts, :]
    scales = lax.rsqrt(squares + epsilon_norm)
    me = me_ref[0]
    first = me * rows
    row_ids = lax.broadcasted_iota(jnp.int32, (rows, LANES), 0) + first
    lane_ids = lax.broadcasted_iota(jnp.int32, (rows, LANES), 1)
    own = jnp.zeros((rows, 1), F32)
    for p in range(local // LANES):
        hit = row_ids == lane_ids + p * LANES
        own = own + jnp.sum(jnp.where(hit, scales[p : p + 1, :], 0.0), axis=1, keepdims=True)
    for p in range(parts):
        part = total[:, p * LANES : (p + 1) * LANES]
        across = scales[p : p + 1, :]
        diagonal = 0.0
        if p < local // LANES:
            hit = row_ids == lane_ids + p * LANES
            part = jnp.where(hit, squares[p : p + 1, :], part)
            diagonal = jnp.where(hit, 1.5, 0.0)
        weights = math.sqrt(total_columns) * across * (diagonal - 0.5 * (own * part * across))
        weights = weights.astype(BF16)
        for share in range(shares):
            out_ref[share, :, p * LANES : (p + 1) * LANES] = weights


def rotate_kernel(chunks, blocks, spans, weights_ref, *refs):
    out_ref = refs[-1]
    grid = [refs[c * blocks : (c + 1) * blocks] for c in range(chunks)]
    local = grid[0][0].shape[1]
    for c in range(chunks):
        for begin, size, column in spans[c]:
            total = None
            for r in range(blocks):
                term = lax.dot_general(
                    weights_ref[:, r * local : (r + 1) * local],
                    grid[c][r][begin : begin + size, :],
                    (((1,), (1,)), ((), ())),
                    preferred_element_type=F32,
                )
                total = term if total is None else total + term
            out_ref[:, column : column + size] = total.astype(BF16)


def lower_blocks(own):
    bit = lax.axis_size("band") // 4
    found = {0: own}
    while bit:
        for index in list(found):
            found[index ^ bit] = swap(found[index], "band", bit)
        bit //= 2
    return [found[index] for index in sorted(found)]


def fast_shards(basis_sizes, coupling_pattern, h_diag, h_couple, bands):
    count, n = h_diag.shape[:2]
    local = bands.shape[0]
    elem_size, band_size = lax.axis_size("elem"), lax.axis_size("band")
    total_columns = elem_size * count * n
    depth = DEGREE - 1
    wide = -(-(3 * n + 1) // LANES) * LANES
    half = band_size // 2
    elem_me = lax.axis_index("elem").astype(jnp.int32).reshape(1)
    band_me = lax.axis_index("band").astype(jnp.int32).reshape(1)

    packs = packed_width(2 * depth, n), packed_width(2 * depth + 1, n)
    first_rows, last_rows = pl.pallas_call(
        ends_kernel,
        out_shape=[jax.ShapeDtypeStruct((n // band_size, pack), BF16) for pack in packs],
        in_specs=[SMEM] + [HBM] * 4,
        out_specs=[VMEM] * 2,
        scratch_shapes=[pltpu.SMEM((count,), jnp.int32)] * 2
        + [pltpu.VMEM((count, n, n), BF16)] * 2
        + [pltpu.VMEM((n, pack), F32) for pack in packs]
        + [pltpu.SemaphoreType.DMA((6,))],
        compiler_params=params(60),
        cost_estimate=about(0.01),
        name="ends",
    )(band_me, basis_sizes, coupling_pattern, h_diag, h_couple)
    rows = pl.pallas_call(
        rows_kernel,
        out_shape=jax.ShapeDtypeStruct((count, n, wide), BF16),
        in_specs=[SMEM] * 2 + [VMEM] * 2,
        out_specs=VMEM,
        compiler_params=params(16),
        cost_estimate=about(0.01),
        name="rows",
    )(basis_sizes, after(coupling_pattern, first_rows), h_diag, h_couple)
    left_rows = from_behind(last_rows, "elem", 1)
    right_rows = from_behind(first_rows, "elem", -1)

    start, *ends = pl.pallas_call(
        functools.partial(vectors_kernel, n, count, math.lcm(n, LANES) // n),
        out_shape=[jax.ShapeDtypeStruct((count * n, local), BF16)]
        + [jax.ShapeDtypeStruct((strip * n, local), BF16) for strip in STRIPS for _ in range(2)],
        in_specs=[SMEM, VMEM],
        out_specs=[VMEM] * (1 + 2 * len(STRIPS)),
        compiler_params=params(16),
        cost_estimate=about(0.01),
        name="vectors",
    )(basis_sizes, bands)

    inner = (count - 2 * DEGREE) * n
    whole = jax.ShapeDtypeStruct((count * n, local), BF16)
    squares_shape = jax.ShapeDtypeStruct((1, local), F32)

    def edges(steps):
        return [jax.ShapeDtypeStruct((steps, 2 * n, local), BF16)] * 2

    left_edge, right_edge, even, odd = pl.pallas_call(
        functools.partial(interior_kernel, n, count, 0, SPLIT),
        out_shape=edges(SPLIT) + [whole] * 2,
        in_specs=[VMEM] * 2,
        out_specs=[VMEM] * 4,
        compiler_params=params(20),
        cost_estimate=about(0.01),
        name="interior_first",
    )(rows, start)
    left_y = [from_behind(ends[1], "elem", 1)]
    right_y = [from_behind(ends[0], "elem", -1)]
    own_rows = [after(side, even) for side in (left_rows, right_rows)]
    across_rows = [swap(side, "band", half) for side in own_rows]
    older, newer = (odd, even) if SPLIT % 2 == 0 else (even, odd)
    left_more, right_more, chunk, squares = pl.pallas_call(
        functools.partial(interior_kernel, n, count, SPLIT, DEGREE),
        out_shape=edges(DEGREE - SPLIT) + [jax.ShapeDtypeStruct((inner, local), BF16), squares_shape],
        in_specs=[VMEM] * 3,
        out_specs=[VMEM] * 4,
        scratch_shapes=[pltpu.VMEM((count * n, local), BF16)] * 2,
        compiler_params=params(20),
        cost_estimate=about(0.01),
        name="interior_rest",
    )(rows, older, newer)
    left_edge = [left_edge, left_more]
    right_edge = [right_edge, right_more]
    across_rows = [after(side, chunk, left_y[0], right_y[0]) for side in across_rows]
    for index in range(1, len(STRIPS)):
        left_y.append(from_behind(after(ends[2 * index + 1], chunk), "elem", 1))
        right_y.append(from_behind(after(ends[2 * index], chunk), "elem", -1))
    both = [block for side in (*own_rows, *across_rows) for block in lower_blocks(side)]
    chunks, across = [chunk], [swap(chunk, "band", half)]
    spans = [[(0, inner, DEGREE * n)]]
    offset = 0
    for index, strip in enumerate(STRIPS):
        last = index == len(STRIPS) - 1
        offset -= strip
        if index:
            left_edge = [after(left_edge[0], across[index - 1])]
        size = 2 * strip * n + (16 if last else 0)
        sizes = [edge.shape[0] for edge in left_edge]
        shape = jax.ShapeDtypeStruct((size, local), BF16)
        spare = [jax.ShapeDtypeStruct((8, LANES), F32)] * 2
        chunk, *others, squares = pl.pallas_call(
            functools.partial(strip_kernel, n, count, strip, offset, last, sizes, half),
            out_shape=[shape, *(spare if last else edges(DEGREE)), squares_shape],
            in_specs=[SMEM] + [VMEM] * (4 + 2 * len(sizes) + 4 * half),
            out_specs=[VMEM] * 4,
            scratch_shapes=[pltpu.VMEM((DEGREE + 1, (strip + 2) * n, local), BF16)] * 2
            + [pltpu.VMEM((depth + 1, n, wide), BF16)] * 2
            + [pltpu.VMEM((n, packs[1]), F32), pltpu.VMEM((n, packs[0]), F32)],
            compiler_params=params(32),
            cost_estimate=about(3),
            name="strip",
        )(band_me, left_y[index], right_y[index], rows, squares, *left_edge, *right_edge, *both)
        left_edge, right_edge = [others[0]], [others[1]]
        chunks.append(chunk)
        across.append(swap(chunk, "band", half))
        first = offset + DEGREE
        spans.append([(0, strip * n, first * n), (strip * n, strip * n, (count - first - strip) * n)])

    group = elem_size // 2
    groups = [list(range(begin, begin + group)) for begin in (0, group)]
    slice_rows = local // group
    all_bands = local * band_size

    def gram(early, *blocks):
        wide = all_bands // 2 if early else all_bands + LANES
        shapes = [jax.ShapeDtypeStruct((group, slice_rows, wide), BF16)]
        if early:
            shapes.append(jax.ShapeDtypeStruct((half, 16, local), BF16))
            shapes.append(jax.ShapeDtypeStruct((local, count * n), BF16))
        return pl.pallas_call(
            functools.partial(gram_kernel, len(chunks), half, group, early),
            out_shape=shapes,
            in_specs=[VMEM] * len(blocks),
            out_specs=[VMEM] * len(shapes),
            compiler_params=params(20),
            cost_estimate=about(0.01),
            name="gram_early" if early else "gram_late",
        )(*blocks)

    lower = [lower_blocks(chunk) for chunk in chunks]
    early, tails, turned = gram(True, *[block for blocks in lower for block in blocks])
    upper = [lower_blocks(chunk) for chunk in across[:-1]]
    upper.append(lower_blocks(after(across[-1], upper[-1][-1], early)))
    (late,) = gram(False, early, turned, tails, *[block for blocks in upper for block in blocks])
    got = lax.all_to_all(late, "elem", 0, 0, tiled=True, axis_index_groups=groups)
    mine = pl.pallas_call(
        sums_kernel,
        out_shape=jax.ShapeDtypeStruct((slice_rows, all_bands + LANES), BF16),
        in_specs=[VMEM],
        out_specs=VMEM,
        compiler_params=params(8),
        cost_estimate=about(0.01),
        name="sums",
    )(got)
    other = from_behind(mine, "elem", group)
    weights = pl.pallas_call(
        functools.partial(weights_kernel, total_columns, band_size),
        out_shape=jax.ShapeDtypeStruct((group, slice_rows, all_bands), BF16),
        in_specs=[SMEM, VMEM, VMEM],
        out_specs=VMEM,
        compiler_params=params(8),
        cost_estimate=about(0.01),
        name="weights",
    )(elem_me % group, mine, other)
    flat = [block for low, high in zip(lower, upper) for block in (*low, *high)]
    weights = lax.all_to_all(weights, "elem", 0, 0, tiled=True, axis_index_groups=groups).reshape(local, all_bands)
    return pl.pallas_call(
        functools.partial(rotate_kernel, len(chunks), band_size, spans),
        out_shape=jax.ShapeDtypeStruct((local, count * n), BF16),
        in_specs=[VMEM] * (1 + len(flat)),
        out_specs=VMEM,
        compiler_params=params(24),
        cost_estimate=about(0.01),
        name="rotate",
    )(weights, *flat)


def identity_block(shape, offset):
    row_ids = lax.broadcasted_iota(jnp.int32, shape, 0) + offset
    col_ids = lax.broadcasted_iota(jnp.int32, shape, 1)
    return (row_ids == col_ids).astype(jnp.float32)


def rotation_columns(gram_strip, scales, offset, total_rows):
    own_scales = lax.dynamic_slice_in_dim(scales, offset, gram_strip.shape[0], 0)
    identity = identity_block(gram_strip.shape, offset)
    normed = own_scales[:, None] * gram_strip * scales[None, :]
    return (math.sqrt(total_rows) * scales[None, :] * (1.5 * identity - 0.5 * normed)).astype(
        jnp.bfloat16
    )


def general_shards(basis_sizes, coupling_pattern, h_diag, h_couple, bands):
    elem_local = h_diag.shape[0]
    basis_width = h_diag.shape[1]
    band_local = bands.shape[0]
    total_rows = elem_local * lax.axis_size("elem") * basis_width
    columns = lax.broadcasted_iota(jnp.int32, (elem_local, basis_width), 1)
    valid_rows = (columns < basis_sizes[:, None]).astype(jnp.float32)
    coupling = h_couple * coupling_pattern.astype(jnp.bfloat16)[:, None, None]
    current = (
        bands.reshape(band_local, elem_local, basis_width) * valid_rows.astype(jnp.bfloat16)[None]
    )
    previous = current
    for degree in range(DEGREE):
        current_float = current.astype(jnp.float32)
        local_term = jnp.einsum("eij,bej->bei", h_diag, current, preferred_element_type=jnp.float32)
        following = from_behind(current[:, 0], "elem", -1)
        ahead_rows = jnp.concatenate([current[:, 1:], following[:, None]], axis=1)
        upper_term = jnp.einsum(
            "eij,bej->bei", coupling, ahead_rows, preferred_element_type=jnp.float32
        )
        carried = jnp.einsum("eji,bej->bei", coupling, current, preferred_element_type=jnp.float32)
        arrived = from_behind(carried[:, -1], "elem", 1)
        lower_term = jnp.concatenate([arrived[:, None], carried[:, :-1]], axis=1)
        applied = (local_term + upper_term + lower_term) * valid_rows[None]
        shifted = applied - center_shift * current_float
        if degree == 0:
            next_iterate = shifted / half_width
        else:
            next_iterate = 2.0 * shifted / half_width - previous.astype(jnp.float32)
        previous, current = (current, next_iterate.astype(jnp.bfloat16))
    filtered = current.reshape(band_local, elem_local * basis_width)
    every_band = lax.all_gather(filtered, "band", axis=0, tiled=True)
    strip = lax.dot_general(
        filtered, every_band, (((1,), (1,)), ((), ())), preferred_element_type=jnp.float32
    )
    squares = jnp.sum(jnp.square(every_band.astype(jnp.float32)), axis=1)
    strip, squares = lax.psum((strip, squares), "elem")
    scales = lax.rsqrt(squares + epsilon_norm)
    offset = lax.axis_index("band") * band_local
    weights = rotation_columns(strip, scales, offset, total_rows)
    return jnp.dot(weights, every_band, preferred_element_type=jnp.float32).astype(jnp.bfloat16)


def shards(basis_sizes, coupling_pattern, h_diag, h_couple, bands):
    count, n = h_diag.shape[:2]
    local = bands.shape[0]
    elem_size, band_size = lax.axis_size("elem"), lax.axis_size("band")
    rows = local // elem_size
    wide = -(-(3 * n + 1) // LANES) * LANES
    fits = (
        band_size & (band_size - 1) == 0
        and n % (8 * band_size) == 0
        and local % LANES == 0
        and elem_size % 2 == 0
        and local % elem_size == 0
        and rows % 16 == 0
        and rows * LANES >= 2 * local * band_size
        and count > 2 * DEGREE
        and n % 16 == 0
    )
    form = fast_shards if fits else general_shards
    return form(basis_sizes, coupling_pattern, h_diag, h_couple, bands)


def solution(mesh):
    in_specs = (
        P("elem"),
        P("elem"),
        P("elem", None, None),
        P("elem", None, None),
        P("band", "elem"),
    )
    out_specs = P("band", "elem")
    return jax.shard_map(shards, mesh=mesh, in_specs=in_specs, out_specs=out_specs, check_vma=False)
```

```python
import functools
import math

import jax
import jax.numpy as jnp
from jax import lax
from jax.experimental import pallas as pl
from jax.experimental.pallas import tpu as pltpu
from jax.sharding import PartitionSpec as P

DEGREE = 6
STRIPS = (3, 3)
SPLIT = 2

center_shift = 0.4
half_width = 2.8
epsilon_norm = 1e-06

LANES = 128
VMEM = pl.BlockSpec(memory_space=pltpu.VMEM)
HBM = pl.BlockSpec(memory_space=pltpu.HBM)
SMEM = pl.BlockSpec(memory_space=pltpu.SMEM)
BF16 = jnp.bfloat16
F32 = jnp.float32


def from_behind(value, axis, steps):
    count = lax.axis_size(axis)
    pairs = [(source, (source + steps) % count) for source in range(count)]
    return lax.ppermute(value, axis, pairs)


def swap(value, axis, bit):
    count = lax.axis_size(axis)
    return lax.ppermute(value, axis, [(source, source ^ bit) for source in range(count)])


def after(value, *others):
    return lax.optimization_barrier((value, *others))[0]


def params(mib):
    return pltpu.CompilerParams(vmem_limit_bytes=mib * 1024 * 1024)


def about(microseconds):
    return pl.CostEstimate(flops=int(microseconds * 1.15e9), bytes_accessed=1, transcendentals=0)


def joined(behind, diag, couple, size, wide):
    n = diag.shape[0]
    whole = jnp.concatenate([behind, diag.astype(F32), couple, jnp.ones((n, wide - 3 * n), F32)], axis=1)
    place = lax.broadcasted_iota(jnp.int32, (n, wide), 0)
    return jnp.where(place < size, whole, 0.0).astype(BF16)


def rows_kernel(sizes_ref, pattern_ref, diag_ref, couple_ref, rows_ref):
    count, n, wide = rows_ref.shape
    behind = jnp.zeros((n, n), F32)
    for e in range(count):
        couple = couple_ref[e].astype(F32) * pattern_ref[e].astype(F32)
        rows_ref[e] = joined(behind, diag_ref[e], couple, sizes_ref[e], wide)
        behind = jnp.transpose(couple)


def packed_width(blocks, width):
    return -(-(blocks * width + DEGREE - 1) // LANES) * LANES


def ends_kernel(me_ref, sizes_in, pattern_in, diag_in, couple_in, first_ref, last_ref, *scratch):
    sizes_ref, pattern_ref, diag_ref, couple_ref, whole_first, whole_last, sems = scratch
    count, n, _ = diag_in.shape
    depth = DEGREE - 1
    share = first_ref.shape[0]
    low, high, before = pl.ds(0, depth), pl.ds(count - depth, depth), pl.ds(count - depth - 1, depth + 1)
    pairs = [(sizes_in, sizes_ref), (pattern_in, pattern_ref)]
    pairs += [(couple_in.at[low], couple_ref.at[low]), (diag_in.at[low], diag_ref.at[low])]
    pairs += [(couple_in.at[before], couple_ref.at[before]), (diag_in.at[high], diag_ref.at[high])]
    copies = [pltpu.make_async_copy(source, target, sems.at[k]) for k, (source, target) in enumerate(pairs)]
    for copy in copies:
        copy.start()
    place = lax.broadcasted_iota(jnp.int32, (n, n), 0)

    def pack(target, out_ref, coupled, elements):
        blocks = []
        for e in coupled:
            block = couple_ref[e].astype(F32) * pattern_ref[e].astype(F32)
            blocks.append(jnp.where(place < sizes_ref[e], block, 0.0))
        for e in elements:
            blocks.append(jnp.where(place < sizes_ref[e], diag_ref[e].astype(F32), 0.0))
        rest = (n, target.shape[1] - len(blocks) * n)
        row, lane = lax.broadcasted_iota(jnp.int32, rest, 0), lax.broadcasted_iota(jnp.int32, rest, 1)
        extra = jnp.zeros(rest, F32)
        for index, e in enumerate(elements):
            extra = jnp.where((lane == index) & (row < sizes_ref[e]), 1.0, extra)
        target[...] = jnp.concatenate([*blocks, extra], axis=1)
        own = pl.ds(pl.multiple_of(me_ref[0] * share, 8), share)
        out_ref[...] = target[own, :].astype(BF16)

    for copy in copies[:4]:
        copy.wait()
    pack(whole_first, first_ref, range(depth), range(depth))
    for copy in copies[4:]:
        copy.wait()
    pack(whole_last, last_ref, range(count - depth - 1, count), range(count - depth, count))


def vectors_kernel(width, count, group, sizes_ref, bands_ref, out_ref, *edge_refs):
    n = width
    local = bands_ref.shape[0]
    place = lax.broadcasted_iota(jnp.int32, (n, local), 0)
    for begin in range(0, count, group):
        turned = jnp.transpose(bands_ref[:, begin * n : (begin + group) * n])
        for e in range(begin, begin + group):
            part = turned[(e - begin) * n : (e - begin + 1) * n, :].astype(F32)
            out_ref[e * n : (e + 1) * n, :] = jnp.where(place < sizes_ref[e], part, 0.0).astype(BF16)
    near = 0
    for index, strip in enumerate(STRIPS):
        far = near + strip
        edge_refs[2 * index][...] = out_ref[near * n : far * n, :]
        edge_refs[2 * index + 1][...] = out_ref[(count - far) * n : (count - near) * n, :]
        near = far


def advance(row, window, center, before, first):
    total = jnp.dot(row, window, preferred_element_type=F32)
    shifted = total - center_shift * center.astype(F32)
    if first:
        return (shifted * (1.0 / half_width)).astype(BF16)
    return (shifted * (2.0 / half_width) - before.astype(F32)).astype(BF16)


def add_squares(total, values):
    values = values.astype(F32)
    return total + jnp.sum(values * values, axis=0, keepdims=True)


def interior_kernel(width, count, begin, end, rows_ref, *refs):
    n = width
    if begin == 0:
        first_ref, refs = refs[0], refs[1:]
    else:
        older_ref, newer_ref, refs = refs[0], refs[1], refs[2:]
    if end < DEGREE:
        left_ref, right_ref, even_ref, odd_ref = refs
    else:
        left_ref, right_ref, out_ref, squares_ref, even_ref, odd_ref = refs
    buffers = (even_ref, odd_ref)
    for step in range(begin, end):
        source = buffers[step % 2]
        older = target = buffers[(step + 1) % 2]
        if step == begin:
            source = first_ref if begin == 0 else newer_ref
        if step == 1 and begin == 0:
            older = first_ref
        elif step == begin and begin > 0:
            older = older_ref
        elif step == begin + 1 and begin > 0:
            older = newer_ref
        left_ref[step - begin] = source[step * n : (step + 2) * n, :]
        right_ref[step - begin] = source[(count - step - 2) * n : (count - step) * n, :]

        def body(e, carry):
            at = pl.multiple_of(e * n, 16)
            window = source[pl.ds(pl.multiple_of((e - 1) * n, 16), 3 * n), :]
            center = source[pl.ds(at, n), :]
            before = older[pl.ds(at, n), :]
            target[pl.ds(at, n), :] = advance(rows_ref[e, :, : 3 * n], window, center, before, step == 0)
            return carry

        lax.fori_loop(step + 1, count - 1 - step, body, 0, unroll=2)
    if end == DEGREE:
        result = buffers[DEGREE % 2][DEGREE * n : (count - DEGREE) * n, :]
        out_ref[...] = result
        squares_ref[...] = add_squares(jnp.zeros(squares_ref.shape, F32), result)


def strip_kernel(
    width,
    count,
    strip,
    offset,
    last,
    edge_sizes,
    pieces,
    me_ref,
    left_y_ref,
    right_y_ref,
    rows_ref,
    squares_in_ref,
    *refs,
):
    n = width
    depth = DEGREE - 1
    me = me_ref[0]
    refs, outs = refs[:-10], refs[-10:]
    half = len(edge_sizes)
    left_edge = [ref.at[k] for ref, size in zip(refs[:half], edge_sizes) for k in range(size)]
    right_edge = [ref.at[k] for ref, size in zip(refs[half : 2 * half], edge_sizes) for k in range(size)]
    refs = refs[2 * half :]
    out_ref, left_out_ref, right_out_ref, squares_ref, left_scr, right_scr, *scratch = outs
    halo_left, halo_right, packed_left, packed_right = scratch
    share = refs[0].shape[0]
    for index in range(pieces):
        for side in range(2):
            at = pl.ds(pl.multiple_of((me ^ (side * pieces + index)) * share, 8), share)
            packed_left[at, :] = refs[2 * side * pieces + index][...].astype(F32)
            packed_right[at, :] = refs[(2 * side + 1) * pieces + index][...].astype(F32)

    def piece(ref, block):
        return ref[:, block * n : (block + 1) * n]

    def valid(ref, blocks, index):
        return ref[:, blocks * n + index : blocks * n + index + 1]

    for index in range(max(depth + offset + 1, 0), depth):
        turned = jnp.transpose(piece(packed_left, index)) * valid(packed_left, 2 * depth + 1, index)
        parts = [turned, piece(packed_left, depth + 1 + index), piece(packed_left, index + 1)]
        halo_left[index, :, : 3 * n] = jnp.concatenate(parts, axis=1).astype(BF16)
    turned = jnp.transpose(piece(packed_left, depth)) * rows_ref[0, :, 3 * n : 3 * n + 1].astype(F32)
    halo_left[depth, :, : 3 * n] = jnp.concatenate([turned.astype(BF16), rows_ref[0, :, n : 3 * n]], axis=1)
    for index in range(min(-offset - 1, depth)):
        if index:
            coupled = piece(packed_right, index - 1)
        else:
            coupled = rows_ref[count - 1, :, 2 * n : 3 * n].astype(F32)
        turned = jnp.transpose(coupled) * valid(packed_right, 2 * depth, index)
        parts = [turned, piece(packed_right, depth + index), piece(packed_right, index)]
        halo_right[index, :, : 3 * n] = jnp.concatenate(parts, axis=1).astype(BF16)

    def left_row(e):
        return halo_left[depth + e, :, : 3 * n] if e <= 0 else rows_ref[e, :, : 3 * n]

    def right_row(e):
        return rows_ref[e, :, : 3 * n] if e < count else halo_right[e - count, :, : 3 * n]

    left_scr[0, : strip * n, :] = left_y_ref[...]
    right_scr[0, 2 * n :, :] = right_y_ref[...]
    for step in range(DEGREE):
        left_scr[step, strip * n :, :] = left_edge[step][...]
        right_scr[step, : 2 * n, :] = right_edge[step][...]
        for j in range(strip):
            e = offset + step + 1 + j
            left_scr[step + 1, j * n : (j + 1) * n, :] = advance(
                left_row(e),
                left_scr[step, j * n : (j + 3) * n, :],
                left_scr[step, (j + 1) * n : (j + 2) * n, :],
                left_scr[max(step - 1, 0), (j + 2) * n : (j + 3) * n, :],
                step == 0,
            )
            e = count - 1 - (offset + strip + step) + j
            right_scr[step + 1, (j + 2) * n : (j + 3) * n, :] = advance(
                right_row(e),
                right_scr[step, j * n : (j + 3) * n, :],
                right_scr[step, (j + 1) * n : (j + 2) * n, :],
                right_scr[max(step - 1, 0), j * n : (j + 1) * n, :],
                step == 0,
            )
        if not last:
            left_out_ref[step] = left_scr[step, : 2 * n, :]
            right_out_ref[step] = right_scr[step, strip * n : (strip + 2) * n, :]
    result_left = left_scr[DEGREE, : strip * n, :]
    result_right = right_scr[DEGREE, 2 * n :, :]
    out_ref[: strip * n, :] = result_left
    out_ref[strip * n : 2 * strip * n, :] = result_right
    squares = add_squares(add_squares(squares_in_ref[...], result_left), result_right)
    squares_ref[...] = squares
    if last:
        high = squares.astype(BF16).astype(F32)
        low = squares - high
        place = lax.broadcasted_iota(jnp.int32, (16, squares.shape[1]), 0)
        both = jnp.where(place == 0, high, jnp.where(place == 1, low, 0.0))
        out_ref[2 * strip * n :, :] = both.astype(BF16)


def gram_kernel(chunks, half, shares, early, *refs):
    if early:
        refs, (out_ref, tails_ref, turned_ref) = refs[:-3], refs[-3:]
    else:
        early_ref, turned_ref, tails_ref, *refs, out_ref = refs
    grid = [refs[c * half : (c + 1) * half] for c in range(chunks)]
    rows = out_ref.shape[1]
    local = grid[0][0].shape[1]
    sizes = [grid[c][0].shape[0] - (16 if c == chunks - 1 else 0) for c in range(chunks)]
    places = [slice(sum(sizes[:c]), sum(sizes[: c + 1])) for c in range(chunks)]
    tails = [grid[-1][r][sizes[-1] :, :] for r in range(half)]
    if early:
        for c in range(chunks):
            turned_ref[:, places[c]] = jnp.transpose(grid[c][0][: sizes[c], :])
        for r in range(half):
            tails_ref[r] = tails[r]
    for r in range(half):
        total = None
        for c in range(chunks):
            term = jnp.dot(turned_ref[:, places[c]], grid[c][r][: sizes[c], :], preferred_element_type=F32)
            total = term if c == 0 else total + term
        at = (r if early else half + r) * local
        out_ref[:, :, at : at + local] = total.astype(BF16).reshape(shares, rows, local)
    if early:
        return
    out_ref[:, :, : half * local] = early_ref[...]
    place = lax.broadcasted_iota(jnp.int32, (rows, LANES), 0)
    parts = local // LANES
    extra = jnp.zeros((rows, LANES), F32)
    for r in range(2 * half):
        both = (tails_ref[r] if r < half else tails[r - half]).astype(F32)
        for p in range(parts):
            for part in range(2):
                line = both[part : part + 1, p * LANES : (p + 1) * LANES]
                extra = jnp.where(place == part * 2 * half * parts + r * parts + p, line, extra)
    for share in range(shares):
        out_ref[share, :, 2 * half * local :] = extra.astype(BF16)


def halves(squares, rows):
    high = squares.astype(BF16).astype(F32)
    spare = jnp.zeros((rows - 2 * squares.shape[0], LANES), F32)
    return jnp.concatenate([high, squares - high, spare])


def sums_kernel(got_ref, out_ref):
    shares, rows, wide = got_ref.shape
    bands = wide - LANES
    parts = bands // LANES
    total = got_ref[0].astype(F32)
    for share in range(1, shares):
        total = total + got_ref[share].astype(F32)
    out_ref[:, :bands] = total[:, :bands].astype(BF16)
    out_ref[:, bands:] = halves(total[:parts, bands:] + total[parts : 2 * parts, bands:], rows).astype(BF16)


def weights_kernel(total_columns, blocks, me_ref, mine_ref, other_ref, out_ref):
    rows, wide = mine_ref.shape
    shares = out_ref.shape[0]
    bands = wide - LANES
    local = bands // blocks
    parts = bands // LANES
    total = mine_ref[...].astype(F32) + other_ref[...].astype(F32)
    tail = total[:, bands:]
    squares = tail[:parts, :] + tail[parts : 2 * parts, :]
    scales = lax.rsqrt(squares + epsilon_norm)
    me = me_ref[0]
    first = me * rows
    row_ids = lax.broadcasted_iota(jnp.int32, (rows, LANES), 0) + first
    lane_ids = lax.broadcasted_iota(jnp.int32, (rows, LANES), 1)
    own = jnp.zeros((rows, 1), F32)
    for p in range(local // LANES):
        hit = row_ids == lane_ids + p * LANES
        own = own + jnp.sum(jnp.where(hit, scales[p : p + 1, :], 0.0), axis=1, keepdims=True)
    for p in range(parts):
        part = total[:, p * LANES : (p + 1) * LANES]
        across = scales[p : p + 1, :]
        diagonal = 0.0
        if p < local // LANES:
            hit = row_ids == lane_ids + p * LANES
            part = jnp.where(hit, squares[p : p + 1, :], part)
            diagonal = jnp.where(hit, 1.5, 0.0)
        weights = math.sqrt(total_columns) * across * (diagonal - 0.5 * (own * part * across))
        weights = weights.astype(BF16)
        for share in range(shares):
            out_ref[share, :, p * LANES : (p + 1) * LANES] = weights


def rotate_kernel(chunks, blocks, spans, weights_ref, *refs):
    out_ref, made_ref, sems = refs[-3:]
    grid = [refs[c * blocks : (c + 1) * blocks] for c in range(chunks)]
    local = grid[0][0].shape[1]
    order = sorted((column, begin, size, c) for c in range(chunks) for begin, size, column in spans[c])
    copies = []
    sent = 0
    for index, (column, begin, size, c) in enumerate(order):
        total = None
        for r in range(blocks):
            term = lax.dot_general(
                weights_ref[:, r * local : (r + 1) * local],
                grid[c][r][begin : begin + size, :],
                (((1,), (1,)), ((), ())),
                preferred_element_type=F32,
            )
            total = term if total is None else total + term
        made_ref[:, column : column + size] = total.astype(BF16)
        done = column + size
        ready = done if index == len(order) - 1 else done // LANES * LANES
        if ready > sent:
            at = pl.ds(sent, ready - sent)
            copies.append(pltpu.make_async_copy(made_ref.at[:, at], out_ref.at[:, at], sems.at[len(copies)]))
            copies[-1].start()
            sent = ready
    for copy in copies:
        copy.wait()


def lower_blocks(own):
    bit = lax.axis_size("band") // 4
    found = {0: own}
    while bit:
        for index in list(found):
            found[index ^ bit] = swap(found[index], "band", bit)
        bit //= 2
    return [found[index] for index in sorted(found)]


def fast_shards(basis_sizes, coupling_pattern, h_diag, h_couple, bands):
    count, n = h_diag.shape[:2]
    local = bands.shape[0]
    elem_size, band_size = lax.axis_size("elem"), lax.axis_size("band")
    total_columns = elem_size * count * n
    depth = DEGREE - 1
    wide = -(-(3 * n + 1) // LANES) * LANES
    half = band_size // 2
    elem_me = lax.axis_index("elem").astype(jnp.int32).reshape(1)
    band_me = lax.axis_index("band").astype(jnp.int32).reshape(1)

    packs = packed_width(2 * depth, n), packed_width(2 * depth + 1, n)
    first_rows, last_rows = pl.pallas_call(
        ends_kernel,
        out_shape=[jax.ShapeDtypeStruct((n // band_size, pack), BF16) for pack in packs],
        in_specs=[SMEM] + [HBM] * 4,
        out_specs=[VMEM] * 2,
        scratch_shapes=[pltpu.SMEM((count,), jnp.int32)] * 2
        + [pltpu.VMEM((count, n, n), BF16)] * 2
        + [pltpu.VMEM((n, pack), F32) for pack in packs]
        + [pltpu.SemaphoreType.DMA((6,))],
        compiler_params=params(60),
        cost_estimate=about(0.01),
        name="ends",
    )(band_me, basis_sizes, coupling_pattern, h_diag, h_couple)
    rows = pl.pallas_call(
        rows_kernel,
        out_shape=jax.ShapeDtypeStruct((count, n, wide), BF16),
        in_specs=[SMEM] * 2 + [VMEM] * 2,
        out_specs=VMEM,
        compiler_params=params(16),
        cost_estimate=about(0.01),
        name="rows",
    )(basis_sizes, after(coupling_pattern, first_rows), h_diag, h_couple)
    left_rows = from_behind(last_rows, "elem", 1)
    right_rows = from_behind(first_rows, "elem", -1)

    start, *ends = pl.pallas_call(
        functools.partial(vectors_kernel, n, count, math.lcm(n, LANES) // n),
        out_shape=[jax.ShapeDtypeStruct((count * n, local), BF16)]
        + [jax.ShapeDtypeStruct((strip * n, local), BF16) for strip in STRIPS for _ in range(2)],
        in_specs=[SMEM, VMEM],
        out_specs=[VMEM] * (1 + 2 * len(STRIPS)),
        compiler_params=params(16),
        cost_estimate=about(0.01),
        name="vectors",
    )(basis_sizes, bands)

    inner = (count - 2 * DEGREE) * n
    whole = jax.ShapeDtypeStruct((count * n, local), BF16)
    squares_shape = jax.ShapeDtypeStruct((1, local), F32)

    def edges(steps):
        return [jax.ShapeDtypeStruct((steps, 2 * n, local), BF16)] * 2

    left_edge, right_edge, even, odd = pl.pallas_call(
        functools.partial(interior_kernel, n, count, 0, SPLIT),
        out_shape=edges(SPLIT) + [whole] * 2,
        in_specs=[VMEM] * 2,
        out_specs=[VMEM] * 4,
        compiler_params=params(20),
        cost_estimate=about(0.01),
        name="interior_first",
    )(rows, start)
    left_y = [from_behind(ends[1], "elem", 1)]
    right_y = [from_behind(ends[0], "elem", -1)]
    own_rows = [after(side, even) for side in (left_rows, right_rows)]
    across_rows = [swap(side, "band", half) for side in own_rows]
    older, newer = (odd, even) if SPLIT % 2 == 0 else (even, odd)
    left_more, right_more, chunk, squares = pl.pallas_call(
        functools.partial(interior_kernel, n, count, SPLIT, DEGREE),
        out_shape=edges(DEGREE - SPLIT) + [jax.ShapeDtypeStruct((inner, local), BF16), squares_shape],
        in_specs=[VMEM] * 3,
        out_specs=[VMEM] * 4,
        scratch_shapes=[pltpu.VMEM((count * n, local), BF16)] * 2,
        compiler_params=params(20),
        cost_estimate=about(0.01),
        name="interior_rest",
    )(rows, older, newer)
    left_edge = [left_edge, left_more]
    right_edge = [right_edge, right_more]
    across_rows = [after(side, chunk, left_y[0], right_y[0]) for side in across_rows]
    for index in range(1, len(STRIPS)):
        left_y.append(from_behind(after(ends[2 * index + 1], chunk), "elem", 1))
        right_y.append(from_behind(after(ends[2 * index], chunk), "elem", -1))
    both = [block for side in (*own_rows, *across_rows) for block in lower_blocks(side)]
    chunks, across = [chunk], [swap(chunk, "band", half)]
    spans = [[(0, inner, DEGREE * n)]]
    offset = 0
    for index, strip in enumerate(STRIPS):
        last = index == len(STRIPS) - 1
        offset -= strip
        if index:
            left_edge = [after(left_edge[0], across[index - 1])]
        size = 2 * strip * n + (16 if last else 0)
        sizes = [edge.shape[0] for edge in left_edge]
        shape = jax.ShapeDtypeStruct((size, local), BF16)
        spare = [jax.ShapeDtypeStruct((8, LANES), F32)] * 2
        chunk, *others, squares = pl.pallas_call(
            functools.partial(strip_kernel, n, count, strip, offset, last, sizes, half),
            out_shape=[shape, *(spare if last else edges(DEGREE)), squares_shape],
            in_specs=[SMEM] + [VMEM] * (4 + 2 * len(sizes) + 4 * half),
            out_specs=[VMEM] * 4,
            scratch_shapes=[pltpu.VMEM((DEGREE + 1, (strip + 2) * n, local), BF16)] * 2
            + [pltpu.VMEM((depth + 1, n, wide), BF16)] * 2
            + [pltpu.VMEM((n, packs[1]), F32), pltpu.VMEM((n, packs[0]), F32)],
            compiler_params=params(32),
            cost_estimate=about(3),
            name="strip",
        )(band_me, left_y[index], right_y[index], rows, squares, *left_edge, *right_edge, *both)
        left_edge, right_edge = [others[0]], [others[1]]
        chunks.append(chunk)
        across.append(swap(chunk, "band", half))
        first = offset + DEGREE
        spans.append([(0, strip * n, first * n), (strip * n, strip * n, (count - first - strip) * n)])

    group = elem_size // 2
    groups = [list(range(begin, begin + group)) for begin in (0, group)]
    slice_rows = local // group
    all_bands = local * band_size

    def gram(early, *blocks):
        wide = all_bands // 2 if early else all_bands + LANES
        shapes = [jax.ShapeDtypeStruct((group, slice_rows, wide), BF16)]
        if early:
            shapes.append(jax.ShapeDtypeStruct((half, 16, local), BF16))
            shapes.append(jax.ShapeDtypeStruct((local, count * n), BF16))
        return pl.pallas_call(
            functools.partial(gram_kernel, len(chunks), half, group, early),
            out_shape=shapes,
            in_specs=[VMEM] * len(blocks),
            out_specs=[VMEM] * len(shapes),
            compiler_params=params(20),
            cost_estimate=about(0.01),
            name="gram_early" if early else "gram_late",
        )(*blocks)

    lower = [lower_blocks(chunk) for chunk in chunks]
    early, tails, turned = gram(True, *[block for blocks in lower for block in blocks])
    upper = [lower_blocks(chunk) for chunk in across[:-1]]
    upper.append(lower_blocks(after(across[-1], upper[-1][-1], early)))
    (late,) = gram(False, early, turned, tails, *[block for blocks in upper for block in blocks])
    got = lax.all_to_all(late, "elem", 0, 0, tiled=True, axis_index_groups=groups)
    mine = pl.pallas_call(
        sums_kernel,
        out_shape=jax.ShapeDtypeStruct((slice_rows, all_bands + LANES), BF16),
        in_specs=[VMEM],
        out_specs=VMEM,
        compiler_params=params(8),
        cost_estimate=about(0.01),
        name="sums",
    )(got)
    other = from_behind(mine, "elem", group)
    weights = pl.pallas_call(
        functools.partial(weights_kernel, total_columns, band_size),
        out_shape=jax.ShapeDtypeStruct((group, slice_rows, all_bands), BF16),
        in_specs=[SMEM, VMEM, VMEM],
        out_specs=VMEM,
        compiler_params=params(8),
        cost_estimate=about(0.01),
        name="weights",
    )(elem_me % group, mine, other)
    flat = [block for low, high in zip(lower, upper) for block in (*low, *high)]
    weights = lax.all_to_all(weights, "elem", 0, 0, tiled=True, axis_index_groups=groups).reshape(local, all_bands)
    return pl.pallas_call(
        functools.partial(rotate_kernel, len(chunks), band_size, spans),
        out_shape=jax.ShapeDtypeStruct((local, count * n), BF16),
        in_specs=[VMEM] * (1 + len(flat)),
        out_specs=HBM,
        scratch_shapes=[
            pltpu.VMEM((local, count * n), BF16),
            pltpu.SemaphoreType.DMA((1 + 2 * len(STRIPS),)),
        ],
        compiler_params=params(24),
        cost_estimate=about(0.01),
        name="rotate",
    )(weights, *flat)


def identity_block(shape, offset):
    row_ids = lax.broadcasted_iota(jnp.int32, shape, 0) + offset
    col_ids = lax.broadcasted_iota(jnp.int32, shape, 1)
    return (row_ids == col_ids).astype(jnp.float32)


def rotation_columns(gram_strip, scales, offset, total_rows):
    own_scales = lax.dynamic_slice_in_dim(scales, offset, gram_strip.shape[0], 0)
    identity = identity_block(gram_strip.shape, offset)
    normed = own_scales[:, None] * gram_strip * scales[None, :]
    return (math.sqrt(total_rows) * scales[None, :] * (1.5 * identity - 0.5 * normed)).astype(
        jnp.bfloat16
    )


def general_shards(basis_sizes, coupling_pattern, h_diag, h_couple, bands):
    elem_local = h_diag.shape[0]
    basis_width = h_diag.shape[1]
    band_local = bands.shape[0]
    total_rows = elem_local * lax.axis_size("elem") * basis_width
    columns = lax.broadcasted_iota(jnp.int32, (elem_local, basis_width), 1)
    valid_rows = (columns < basis_sizes[:, None]).astype(jnp.float32)
    coupling = h_couple * coupling_pattern.astype(jnp.bfloat16)[:, None, None]
    current = (
        bands.reshape(band_local, elem_local, basis_width) * valid_rows.astype(jnp.bfloat16)[None]
    )
    previous = current
    for degree in range(DEGREE):
        current_float = current.astype(jnp.float32)
        local_term = jnp.einsum("eij,bej->bei", h_diag, current, preferred_element_type=jnp.float32)
        following = from_behind(current[:, 0], "elem", -1)
        ahead_rows = jnp.concatenate([current[:, 1:], following[:, None]], axis=1)
        upper_term = jnp.einsum(
            "eij,bej->bei", coupling, ahead_rows, preferred_element_type=jnp.float32
        )
        carried = jnp.einsum("eji,bej->bei", coupling, current, preferred_element_type=jnp.float32)
        arrived = from_behind(carried[:, -1], "elem", 1)
        lower_term = jnp.concatenate([arrived[:, None], carried[:, :-1]], axis=1)
        applied = (local_term + upper_term + lower_term) * valid_rows[None]
        shifted = applied - center_shift * current_float
        if degree == 0:
            next_iterate = shifted / half_width
        else:
            next_iterate = 2.0 * shifted / half_width - previous.astype(jnp.float32)
        previous, current = (current, next_iterate.astype(jnp.bfloat16))
    filtered = current.reshape(band_local, elem_local * basis_width)
    every_band = lax.all_gather(filtered, "band", axis=0, tiled=True)
    strip = lax.dot_general(
        filtered, every_band, (((1,), (1,)), ((), ())), preferred_element_type=jnp.float32
    )
    squares = jnp.sum(jnp.square(every_band.astype(jnp.float32)), axis=1)
    strip, squares = lax.psum((strip, squares), "elem")
    scales = lax.rsqrt(squares + epsilon_norm)
    offset = lax.axis_index("band") * band_local
    weights = rotation_columns(strip, scales, offset, total_rows)
    return jnp.dot(weights, every_band, preferred_element_type=jnp.float32).astype(jnp.bfloat16)


def shards(basis_sizes, coupling_pattern, h_diag, h_couple, bands):
    count, n = h_diag.shape[:2]
    local = bands.shape[0]
    elem_size, band_size = lax.axis_size("elem"), lax.axis_size("band")
    rows = local // elem_size
    wide = -(-(3 * n + 1) // LANES) * LANES
    fits = (
        band_size & (band_size - 1) == 0
        and n % (8 * band_size) == 0
        and local % LANES == 0
        and elem_size % 2 == 0
        and local % elem_size == 0
        and rows % 16 == 0
        and rows * LANES >= 2 * local * band_size
        and count > 2 * DEGREE
        and n % 16 == 0
    )
    form = fast_shards if fits else general_shards
    return form(basis_sizes, coupling_pattern, h_diag, h_couple, bands)


def solution(mesh):
    in_specs = (
        P("elem"),
        P("elem"),
        P("elem", None, None),
        P("elem", None, None),
        P("band", "elem"),
    )
    out_specs = P("band", "elem")
    return jax.shard_map(shards, mesh=mesh, in_specs=in_specs, out_specs=out_specs, check_vma=False)
```
